32 devices in a mesh: cfg: 2 (over core), tok: 16 (over z, y, x).
Axes of the slice: x: 2, y: 2, z: 4, core: 2. Of those that a mesh axis runs over, the one named last changes fastest.
Arguments:
- hidden_in: bfloat16 [3072, 1152], P('tok'), may hold values from -6 to 6
- noisy_latent: float32 [3072, 16], P('tok'), may hold values from -6 to 6
- piece_rows: int32 [2, 8], replicated, may hold values from 1 to 192, 1024 in all within a row
- modulation: float32 [2, 2, 8, 1152], P('cfg'), may hold values from -3 to 3
- qkv_weight: bfloat16 [16, 1152, 432], P('tok'), may hold values from -1 to 1, as said below
- proj_weight: bfloat16 [16, 1152, 144], P('tok'), may hold values from -1 to 1, as said below
- up_weight: bfloat16 [16, 1152, 576], P('tok'), may hold values from -1 to 1, as said below
- down_weight: bfloat16 [16, 1152, 576], P('tok'), may hold values from -1 to 1, as said below
- final_weight: bfloat16 [1152, 16], replicated, may hold values from -0.1875 to 0.1875
- guidance: float32 [2], replicated, may hold values from 1.5 to 4.5
- solver_coef: float32 [2, 2], replicated, may hold values from 0.3 to 1.2
Outputs:
- next_latent: float32 [3072, 16], P('tok')
- block_out: bfloat16 [2, 3072, 1152], P('cfg', 'tok')
The draws below stay inside these ranges and needn't reach their ends.
Inputs may be any that keep to these rules, and one draw needn't show every extreme that they name: Row l of piece_rows sums to 1024; in every row the largest entry is 192. `qkv_weight`: copy i equals copy i % 8. `proj_weight`: copy i equals copy i % 8. `up_weight`: copy i equals copy i % 8. `down_weight`: copy i equals copy i % 8.
All inputs are finite; a program needn't handle non-finite values.
Results may differ from the reference program's by a relative error of at most 0.008.
Values may be sent and summed in bfloat16 or wider, within the bound.
No kernel may reach another device: no remote copies, remote signals or barrier semaphores. Data moves between devices by JAX's collectives and lax.ppermute only.
A program may use at most 64 MiB of HBM per device.

```python
import math
import jax
import jax.numpy as jnp
import numpy as np
from jax import lax

D = 1152
HEADS = 16
HEAD_DIM = 72
FF = 4608
OUTC = 16
GROUP = 8
LEN = 1024
CAP = 192
LATENTS = 2
SLOTS = 3072


def copy_blocks(full_cols, block_width):
    row_count = full_cols.shape[0]
    blocks = full_cols.reshape(row_count, GROUP, block_width).transpose(1, 0, 2)
    return jnp.tile(blocks, (LATENTS, 1, 1))


def drawn_matrix(key, rows, cols, fan_in):
    return jnp.clip(jnp.clip(jax.random.normal(key, (rows, cols), jnp.float32), -6.0, 6.0) * fan_in ** (-0.5), -1.0, 1.0)


def draw_qkv_weight(key, part):
    key_base = jax.random.fold_in(key, 11)
    base_cols = jnp.clip(jax.random.normal(key_base, (D, 3 * D), jnp.float32), -6.0, 6.0) * D ** (-0.5)
    full_cols = jnp.clip(base_cols, -1.0, 1.0)
    head_width = D // GROUP
    blocks = full_cols.reshape(D, 3, GROUP, head_width).transpose(2, 0, 1, 3).reshape(GROUP, D, 3 * head_width)
    return jnp.tile(blocks, (LATENTS, 1, 1)).astype(jnp.bfloat16)


def draw_proj_weight(key, part):
    return copy_blocks(drawn_matrix(jax.random.fold_in(key, 21), D, D, D), D // GROUP).astype(jnp.bfloat16)


def draw_up_weight(key, part):
    return copy_blocks(drawn_matrix(jax.random.fold_in(key, 31), D, FF, D), FF // GROUP).astype(jnp.bfloat16)


def draw_down_weight(key, part):
    return copy_blocks(drawn_matrix(jax.random.fold_in(key, 41), D, FF, FF), FF // GROUP).astype(jnp.bfloat16)


def block_scale(rng, extent, cuts, low, largest):
    factor_of = 1.0
    for dim, blocks in cuts:
        draws = jax.random.uniform(jax.random.fold_in(jax.random.fold_in(rng, 6), dim), (blocks,), jnp.float32, low / len(cuts), largest / len(cuts))
        factor_of = factor_of * jnp.repeat(jnp.exp(draws), extent[dim] // blocks).reshape((-1,) + (1,) * (len(extent) - 1 - dim))
    return factor_of


def split_up(count, total, bound, lean):
    portions = [(1 << 20) // math.isqrt(standing ** lean) + 1 for standing in range(2, count + 1)]
    rest, given = total - bound - (count - 1), [1] * (count - 1)
    while rest > 0:
        candidates = [i for i in range(count - 1) if given[i] < bound]
        pool, remaining = sum([portions[i] for i in candidates]), rest
        for i in candidates:
            extra = min(bound - given[i], max(1, remaining * portions[i] // pool), rest)
            given[i] = given[i] + extra
            rest = rest - extra
    return np.array([bound] + given)


def ragged(key, number_of, total, most, lean):
    if number_of == 2:
        one = jax.random.randint(key, (), max(1, total - most), min(most, total - 1) + 1)
        return jnp.stack([one, total - one])
    tallies = jnp.asarray(split_up(number_of, total, most, lean), jnp.int32)
    pairs = (number_of - 1) // 2
    donor, receiver = tallies[1:1 + 2 * pairs:2], tallies[2:2 + 2 * pairs:2]
    margin = jnp.minimum(donor - 1, most - receiver)
    moved = jax.random.randint(jax.random.fold_in(key, 1), (pairs,), 0, 1 << 20) % (margin + 1)
    tallies = tallies.at[1:1 + 2 * pairs:2].set(donor - moved).at[2:2 + 2 * pairs:2].set(receiver + moved)
    return tallies[jax.random.permutation(jax.random.fold_in(key, 2), number_of)]


def bell_draw(own_key, dims, scale, most, split=(), kind=jnp.bfloat16):
    values = scale * jax.random.normal(own_key, dims, jnp.float32)
    if split:
        values = values * block_scale(own_key, dims, split, -0.22, 0.18)
    return jnp.clip(values, -most, most).astype(kind)


def setup_inputs(seed: int = 0) -> dict:
    streams_of = jax.random.split(jax.random.key(seed), 12)
    hidden_in = bell_draw(streams_of[0], (SLOTS, D), 1.0, 6.0, ((0, 16),))
    noisy_latent = bell_draw(streams_of[1], (SLOTS, OUTC), 1.0, 6.0, ((0, 16),), jnp.float32)
    piece_rows = jax.vmap(lambda own: ragged(own, GROUP, LEN, CAP, 2))(jax.random.split(streams_of[2], LATENTS)).reshape((LATENTS, GROUP)).astype(jnp.int32)
    modulation = bell_draw(streams_of[3], (2, LATENTS, 8, D), 0.6, 3.0, ((0, 2),), jnp.float32)
    qkv_weight = draw_qkv_weight(jax.random.fold_in(streams_of[11], 71), 0)
    proj_weight = draw_proj_weight(jax.random.fold_in(streams_of[11], 71), 0)
    up_weight = draw_up_weight(jax.random.fold_in(streams_of[11], 71), 0)
    down_weight = draw_down_weight(jax.random.fold_in(streams_of[11], 71), 0)
    final_weight = bell_draw(streams_of[8], (D, OUTC), D ** -0.5, 0.1875)
    guidance = jnp.clip(jax.random.uniform(streams_of[9], (LATENTS,), jnp.float32, 1.5, 4.5), 1.5, 4.5)
    solver_coef = jnp.clip(jax.random.uniform(streams_of[10], (LATENTS, 2), jnp.float32, 0.3, 1.2), 0.3, 1.2)
    return {"hidden_in": hidden_in, "noisy_latent": noisy_latent, "piece_rows": piece_rows, "modulation": modulation, "qkv_weight": qkv_weight, "proj_weight": proj_weight, "up_weight": up_weight, "down_weight": down_weight, "final_weight": final_weight, "guidance": guidance, "solver_coef": solver_coef}


def layer_norm(values):
    center = values - lax.optimization_barrier(jnp.mean(values, axis=-1, keepdims=True))
    spread = lax.optimization_barrier(jnp.mean(center * center, axis=-1, keepdims=True))
    return center / jnp.sqrt(spread + 1e-06)

def modulate(values, shift_vec, scale_vec):
    return layer_norm(values) * (1.0 + scale_vec) + shift_vec

def latent_block(rows_now, valid_now, factors, qkv_weight, proj_weight, up_weight, down_weight, final_weight):
    row_count = rows_now.shape[0]
    inv_root = HEAD_DIM ** (-0.5)
    inputs = rows_now.astype(jnp.float32)
    attn_in = modulate(inputs, factors[0], factors[1]).astype(jnp.bfloat16)
    projected = jnp.dot(attn_in, qkv_weight, preferred_element_type=jnp.float32).astype(jnp.bfloat16)
    split_heads = projected.reshape(row_count, 3, HEADS, HEAD_DIM).transpose(1, 2, 0, 3)

    def one_head(operands):
        query_head, key_head, value_head = operands
        scores = jnp.dot(query_head, key_head.T, preferred_element_type=jnp.float32) * inv_root
        scores = jnp.where(valid_now[None, :], scores, -1e+30)
        row_peak = lax.optimization_barrier(jnp.max(scores, axis=-1, keepdims=True))
        exp_scores = jnp.exp(scores - row_peak)
        attn_probs = (exp_scores / lax.optimization_barrier(jnp.sum(exp_scores, axis=-1, keepdims=True))).astype(jnp.bfloat16)
        return jnp.dot(attn_probs, value_head, preferred_element_type=jnp.float32).astype(jnp.bfloat16)
    heads_out = lax.map(one_head, (split_heads[0], split_heads[1], split_heads[2]))
    heads_flat = heads_out.transpose(1, 0, 2).reshape(row_count, HEADS * HEAD_DIM)
    attn_out = jnp.dot(heads_flat, proj_weight.T, preferred_element_type=jnp.float32)
    residual_mid = inputs + factors[2] * attn_out
    mlp_input = modulate(residual_mid, factors[3], factors[4]).astype(jnp.bfloat16)
    hidden_units = jax.nn.gelu(jnp.dot(mlp_input, up_weight, preferred_element_type=jnp.float32), approximate=True).astype(jnp.bfloat16)
    mlp_out = jnp.dot(hidden_units, down_weight.T, preferred_element_type=jnp.float32)
    block_rows = (residual_mid + factors[5] * mlp_out).astype(jnp.bfloat16)
    block_rows = jnp.where(valid_now[:, None], block_rows, jnp.zeros_like(block_rows))
    final_in = modulate(block_rows.astype(jnp.float32), factors[6], factors[7]).astype(jnp.bfloat16)
    noise_pred = jnp.dot(final_in, final_weight, preferred_element_type=jnp.float32)
    return (block_rows, noise_pred)

def reference(hidden_in, noisy_latent, piece_rows, modulation, qkv_weight, proj_weight, up_weight, down_weight, final_weight, guidance, solver_coef):
    head_width = D // GROUP
    full_qkv = qkv_weight[:GROUP].reshape(GROUP, D, 3, head_width).transpose(1, 2, 0, 3).reshape(D, 3 * D)
    full_proj = proj_weight[:GROUP].transpose(1, 0, 2).reshape(D, D)
    full_up = up_weight[:GROUP].transpose(1, 0, 2).reshape(D, FF)
    full_down = down_weight[:GROUP].transpose(1, 0, 2).reshape(D, FF)
    latent_rows = hidden_in.reshape(LATENTS, GROUP * CAP, D)
    slot_pos = jnp.arange(CAP, dtype=jnp.int32)
    valid_rows = (slot_pos[None, None, :] < piece_rows[:, :, None]).reshape(LATENTS, GROUP * CAP)

    def per_latent(operands):
        rows_now, valid_now, cond_factors, uncond_factors = operands
        cond_block, cond_pred = latent_block(rows_now, valid_now, cond_factors, full_qkv, full_proj, full_up, full_down, final_weight)
        uncond_block, uncond_pred = latent_block(rows_now, valid_now, uncond_factors, full_qkv, full_proj, full_up, full_down, final_weight)
        return (cond_block, uncond_block, cond_pred, uncond_pred)
    cond_block, uncond_block, cond_pred, uncond_pred = lax.map(per_latent, (latent_rows, valid_rows, modulation[0], modulation[1]))
    scale_now = guidance[:, None, None]
    guided = scale_now * cond_pred + (1.0 - scale_now) * uncond_pred
    coef_keep = solver_coef[:, 0][:, None, None]
    coef_noise = solver_coef[:, 1][:, None, None]
    stepped = coef_keep * noisy_latent.reshape(LATENTS, GROUP * CAP, OUTC) - coef_noise * guided
    next_latent = jnp.where(valid_rows[:, :, None], stepped, jnp.zeros_like(stepped)).reshape(SLOTS, OUTC)
    block_out = jnp.stack([cond_block, uncond_block]).reshape(2, SLOTS, D)
    return (next_latent, block_out)
```

```python
import jax
import jax.numpy as jnp
from jax import lax
from jax.sharding import PartitionSpec as P

HEAD_DIM = 72
GROUP = 8
AXIS_ORDERS = ((1, 2, 4), (2, 4, 1), (4, 1, 2))


def from_member(block, offset):
    count = lax.axis_size("tok")
    return lax.ppermute(block, "tok", [(i, i ^ offset) for i in range(count)])


def from_other_half(block):
    return lax.ppermute(block, "cfg", [(0, 1), (1, 0)])


def after(value, *earlier):
    return lax.optimization_barrier((value,) + earlier)[0]


def layer_norm(values):
    center = values - jnp.mean(values, axis=-1, keepdims=True)
    spread = jnp.mean(center * center, axis=-1, keepdims=True)
    return center / jnp.sqrt(spread + 1e-06)


def modulate(values, shift_vec, scale_vec):
    return layer_norm(values) * (1.0 + scale_vec) + shift_vec


def cube_gather(own_rows):
    piece_rows = own_rows.shape[0] // 3
    first, second, third = [], [], []
    for piece, (b0, b1, b2) in enumerate(AXIS_ORDERS):
        own = own_rows[piece * piece_rows : (piece + 1) * piece_rows]
        first.append((own, b0, b1, b2))
    one = [from_member(own, b0) for own, b0, b1, b2 in first]
    for (own, b0, b1, b2), r1 in zip(first, one):
        second.append(jnp.concatenate([own, r1]))
    two = [from_member(s2, o[2]) for s2, o in zip(second, first)]
    for s2, r2 in zip(second, two):
        third.append(jnp.concatenate([s2, r2]))
    three = [from_member(s3, o[3]) for s3, o in zip(third, first)]
    near = from_other_half(jnp.concatenate([s3[piece_rows:] for s3 in third]))
    far = from_other_half(jnp.concatenate(three))

    def by_offset(s3_of, r3_of):
        found = {}
        for piece, (b0, b1, b2) in enumerate(AXIS_ORDERS):
            order = (0, b0, b1, b0 ^ b1)
            for pos, offset in enumerate(order):
                rows = slice(pos * piece_rows, (pos + 1) * piece_rows)
                if s3_of[piece] is not None:
                    if s3_of[piece].shape[0] == 4 * piece_rows:
                        found[offset, piece] = s3_of[piece][rows]
                    elif pos:
                        found[offset, piece] = s3_of[piece][(pos - 1) * piece_rows : pos * piece_rows]
                found[offset ^ b2, piece] = r3_of[piece][rows]
        return found

    mine = by_offset(third, three)
    other = by_offset(
        [near[3 * i * piece_rows : 3 * (i + 1) * piece_rows] for i in range(3)],
        [far[4 * i * piece_rows : 4 * (i + 1) * piece_rows] for i in range(3)],
    )
    return mine, other, two


def attention(attn_in, key_valid, qkv_cols):
    row_count = attn_in.shape[0]
    qkv_now = jnp.dot(attn_in, qkv_cols, preferred_element_type=jnp.float32).astype(jnp.bfloat16)
    local_width = qkv_now.shape[1] // 3
    head_count = local_width // HEAD_DIM
    block_size = 512
    block_count = row_count // block_size
    inv_root = HEAD_DIM ** (-0.5)
    results = []
    for head_pos in range(head_count):
        start = head_pos * HEAD_DIM
        queries = qkv_now[:, start : start + HEAD_DIM].reshape(block_count, block_size, HEAD_DIM)
        keys_head = qkv_now[:, local_width + start : local_width + start + HEAD_DIM]
        values_head = qkv_now[:, 2 * local_width + start : 2 * local_width + start + HEAD_DIM]

        def one_block(query_block):
            scores = (
                lax.dot_general(
                    query_block,
                    keys_head,
                    (((1,), (1,)), ((), ())),
                    preferred_element_type=jnp.float32,
                )
                * inv_root
            )
            scores = jnp.where(key_valid[None, :], scores, -1e30)
            row_peak = jnp.max(scores, axis=-1, keepdims=True)
            exp_scores = jnp.exp(scores - row_peak)
            attn_probs = (exp_scores / jnp.sum(exp_scores, axis=-1, keepdims=True)).astype(
                jnp.bfloat16
            )
            return jnp.dot(attn_probs, values_head, preferred_element_type=jnp.float32).astype(
                jnp.bfloat16
            )

        results.append(lax.map(one_block, queries).reshape(row_count, HEAD_DIM))
    return jnp.concatenate(results, axis=1)


def shards(
    hidden_in,
    noisy_latent,
    piece_rows,
    modulation,
    qkv_weight,
    proj_weight,
    up_weight,
    down_weight,
    final_weight,
    guidance,
    solver_coef,
):
    capacity = hidden_in.shape[0]
    half_cap = capacity // 2
    device_pos = lax.axis_index("tok")
    cfg_half = lax.axis_index("cfg")
    latent_id = device_pos // GROUP
    member_id = device_pos % GROUP
    counts = lax.dynamic_index_in_dim(piece_rows, latent_id, 0, keepdims=False)
    factors = lax.dynamic_index_in_dim(modulation[0], latent_id, 0, keepdims=False)
    scale_now = lax.dynamic_index_in_dim(guidance, latent_id, 0, keepdims=False)
    coef_pair = lax.dynamic_index_in_dim(solver_coef, latent_id, 0, keepdims=False)
    rel_counts = jnp.stack(
        [lax.dynamic_index_in_dim(counts, member_id ^ d, 0, keepdims=False) for d in range(GROUP)]
    )
    half_pos = jnp.arange(half_cap, dtype=jnp.int32)
    slot_pos = jnp.concatenate([half_pos + cfg_half * half_cap, half_pos + (1 - cfg_half) * half_cap])
    own_valid = slot_pos < rel_counts[0]
    key_valid = (slot_pos[None, :] < rel_counts[:, None]).reshape(-1)

    def swapped(rows):
        mine = lax.dynamic_slice_in_dim(rows, cfg_half * half_cap, half_cap)
        other = lax.dynamic_slice_in_dim(rows, (1 - cfg_half) * half_cap, half_cap)
        return mine, other

    own_mine, own_other = swapped(hidden_in)
    mine, other, stage = cube_gather(own_mine)
    sub = half_cap // 3
    for piece in range(3):
        other[0, piece] = own_other[piece * sub : (piece + 1) * sub]
    gathered = jnp.concatenate(
        [
            part[d, piece]
            for d in range(GROUP)
            for part in (mine, other)
            for piece in range(3)
        ]
    )

    proj_rows = after(proj_weight[0].T, *stage)
    width = proj_rows.shape[0]
    proj_half = lax.dynamic_slice_in_dim(proj_rows, cfg_half * (width // 2), width // 2)
    proj_mine, proj_other, proj_stage = cube_gather(proj_half)
    other_half = lax.dynamic_slice_in_dim(proj_rows, (1 - cfg_half) * (width // 2), width // 2)
    psub = width // 6
    for piece in range(3):
        proj_other[0, piece] = other_half[piece * psub : (piece + 1) * psub]
    first_half = []
    second_half = []
    for d in range(GROUP):
        pm = jnp.concatenate([proj_mine[d, piece] for piece in range(3)])
        po = jnp.concatenate([proj_other[d, piece] for piece in range(3)])
        first_half.append(pm)
        second_half.append(po)
    pm = jnp.stack(first_half)
    po = jnp.stack(second_half)
    lower = jnp.where(cfg_half == 0, pm, po)
    upper = jnp.where(cfg_half == 0, po, pm)
    proj_all = jnp.concatenate([lower, upper], axis=1).reshape(GROUP * width, -1)

    up_cols = up_weight[0]
    down_cols = down_weight[0]
    sent = jnp.where(cfg_half == 0, up_cols, down_cols).T
    sent = after(sent, *stage)
    got = from_member(sent, 4)
    swapped_got = from_other_half(got)
    far_up = jnp.where(cfg_half == 0, got, swapped_got)
    far_down = jnp.where(cfg_half == 0, swapped_got, got)

    attn_in = modulate(gathered.astype(jnp.float32), factors[0], factors[1]).astype(jnp.bfloat16)
    heads_out = attention(attn_in, key_valid, qkv_weight[0])
    heads_t = heads_out.T
    blocks = [heads_t[:, d * capacity : (d + 1) * capacity] for d in range(GROUP)]
    blocks = [blocks[0]] + [from_member(blocks[d], d) for d in range(1, GROUP)]
    heads_flat = jnp.concatenate(blocks)
    attn_out = lax.dot_general(
        heads_flat, proj_all, (((0,), (0,)), ((), ())), preferred_element_type=jnp.float32
    )
    inputs = jnp.concatenate([own_mine, own_other]).astype(jnp.float32)
    residual_mid = inputs + factors[2] * attn_out
    mlp_input = modulate(residual_mid, factors[3], factors[4]).astype(jnp.bfloat16)

    from_x = from_member(mlp_input, 1)
    from_y = from_member(mlp_input, 2)
    diag_low = from_member(from_x[:half_cap], 2)
    diag_high = from_member(from_y[half_cap:], 1)
    rows = jnp.concatenate([mlp_input, from_x, from_y, diag_low, diag_high])
    near_hidden = jax.nn.gelu(
        jnp.dot(rows, up_cols, preferred_element_type=jnp.float32), approximate=True
    ).astype(jnp.bfloat16)
    far_hidden = jax.nn.gelu(
        lax.dot_general(rows, far_up, (((1,), (1,)), ((), ())), preferred_element_type=jnp.float32),
        approximate=True,
    ).astype(jnp.bfloat16)
    partial = lax.dot_general(
        near_hidden, down_cols, (((1,), (1,)), ((), ())), preferred_element_type=jnp.float32
    ) + jnp.dot(far_hidden, far_down, preferred_element_type=jnp.float32)
    own_part = partial[:capacity]
    x_part = partial[capacity : 2 * capacity]
    y_part = partial[2 * capacity : 3 * capacity]
    diag = partial[3 * capacity :].astype(jnp.bfloat16)
    via_x = from_member(diag[:half_cap], 1).astype(jnp.float32)
    via_y = from_member(diag[half_cap:], 2).astype(jnp.float32)
    to_y = jnp.concatenate([y_part[:half_cap] + via_x, y_part[half_cap:]]).astype(jnp.bfloat16)
    to_x = jnp.concatenate([x_part[:half_cap], x_part[half_cap:] + via_y]).astype(jnp.bfloat16)
    mlp_out = (
        own_part
        + from_member(to_x, 1).astype(jnp.float32)
        + from_member(to_y, 2).astype(jnp.float32)
    )
    block_rows = (residual_mid + factors[5] * mlp_out).astype(jnp.bfloat16)
    block_rows = jnp.where(own_valid[:, None], block_rows, jnp.zeros_like(block_rows))
    final_in = modulate(block_rows.astype(jnp.float32), factors[6], factors[7]).astype(jnp.bfloat16)
    noise_pred = jnp.dot(final_in, final_weight, preferred_element_type=jnp.float32)
    noise_pred = jnp.concatenate(swapped(noise_pred))
    block_rows = jnp.concatenate(swapped(block_rows))
    weight_now = jnp.where(cfg_half == 0, scale_now, 1.0 - scale_now)
    weighted = weight_now * noise_pred
    guided = weighted + from_other_half(weighted)
    stepped = coef_pair[0] * noisy_latent - coef_pair[1] * guided
    in_piece = jnp.arange(capacity, dtype=jnp.int32) < rel_counts[0]
    next_latent = jnp.where(in_piece[:, None], stepped, jnp.zeros_like(stepped))
    return (next_latent, block_rows[None])


def solution(mesh):
    placed = (
        P("tok", None),
        P("tok", None),
        P(),
        P("cfg", None, None, None),
        P("tok", None, None),
        P("tok", None, None),
        P("tok", None, None),
        P("tok", None, None),
        P(),
        P(),
        P(),
    )
    return jax.shard_map(
        shards,
        mesh=mesh,
        in_specs=placed,
        out_specs=(P("tok", None), P("cfg", "tok", None)),
        check_vma=False,
    )
```

```python
import jax
import jax.numpy as jnp
from jax import lax
from jax.sharding import PartitionSpec as P

HEAD_DIM = 72
GROUP = 8


def from_member(block, offset):
    count = lax.axis_size("tok")
    return lax.ppermute(block, "tok", [(i, i ^ offset) for i in range(count)])


def from_other_half(block):
    return lax.ppermute(block, "cfg", [(0, 1), (1, 0)])


def after(value, *earlier):
    return lax.optimization_barrier((value,) + earlier)[0]


def layer_norm(values):
    center = values - jnp.mean(values, axis=-1, keepdims=True)
    spread = jnp.mean(center * center, axis=-1, keepdims=True)
    return center / jnp.sqrt(spread + 1e-06)


def modulate(values, shift_vec, scale_vec):
    return layer_norm(values) * (1.0 + scale_vec) + shift_vec


def cube_groups():
    halves, count = lax.axis_size("cfg"), lax.axis_size("tok")
    return [
        [half * count + first + m for half in range(halves) for m in range(GROUP)]
        for first in range(0, count, GROUP)
    ]


def pair_groups():
    halves, count = lax.axis_size("cfg"), lax.axis_size("tok")
    far = GROUP // 2
    return [
        [half * count + first + m for half in range(halves) for m in (low, low + far)]
        for first in range(0, count, GROUP)
        for low in range(far)
    ]


def member_groups():
    count = lax.axis_size("tok")
    return [[first + m for m in range(GROUP)] for first in range(0, count, GROUP)]


def attention(attn_in, key_valid, qkv_cols):
    row_count = attn_in.shape[0]
    qkv_now = jnp.dot(attn_in, qkv_cols, preferred_element_type=jnp.float32).astype(jnp.bfloat16)
    local_width = qkv_now.shape[1] // 3
    head_count = local_width // HEAD_DIM
    block_size = 512
    block_count = row_count // block_size
    inv_root = HEAD_DIM ** (-0.5)
    results = []
    for head_pos in range(head_count):
        start = head_pos * HEAD_DIM
        queries = qkv_now[:, start : start + HEAD_DIM].reshape(block_count, block_size, HEAD_DIM)
        keys_head = qkv_now[:, local_width + start : local_width + start + HEAD_DIM]
        values_head = qkv_now[:, 2 * local_width + start : 2 * local_width + start + HEAD_DIM]

        def one_block(query_block):
            scores = (
                lax.dot_general(
                    query_block,
                    keys_head,
                    (((1,), (1,)), ((), ())),
                    preferred_element_type=jnp.float32,
                )
                * inv_root
            )
            scores = jnp.where(key_valid[None, :], scores, -1e30)
            row_peak = jnp.max(scores, axis=-1, keepdims=True)
            exp_scores = jnp.exp(scores - row_peak)
            attn_probs = (exp_scores / jnp.sum(exp_scores, axis=-1, keepdims=True)).astype(
                jnp.bfloat16
            )
            return jnp.dot(attn_probs, values_head, preferred_element_type=jnp.float32).astype(
                jnp.bfloat16
            )

        results.append(lax.map(one_block, queries).reshape(row_count, HEAD_DIM))
    return jnp.concatenate(results, axis=1)


def shards(
    hidden_in,
    noisy_latent,
    piece_rows,
    modulation,
    qkv_weight,
    proj_weight,
    up_weight,
    down_weight,
    final_weight,
    guidance,
    solver_coef,
):
    capacity = hidden_in.shape[0]
    half_cap = capacity // 2
    device_pos = lax.axis_index("tok")
    cfg_half = lax.axis_index("cfg")
    latent_id = device_pos // GROUP
    member_id = device_pos % GROUP
    counts = lax.dynamic_index_in_dim(piece_rows, latent_id, 0, keepdims=False)
    factors = lax.dynamic_index_in_dim(modulation[0], latent_id, 0, keepdims=False)
    scale_now = lax.dynamic_index_in_dim(guidance, latent_id, 0, keepdims=False)
    coef_pair = lax.dynamic_index_in_dim(solver_coef, latent_id, 0, keepdims=False)
    own_count = lax.dynamic_index_in_dim(counts, member_id, 0, keepdims=False)
    slot_pos = jnp.arange(capacity, dtype=jnp.int32)
    own_valid = slot_pos < own_count
    halves = slot_pos.reshape(2, 1, half_cap)
    key_valid = (halves < counts[None, :, None]).reshape(-1)
    inputs = hidden_in.astype(jnp.float32)
    own_half = lax.dynamic_slice_in_dim(hidden_in, cfg_half * half_cap, half_cap)
    gathered = lax.all_gather(own_half, ("cfg", "tok"), axis_index_groups=cube_groups(), tiled=True)

    proj_rows = after(proj_weight[0], gathered).T
    width = proj_rows.shape[0]
    proj_half = lax.dynamic_slice_in_dim(proj_rows, cfg_half * (width // 2), width // 2)
    proj_all = lax.all_gather(proj_half, ("cfg", "tok"), axis_index_groups=cube_groups(), tiled=True)

    up_cols, down_cols = after(up_weight[0], gathered), after(down_weight[0], gathered)
    depth = up_cols.shape[0]
    both = jnp.stack(
        [
            lax.dynamic_slice_in_dim(w, cfg_half * (depth // 2), depth // 2)
            for w in (up_cols, down_cols)
        ]
    )
    pair = lax.all_gather(both, ("cfg", "tok"), axis_index_groups=pair_groups())
    pair_up = [jnp.concatenate([pair[z, 0], pair[z + 2, 0]]) for z in range(2)]
    pair_down = [jnp.concatenate([pair[z, 1], pair[z + 2, 1]]) for z in range(2)]

    attn_in = modulate(gathered.astype(jnp.float32), factors[0], factors[1]).astype(jnp.bfloat16)
    heads_out = attention(attn_in, key_valid, qkv_weight[0])
    blocks = heads_out.reshape(2, GROUP, half_cap, 2, width // 2).transpose(1, 3, 4, 0, 2)
    blocks = blocks.reshape(GROUP, width, capacity)
    heads = lax.all_to_all(blocks, "tok", 0, 0, axis_index_groups=member_groups())
    heads_flat = heads.reshape(GROUP, 2, width // 2, capacity).transpose(1, 0, 2, 3)
    heads_flat = heads_flat.reshape(GROUP * width, capacity)
    attn_out = lax.dot_general(
        heads_flat, proj_all, (((0,), (0,)), ((), ())), preferred_element_type=jnp.float32
    )
    residual_mid = inputs + factors[2] * attn_out
    mlp_input = modulate(residual_mid, factors[3], factors[4]).astype(jnp.bfloat16)

    from_x = from_member(mlp_input, 1)
    from_y = from_member(mlp_input, 2)
    diag_low = from_member(from_x[:half_cap], 2)
    diag_high = from_member(from_y[half_cap:], 1)
    rows = jnp.concatenate([mlp_input, from_x, from_y, diag_low, diag_high])
    partial = 0.0
    for up_now, down_now in zip(pair_up, pair_down):
        hidden_units = jax.nn.gelu(
            jnp.dot(rows, up_now, preferred_element_type=jnp.float32), approximate=True
        ).astype(jnp.bfloat16)
        partial = partial + lax.dot_general(
            hidden_units, down_now, (((1,), (1,)), ((), ())), preferred_element_type=jnp.float32
        )
    own_part = partial[:capacity]
    x_part = partial[capacity : 2 * capacity]
    y_part = partial[2 * capacity : 3 * capacity]
    diag = partial[3 * capacity :].astype(jnp.bfloat16)
    via_x = from_member(diag[:half_cap], 1).astype(jnp.float32)
    via_y = from_member(diag[half_cap:], 2).astype(jnp.float32)
    to_y = jnp.concatenate([y_part[:half_cap] + via_x, y_part[half_cap:]]).astype(jnp.bfloat16)
    to_x = jnp.concatenate([x_part[:half_cap], x_part[half_cap:] + via_y]).astype(jnp.bfloat16)
    mlp_out = (
        own_part
        + from_member(to_x, 1).astype(jnp.float32)
        + from_member(to_y, 2).astype(jnp.float32)
    )
    block_rows = (residual_mid + factors[5] * mlp_out).astype(jnp.bfloat16)
    block_rows = jnp.where(own_valid[:, None], block_rows, jnp.zeros_like(block_rows))
    final_in = modulate(block_rows.astype(jnp.float32), factors[6], factors[7]).astype(jnp.bfloat16)
    noise_pred = jnp.dot(final_in, final_weight, preferred_element_type=jnp.float32)
    weight_now = jnp.where(cfg_half == 0, scale_now, 1.0 - scale_now)
    weighted = weight_now * noise_pred
    guided = weighted + from_other_half(weighted)
    stepped = coef_pair[0] * noisy_latent - coef_pair[1] * guided
    next_latent = jnp.where(own_valid[:, None], stepped, jnp.zeros_like(stepped))
    return (next_latent, block_rows[None])


def solution(mesh):
    placed = (
        P("tok", None),
        P("tok", None),
        P(),
        P("cfg", None, None, None),
        P("tok", None, None),
        P("tok", None, None),
        P("tok", None, None),
        P("tok", None, None),
        P(),
        P(),
        P(),
    )
    return jax.shard_map(
        shards,
        mesh=mesh,
        in_specs=placed,
        out_specs=(P("tok", None), P("cfg", "tok", None)),
        check_vma=False,
    )
```

```python
import functools
import math

import jax
import jax.numpy as jnp
from jax import lax
from jax.experimental import pallas as pl
from jax.experimental.pallas import tpu as pltpu
from jax.sharding import PartitionSpec as P

HEAD_DIM = 72
GROUP = 8
LEN = 1024
LANES = 128
ALIGN = 16
LARGE = ((1, 2, 4), (4, 1, 2))
SMALL = (2, 4, 1)
F32 = jnp.float32
BF16 = jnp.bfloat16


def permute_by(block, offsets):
    count = lax.axis_size("tok")
    route = [
        (half * count + i, half * count + (i ^ offset))
        for half, offset in enumerate(offsets)
        for i in range(count)
    ]
    return lax.ppermute(block, ("cfg", "tok"), route)


def from_other_half(block):
    return lax.ppermute(block, "cfg", [(0, 1), (1, 0)])


def after(value, *earlier):
    return lax.optimization_barrier((value,) + earlier)[0]


def cube_groups():
    halves, count = lax.axis_size("cfg"), lax.axis_size("tok")
    return [
        [half * count + first + m for half in range(halves) for m in range(GROUP)]
        for first in range(0, count, GROUP)
    ]


def place():
    pos = lax.axis_index("tok")
    return lax.axis_index("cfg"), pos // GROUP, pos % GROUP


def normalized(values):
    center = values - jnp.mean(values, axis=-1, keepdims=True)
    spread = jnp.mean(center * center, axis=-1, keepdims=True)
    return center * lax.rsqrt(spread + 1e-06)


def mod_row(mod_ref, latent, k):
    return mod_ref[latent, k : k + 1, :]


def call(kernel, out_shape, operands, scratch=(), specs=None, flops=0, name=None):
    whole = pl.BlockSpec(memory_space=pltpu.VMEM)
    moved = sum(math.prod(o.shape) * o.dtype.itemsize for o in operands)
    return pl.pallas_call(
        kernel,
        out_shape=out_shape,
        in_specs=specs or [whole] * len(operands),
        out_specs=jax.tree.map(lambda _: whole, out_shape),
        scratch_shapes=list(scratch),
        compiler_params=pltpu.CompilerParams(vmem_limit_bytes=48 << 20),
        cost_estimate=pl.CostEstimate(flops=flops, bytes_accessed=moved, transcendentals=0),
        name=name,
    )(*operands)


def qkv_kernel(first_rows, mod_ref, weight_ref, *refs):
    row_refs, out_ref, normed = refs[:-2], refs[-2], refs[-1]
    _, latent, _ = place()
    shift, scale = mod_row(mod_ref, latent, 0), 1.0 + mod_row(mod_ref, latent, 1)
    chunk = 32
    at = 0
    for ref, first in zip(row_refs, first_rows):
        for low in range(first, ref.shape[0], chunk):
            rows = ref[low : low + chunk, :].astype(F32)
            normed[at : at + chunk, :] = (normalized(rows) * scale + shift).astype(BF16)
            at += chunk
    lane = lax.broadcasted_iota(jnp.int32, (1, weight_ref.shape[1]), 1)
    width = weight_ref.shape[1] // 3
    factor = jnp.where(lane < width, HEAD_DIM ** (-0.5) * math.log2(math.e), 1.0)
    ones = jnp.where((lane >= 2 * width) & (lane % LANES == HEAD_DIM), 1.0, 0.0)
    block = at // 2
    for low in range(0, at, block):
        out = jnp.dot(normed[low : low + block, :], weight_ref[...], preferred_element_type=F32)
        out_ref[low : low + block, :] = (out * factor + ones).astype(BF16)


def qkv_rows(modulation, weight, pieces, first_rows, name):
    count = sum(p.shape[0] - f for p, f in zip(pieces, first_rows))
    return call(
        functools.partial(qkv_kernel, first_rows),
        jax.ShapeDtypeStruct((count, weight.shape[1]), BF16),
        (modulation, weight) + tuple(pieces),
        scratch=[pltpu.VMEM((count, weight.shape[0]), BF16)],
        flops=2 * count * weight.shape[0] * weight.shape[1],
        name=name,
    )


def position(order, offset):
    return sum(1 << i for i, bit in enumerate(order) if offset & bit)


def attention_kernel(cap, packed_rows, counts_ref, early_ref, late_ref, near_ref, far_ref, packed, out):
    core, latent, member = place()
    half = cap // 2
    large, small = 2 * half // 3, half // 3
    width = early_ref.shape[1] // 3
    heads = width // LANES
    counts = [counts_ref[latent, member ^ d] for d in range(GROUP)]
    starts = [jnp.int32(0)]
    for d in range(GROUP):
        starts.append(starts[-1] + (counts[d] + ALIGN - 1) // ALIGN * ALIGN)
    total_rows = packed.shape[0]
    spare = total_rows - LEN
    packed[LEN:, :] = jnp.zeros((spare, packed.shape[1]), BF16)
    for d in range(GROUP):
        for k in range(2):
            away = (core != k).astype(jnp.int32)
            for is_small in range(2):
                size = small if is_small else large
                first = k * half + is_small * large
                where = position(SMALL if is_small else LARGE[k], d)
                if where == 0:
                    rows = early_ref[first : first + size, :]
                elif where < 4:
                    base = cap + is_small * 3 * large + (where - 1) * size
                    base = pl.multiple_of(base + away * (3 * half), 32)
                    rows = early_ref[pl.ds(base, size), :]
                else:
                    base = is_small * 4 * large + (where - 4) * size
                    base = pl.multiple_of(base + away * (4 * half), 32)
                    rows = late_ref[pl.ds(base, size), :]
                packed[pl.ds(pl.multiple_of(starts[d] + first, ALIGN), size), :] = rows
    slot = lax.broadcasted_iota(jnp.int32, (1, packed_rows), 1)
    valid = jnp.zeros((1, packed_rows), jnp.bool_)
    for d in range(GROUP):
        valid = valid | ((slot >= starts[d]) & (slot < starts[d] + counts[d]))
    bias = jnp.where(valid, 0.0, -1e30)
    out[LEN:, :] = jnp.zeros((spare, out.shape[1]), F32)
    block = packed_rows // 3
    for low in range(0, packed_rows, block):
        for head in range(heads):
            lanes = head * LANES
            queries = packed[low : low + block, lanes : lanes + LANES]
            keys = packed[:packed_rows, width + lanes : width + lanes + LANES]
            values = packed[:packed_rows, 2 * width + lanes : 2 * width + lanes + LANES]
            scores = lax.dot_general(
                queries, keys, (((1,), (1,)), ((), ())), preferred_element_type=F32
            )
            scores = scores + bias
            peak = jnp.max(scores, axis=-1, keepdims=True)
            probs = jnp.exp2(scores - peak).astype(BF16)
            mixed = jnp.dot(probs, values, preferred_element_type=F32)
            mixed = mixed / mixed[:, HEAD_DIM : HEAD_DIM + 1]
            out[low : low + block, lanes : lanes + LANES] = mixed
    for pair in range(0, GROUP, 2):
        columns = []
        for head in range(heads):
            rows = [
                out[pl.ds(pl.multiple_of(starts[d], ALIGN), cap), head * LANES : (head + 1) * LANES]
                for d in (pair, pair + 1)
            ]
            columns.append(jnp.concatenate(rows).T[:HEAD_DIM])
        dest = near_ref if pair < GROUP // 2 else far_ref
        at = pair % (GROUP // 2) * cap
        dest[:, at : at + 2 * cap] = jnp.concatenate(columns).astype(BF16)


def attention(piece_rows, early, late, cap):
    packed_rows = LEN + GROUP * ALIGN
    total = -(-(packed_rows + cap) // 32) * 32
    width = early.shape[1] // 3
    heads = width // LANES
    shape = jax.ShapeDtypeStruct((heads * HEAD_DIM, GROUP // 2 * cap), BF16)
    return call(
        functools.partial(attention_kernel, cap, packed_rows),
        (shape, shape),
        (piece_rows, early, late),
        scratch=[pltpu.VMEM((total, 3 * width), BF16), pltpu.VMEM((total, width), F32)],
        specs=[pl.BlockSpec(memory_space=pltpu.SMEM)] + [pl.BlockSpec(memory_space=pltpu.VMEM)] * 2,
        flops=4 * heads * packed_rows * packed_rows * LANES,
        name="attend",
    )


def project_kernel(cap, mod_ref, hidden_ref, proj_ref, mine_ref, zmate_ref, *refs):
    plane_refs, (mid_ref, mlp_ref, flat) = refs[:-3], refs[-3:]
    _, latent, member = place()
    heads = mine_ref.shape[0] // HEAD_DIM

    def put(block, offset):
        for head in range(heads):
            rows = block[head * HEAD_DIM : (head + 1) * HEAD_DIM]
            flat[head * GROUP + (member ^ offset)] = rows

    put(mine_ref[...][:, :cap].astype(F32), 0)
    put(zmate_ref[...][:, :cap].astype(F32), GROUP // 2)
    for j, ref in enumerate(plane_refs):
        both = ref[...].astype(F32)
        put(both[:, :cap], j + 1)
        put(both[:, cap:], (j + 1) ^ (GROUP // 2))
    stacked = flat[...].reshape(heads * GROUP * HEAD_DIM, cap).astype(BF16)
    attn_out = lax.dot_general(
        stacked, proj_ref[...], (((0,), (0,)), ((), ())), preferred_element_type=F32
    )
    mid = hidden_ref[...].astype(F32) + mod_row(mod_ref, latent, 2) * attn_out
    mid_ref[...] = mid
    scale, shift = 1.0 + mod_row(mod_ref, latent, 4), mod_row(mod_ref, latent, 3)
    mlp_ref[...] = (normalized(mid) * scale + shift).astype(BF16)


def project(modulation, hidden_in, proj_all, mine, zmate, plane):
    cap, width = hidden_in.shape
    heads = mine.shape[0] // HEAD_DIM
    return call(
        functools.partial(project_kernel, cap),
        (jax.ShapeDtypeStruct((cap, width), F32), jax.ShapeDtypeStruct((cap, width), BF16)),
        (modulation, hidden_in, proj_all, mine, zmate) + tuple(plane),
        scratch=[pltpu.VMEM((heads * GROUP, HEAD_DIM, cap), F32)],
        flops=2 * cap * width * width,
        name="project",
    )


def mlp_kernel(row_count, up_ref, down_ref, got_ref, other_ref, *refs):
    row_refs, (out_ref, far, rows, sems) = refs[:row_count], refs[row_count:]
    core, _, _ = place()
    copies = [
        pltpu.make_async_copy(got_ref, far.at[core], sems.at[0]),
        pltpu.make_async_copy(other_ref, far.at[1 - core], sems.at[1]),
    ]
    for copy in copies:
        copy.start()
    at = 0
    for ref in row_refs:
        rows[at : at + ref.shape[0], :] = ref[...]
        at += ref.shape[0]

    def gelu(v):
        return (0.5 * v * (1.0 + jnp.tanh(0.7978845608 * (v + 0.044715 * (v * v * v))))).astype(BF16)

    near = gelu(jnp.dot(rows[...], up_ref[...], preferred_element_type=F32))
    partial = lax.dot_general(
        near, down_ref[...], (((1,), (1,)), ((), ())), preferred_element_type=F32
    )
    for copy in copies:
        copy.wait()
    distant = gelu(
        lax.dot_general(rows[...], far[0], (((1,), (1,)), ((), ())), preferred_element_type=F32)
    )
    partial = partial + jnp.dot(distant, far[1], preferred_element_type=F32)
    out_ref[...] = partial.astype(out_ref.dtype)


def mlp_rows(pieces, up, down, got, other, dtype, name):
    count = sum(p.shape[0] for p in pieces)
    width, hidden = up.shape
    vmem, anywhere = pl.BlockSpec(memory_space=pltpu.VMEM), pl.BlockSpec(memory_space=pl.ANY)
    return call(
        functools.partial(mlp_kernel, len(pieces)),
        jax.ShapeDtypeStruct((count, width), dtype),
        (up, down, got, other) + tuple(pieces),
        scratch=[
            pltpu.VMEM((2, hidden, width), BF16),
            pltpu.VMEM((count, width), BF16),
            pltpu.SemaphoreType.DMA((2,)),
        ],
        specs=[vmem, vmem, anywhere, anywhere] + [vmem] * len(pieces),
        flops=8 * count * width * hidden,
        name=name,
    )


def final_kernel(counts_ref, guide_ref, mod_ref, mid_ref, part_ref, first_ref, second_ref, weight_ref, block_ref, pred_ref):
    core, latent, member = place()
    cap = mid_ref.shape[0]
    total = part_ref[:cap, :] + first_ref[:cap, :].astype(F32) + second_ref[...].astype(F32)
    rows = (mid_ref[...] + mod_row(mod_ref, latent, 5) * total).astype(BF16).astype(F32)
    valid = lax.broadcasted_iota(jnp.int32, (cap, 1), 0) < counts_ref[latent, member]
    rows = jnp.where(valid, rows, 0.0)
    block_ref[...] = rows.astype(BF16)
    scale, shift = 1.0 + mod_row(mod_ref, latent, 7), mod_row(mod_ref, latent, 6)
    final_in = (normalized(rows) * scale + shift).astype(BF16)
    pred = jnp.dot(final_in, weight_ref[...], preferred_element_type=F32)
    guide = guide_ref[latent]
    pred_ref[...] = jnp.where(core == 0, guide, 1.0 - guide) * pred


def final(piece_rows, guidance, modulation, mid, part, first, second, weight):
    cap, width = mid.shape
    smem, vmem = pl.BlockSpec(memory_space=pltpu.SMEM), pl.BlockSpec(memory_space=pltpu.VMEM)
    return call(
        final_kernel,
        (
            jax.ShapeDtypeStruct((cap, width), BF16),
            jax.ShapeDtypeStruct((cap, weight.shape[1]), F32),
        ),
        (piece_rows, guidance, modulation, mid, part, first, second, weight),
        specs=[smem, smem] + [vmem] * 6,
        flops=2 * cap * width * weight.shape[1],
        name="finish",
    )


def shards(
    hidden_in,
    noisy_latent,
    piece_rows,
    modulation,
    qkv_weight,
    proj_weight,
    up_weight,
    down_weight,
    final_weight,
    guidance,
    solver_coef,
):
    cap, width = hidden_in.shape
    half = cap // 2
    large, small = 2 * half // 3, half // 3
    core, latent, member = place()
    modulation = modulation[0]

    large_rows = lax.dynamic_slice_in_dim(hidden_in, core * half, large)
    small_rows = lax.dynamic_slice_in_dim(hidden_in, core * half + large, small)
    for step in range(3):
        offsets = [order[step] for order in LARGE]
        got_large = permute_by(large_rows, offsets)
        got_small = permute_by(small_rows, [SMALL[step]] * 2)
        if step == 0:
            first_got = got_large
        if step < 2:
            large_rows = jnp.concatenate([large_rows, got_large])
            small_rows = jnp.concatenate([small_rows, got_small])
    near = from_other_half(jnp.concatenate([large_rows[large:], small_rows[small:]]))
    late_far = from_other_half(jnp.concatenate([got_large, got_small]))

    parts = 3 * (qkv_weight.shape[2] // 3 // HEAD_DIM)
    qkv_cols = after(qkv_weight[0], first_got).reshape(width, parts, HEAD_DIM)
    qkv_cols = jnp.pad(qkv_cols, ((0, 0), (0, 0), (0, LANES - HEAD_DIM))).reshape(width, parts * LANES)

    proj_rows = after(proj_weight[0], first_got).T
    proj_half = lax.dynamic_slice_in_dim(proj_rows, core * HEAD_DIM, HEAD_DIM)
    proj_all = lax.all_gather(proj_half, ("cfg", "tok"), axis_index_groups=cube_groups(), tiled=True)

    up_cols, down_cols = up_weight[0], down_weight[0]
    sent = jnp.where(core == 0, after(up_cols, first_got), after(down_cols, first_got)).T
    got = permute_by(after(sent, got_large), [GROUP // 2] * 2)
    other = from_other_half(got)

    early = qkv_rows(
        modulation, qkv_cols, (hidden_in, large_rows, small_rows, near), (0, large, small, 0), "qkv_early"
    )
    late = qkv_rows(modulation, qkv_cols, (got_large, got_small, late_far), (0, 0, 0), "qkv_late")
    mine, sent_heads = attention(piece_rows, early, late, cap)
    zmate = permute_by(sent_heads, [GROUP // 2] * 2)
    plane = []
    for j in range(1, GROUP // 2):
        both = jnp.concatenate([a[:, j * cap : (j + 1) * cap] for a in (mine, zmate)], axis=1)
        plane.append(permute_by(both, [j, j]))
    mid, mlp_in = project(modulation, hidden_in, proj_all, mine, zmate, plane)

    side = permute_by(mlp_in, (1, 2))
    across = permute_by(jnp.concatenate([mlp_in, side]), (2, 1))
    part = mlp_rows((mlp_in, side), up_cols, down_cols, got, other, F32, "mlp_near")
    part_far = mlp_rows((across,), up_cols, down_cols, got, other, BF16, "mlp_far")
    first = permute_by(part_far, (2, 1))
    second = permute_by((part[cap:] + first[cap:].astype(F32)).astype(BF16), (1, 2))
    block_rows, pred = final(
        piece_rows, guidance, modulation, mid, part, first, second, final_weight
    )
    guided = pred + from_other_half(pred)
    coef_pair = lax.dynamic_index_in_dim(solver_coef, latent, 0, keepdims=False)
    own_count = piece_rows[latent, member]
    stepped = coef_pair[0] * noisy_latent - coef_pair[1] * guided
    valid = jnp.arange(cap, dtype=jnp.int32) < own_count
    next_latent = jnp.where(valid[:, None], stepped, jnp.zeros_like(stepped))
    return (next_latent, block_rows[None])


def solution(mesh):
    placed = (
        P("tok", None),
        P("tok", None),
        P(),
        P("cfg", None, None, None),
        P("tok", None, None),
        P("tok", None, None),
        P("tok", None, None),
        P("tok", None, None),
        P(),
        P(),
        P(),
    )
    return jax.shard_map(
        shards,
        mesh=mesh,
        in_specs=placed,
        out_specs=(P("tok", None), P("cfg", "tok", None)),
        check_vma=False,
    )
```

```python
import functools
import math

import jax
import jax.numpy as jnp
from jax import lax
from jax.experimental import pallas as pl
from jax.experimental.pallas import tpu as pltpu
from jax.sharding import PartitionSpec as P

HEAD_DIM = 72
GROUP = 8
LEN = 1024
LANES = 128
ALIGN = 16
LARGE = ((1, 2, 4), (4, 1, 2))
SMALL = (2, 4, 1)
PROJ = ((4, 1, 2), (4, 2, 1))
HEADS_TO = ((2, 4, 1), (4, 1, 2))
FAR_EARLY = 224
F32 = jnp.float32
BF16 = jnp.bfloat16


def permute_by(block, offsets):
    count = lax.axis_size("tok")
    route = [
        (half * count + i, half * count + (i ^ offset))
        for half, offset in enumerate(offsets)
        for i in range(count)
    ]
    return lax.ppermute(block, ("cfg", "tok"), route)


def from_other_half(block):
    return lax.ppermute(block, "cfg", [(0, 1), (1, 0)])


def after(value, *earlier):
    return lax.optimization_barrier((value,) + earlier)[0]


def place():
    pos = lax.axis_index("tok")
    return lax.axis_index("cfg"), pos // GROUP, pos % GROUP


def normalized(values):
    center = values - jnp.mean(values, axis=-1, keepdims=True)
    spread = jnp.mean(center * center, axis=-1, keepdims=True)
    return center * lax.rsqrt(spread + 1e-06)


def mod_row(mod_ref, latent, k):
    return mod_ref[latent, k : k + 1, :]


def call(kernel, out_shape, operands, scratch=(), specs=None, flops=0, name=None, vmem=40):
    whole = pl.BlockSpec(memory_space=pltpu.VMEM)
    moved = sum(math.prod(o.shape) * o.dtype.itemsize for o in operands)
    return pl.pallas_call(
        kernel,
        out_shape=out_shape,
        in_specs=specs or [whole] * len(operands),
        out_specs=jax.tree.map(lambda _: whole, out_shape),
        scratch_shapes=list(scratch),
        compiler_params=pltpu.CompilerParams(vmem_limit_bytes=vmem << 20),
        cost_estimate=pl.CostEstimate(flops=flops, bytes_accessed=moved, transcendentals=0),
        name=name,
    )(*operands)


def qkv_kernel(mod_ref, weight_ref, *refs):
    row_refs, out_ref, normed, padded = refs[:-3], refs[-3], refs[-2], refs[-1]
    _, latent, _ = place()
    shift, scale = mod_row(mod_ref, latent, 0), 1.0 + mod_row(mod_ref, latent, 1)
    chunk = 32
    at = 0
    for ref in row_refs:
        for low in range(0, ref.shape[0], chunk):
            rows = ref[low : low + chunk, :].astype(F32)
            normed[at : at + chunk, :] = (normalized(rows) * scale + shift).astype(BF16)
            at += chunk
    weight = weight_ref[...].astype(F32)
    unused = jnp.zeros((LANES - HEAD_DIM, weight.shape[1]), F32)
    for part in range(weight.shape[0] // HEAD_DIM):
        rows = jnp.concatenate([weight[part * HEAD_DIM : (part + 1) * HEAD_DIM], unused])
        padded[part * LANES : (part + 1) * LANES, :] = rows.astype(BF16)
    lane = lax.broadcasted_iota(jnp.int32, (1, padded.shape[0]), 1)
    width = padded.shape[0] // 3
    factor = jnp.where(lane < width, HEAD_DIM ** (-0.5) * math.log2(math.e), 1.0)
    ones = jnp.where((lane >= 2 * width) & (lane % LANES == HEAD_DIM), 1.0, 0.0)
    block = at // 2
    for low in range(0, at, block):
        out = lax.dot_general(
            normed[low : low + block, :], padded[...], (((1,), (1,)), ((), ())), preferred_element_type=F32
        )
        out_ref[low : low + block, :] = (out * factor + ones).astype(BF16)


def qkv_rows(modulation, weight, pieces, name):
    count = sum(p.shape[0] for p in pieces)
    parts, width = weight.shape[0] // HEAD_DIM, weight.shape[1]
    return call(
        qkv_kernel,
        jax.ShapeDtypeStruct((count, parts * LANES), BF16),
        (modulation, weight) + tuple(pieces),
        scratch=[pltpu.VMEM((count, width), BF16), pltpu.VMEM((parts * LANES, width), BF16)],
        flops=2 * count * width * parts * LANES,
        name=name,
    )


def position(order, offset):
    return sum(1 << i for i, bit in enumerate(order) if offset & bit)


def spread(order, index):
    return sum(bit for i, bit in enumerate(order) if index >> i & 1)


def attention_kernel(cap, packed_rows, counts_ref, early_ref, late_ref, near_ref, far_ref, packed, out):
    core, latent, member = place()
    half = cap // 2
    large, small = 2 * half // 3, half // 3
    width = early_ref.shape[1] // 3
    heads = width // LANES
    counts = [counts_ref[latent, member ^ d] for d in range(GROUP)]
    starts = [jnp.int32(0)]
    for d in range(GROUP):
        starts.append(starts[-1] + (counts[d] + ALIGN - 1) // ALIGN * ALIGN)
    total_rows = packed.shape[0]
    spare = total_rows - LEN
    packed[LEN:, :] = jnp.zeros((spare, packed.shape[1]), BF16)
    for d in range(GROUP):
        for k in range(2):
            away = (core != k).astype(jnp.int32)
            for is_small in range(2):
                size = small if is_small else large
                first = k * half + is_small * large
                where = position(SMALL if is_small else LARGE[k], d)
                if where == 0:
                    rows = early_ref[first : first + size, :]
                elif where < 4:
                    base = cap + is_small * 3 * large + (where - 1) * size
                    base = pl.multiple_of(base + away * (3 * half), 32)
                    rows = early_ref[pl.ds(base, size), :]
                else:
                    base = is_small * 4 * large + (where - 4) * size
                    base = pl.multiple_of(base + away * (4 * half), 32)
                    rows = late_ref[pl.ds(base, size), :]
                packed[pl.ds(pl.multiple_of(starts[d] + first, ALIGN), size), :] = rows
    slot = lax.broadcasted_iota(jnp.int32, (1, packed_rows), 1)
    valid = jnp.zeros((1, packed_rows), jnp.bool_)
    for d in range(GROUP):
        valid = valid | ((slot >= starts[d]) & (slot < starts[d] + counts[d]))
    bias = jnp.where(valid, 0.0, -1e30)
    out[LEN:, :] = jnp.zeros((spare, out.shape[1]), F32)
    block = packed_rows // 3
    for low in range(0, packed_rows, block):
        for head in range(heads):
            lanes = head * LANES
            queries = packed[low : low + block, lanes : lanes + LANES]
            keys = packed[:packed_rows, width + lanes : width + lanes + LANES]
            values = packed[:packed_rows, 2 * width + lanes : 2 * width + lanes + LANES]
            scores = lax.dot_general(
                queries, keys, (((1,), (1,)), ((), ())), preferred_element_type=F32
            )
            scores = scores + bias
            peak = jnp.max(scores, axis=-1, keepdims=True)
            probs = jnp.exp2(scores - peak).astype(BF16)
            mixed = jnp.dot(probs, values, preferred_element_type=F32)
            mixed = mixed / mixed[:, HEAD_DIM : HEAD_DIM + 1]
            out[low : low + block, lanes : lanes + LANES] = mixed
    targets = [
        jnp.where(core == 0, starts[spread(HEADS_TO[0], j)], starts[spread(HEADS_TO[1], j)])
        for j in range(GROUP)
    ]
    for pair in range(0, GROUP, 2):
        columns = []
        for head in range(heads):
            rows = [
                out[pl.ds(pl.multiple_of(targets[j], ALIGN), cap), head * LANES : (head + 1) * LANES]
                for j in (pair, pair + 1)
            ]
            columns.append(jnp.concatenate(rows).T[:HEAD_DIM])
        dest = near_ref if pair < GROUP // 2 else far_ref
        at = pair % (GROUP // 2) * cap
        dest[:, at : at + 2 * cap] = jnp.concatenate(columns).astype(BF16)


def attention(piece_rows, early, late, cap):
    packed_rows = LEN + GROUP * ALIGN
    total = -(-(packed_rows + cap) // 32) * 32
    width = early.shape[1] // 3
    heads = width // LANES
    shape = jax.ShapeDtypeStruct((heads * HEAD_DIM, GROUP // 2 * cap), BF16)
    return call(
        functools.partial(attention_kernel, cap, packed_rows),
        (shape, shape),
        (piece_rows, early, late),
        scratch=[pltpu.VMEM((total, 3 * width), BF16), pltpu.VMEM((total, width), F32)],
        specs=[pl.BlockSpec(memory_space=pltpu.SMEM)] + [pl.BlockSpec(memory_space=pltpu.VMEM)] * 2,
        flops=4 * heads * packed_rows * packed_rows * LANES,
        name="attend",
    )


def project_kernel(cap, mod_ref, hidden_ref, mine_ref, mate_ref, *refs):
    proj_refs, plane_refs = refs[:8], refs[8 : 8 + GROUP // 2 - 1]
    mid_ref, low_ref, high_ref, flat, weights = refs[8 + GROUP // 2 - 1 :]
    core, latent, member = place()
    heads = mine_ref.shape[0] // HEAD_DIM

    def put(block, j):
        offset = jnp.where(core == 0, spread(HEADS_TO[0], j), spread(HEADS_TO[1], j))
        for head in range(heads):
            rows = block[head * HEAD_DIM : (head + 1) * HEAD_DIM]
            flat[head * GROUP + offset] = rows

    put(mine_ref[...][:, :cap].astype(F32), 0)
    put(mate_ref[...][:, :cap].astype(F32), GROUP // 2)
    for j, ref in enumerate(plane_refs):
        both = ref[...].astype(F32)
        put(both[:, :cap], j + 1)
        put(both[:, cap:], (j + 1) ^ (GROUP // 2))
    for away in range(2):
        head = core if away == 0 else 1 - core
        at = 0
        for ref in proj_refs[4 * away : 4 * away + 4]:
            block = ref[...].astype(F32)
            for row in range(0, block.shape[0], HEAD_DIM):
                offset = jnp.where(head == 0, spread(PROJ[0], at), spread(PROJ[1], at))
                weights[head * GROUP + offset] = block[row : row + HEAD_DIM]
                at += 1
    stacked = flat[...].reshape(heads * GROUP * HEAD_DIM, cap).astype(BF16)
    proj = weights[...].reshape(heads * GROUP * HEAD_DIM, weights.shape[2]).astype(BF16)
    attn_out = lax.dot_general(stacked, proj, (((0,), (0,)), ((), ())), preferred_element_type=F32)
    mid = hidden_ref[...].astype(F32) + mod_row(mod_ref, latent, 2) * attn_out
    mid_ref[...] = mid
    scale, shift = 1.0 + mod_row(mod_ref, latent, 4), mod_row(mod_ref, latent, 3)
    mlp_in = (normalized(mid) * scale + shift).astype(BF16)
    low_ref[...] = mlp_in[: cap // 2]
    high_ref[...] = mlp_in[cap // 2 :]


def project(modulation, hidden_in, proj_parts, mine, mate, plane):
    cap, width = hidden_in.shape
    heads = mine.shape[0] // HEAD_DIM
    half = jax.ShapeDtypeStruct((cap // 2, width), BF16)
    return call(
        functools.partial(project_kernel, cap),
        (jax.ShapeDtypeStruct((cap, width), F32), half, half),
        (modulation, hidden_in, mine, mate) + tuple(proj_parts) + tuple(plane),
        scratch=[
            pltpu.VMEM((heads * GROUP, HEAD_DIM, cap), F32),
            pltpu.VMEM((heads * GROUP, HEAD_DIM, width), F32),
        ],
        flops=2 * cap * width * width,
        name="project",
    )


def pack_kernel(up_ref, down_ref, *refs):
    far_refs, (up_all, down_all, sems) = refs[:-3], refs[-3:]
    core, _, _ = place()
    hidden, parts = up_ref.shape[0], len(far_refs) // 2
    own = [
        pltpu.make_async_copy(up_ref, up_all.at[pl.ds(0, hidden)], sems.at[2 * parts]),
        pltpu.make_async_copy(down_ref, down_all.at[pl.ds(0, hidden)], sems.at[2 * parts + 1]),
    ]
    for copy in own:
        copy.start()

    def fetch(dests):
        copies = []
        for d, dest in enumerate(dests):
            at = hidden
            for ref in far_refs[parts * d : parts * (d + 1)]:
                rows = ref.shape[0]
                copies.append(
                    pltpu.make_async_copy(ref, dest.at[pl.ds(at, rows)], sems.at[len(copies)])
                )
                at += rows
        for copy in copies:
            copy.start()
        for copy in copies:
            copy.wait()

    pl.when(core == 0)(lambda: fetch((up_all, down_all)))
    pl.when(core == 1)(lambda: fetch((down_all, up_all)))
    for copy in own:
        copy.wait()


def pack(up, down, far):
    hidden, width = up.shape
    both = jax.ShapeDtypeStruct((2 * hidden, width), BF16)
    return call(
        pack_kernel,
        (both, both),
        (up, down) + tuple(far),
        scratch=[pltpu.SemaphoreType.DMA((2 + len(far),))],
        specs=[pl.BlockSpec(memory_space=pl.ANY)] * (2 + len(far)),
        name="pack",
    )


def mlp_kernel(row_count, out_count, up_ref, down_ref, *refs):
    row_refs, out_refs, rows = refs[:row_count], refs[row_count:-1], refs[-1]
    at = 0
    for ref in row_refs:
        rows[at : at + ref.shape[0], :] = ref[...]
        at += ref.shape[0]
    units = lax.dot_general(
        rows[...], up_ref[...], (((1,), (1,)), ((), ())), preferred_element_type=F32
    )
    units = 0.5 * units * (1.0 + jnp.tanh(0.7978845608 * (units + 0.044715 * (units * units * units))))
    partial = jnp.dot(units.astype(BF16), down_ref[...], preferred_element_type=F32)
    at = 0
    for ref in out_refs:
        ref[...] = partial[at : at + ref.shape[0]].astype(ref.dtype)
        at += ref.shape[0]


def mlp_rows(pieces, packed, out_rows, dtype, name):
    count = sum(p.shape[0] for p in pieces)
    hidden, width = packed[0].shape
    outs = tuple(jax.ShapeDtypeStruct((rows, width), dtype) for rows in out_rows)
    return call(
        functools.partial(mlp_kernel, len(pieces), len(outs)),
        outs,
        tuple(packed) + tuple(pieces),
        scratch=[pltpu.VMEM((count, width), BF16)],
        flops=4 * count * width * hidden,
        name=name,
    )


def final_kernel(
    counts_ref, guide_ref, coef_ref, mod_ref, mid_ref, part_ref, noisy_ref, weight_ref,
    first_low, first_high, second_low, second_high, block_ref, pred_ref, base_ref, total,
):
    core, latent, member = place()
    cap = mid_ref.shape[0]
    half = cap // 2
    for low, first, second in ((0, first_low, second_low), (half, first_high, second_high)):
        total[low : low + half, :] = (
            part_ref[low : low + half, :] + first[:half, :].astype(F32) + second[...].astype(F32)
        )
    rows = (mid_ref[...] + mod_row(mod_ref, latent, 5) * total[...]).astype(BF16).astype(F32)
    count = counts_ref[latent, member]
    rows = jnp.where(lax.broadcasted_iota(jnp.int32, (cap, 1), 0) < count, rows, 0.0)
    block_ref[...] = rows.astype(BF16)
    scale, shift = 1.0 + mod_row(mod_ref, latent, 7), mod_row(mod_ref, latent, 6)
    final_in = (normalized(rows) * scale + shift).astype(BF16)
    pred = lax.dot_general(
        weight_ref[...], final_in, (((1,), (1,)), ((), ())), preferred_element_type=F32
    )
    guide = guide_ref[latent]
    valid = lax.broadcasted_iota(jnp.int32, (1, cap), 1) < count
    weighted = (-coef_ref[latent, 1] * jnp.where(core == 0, guide, 1.0 - guide)) * pred
    pred_ref[...] = jnp.where(valid, weighted, 0.0)
    base_ref[...] = jnp.where(valid, coef_ref[latent, 0] * noisy_ref[...], 0.0)


def final(scalars, modulation, mid, part, noisy, weight, firsts, seconds):
    cap, width = mid.shape
    smem, vmem = pl.BlockSpec(memory_space=pltpu.SMEM), pl.BlockSpec(memory_space=pltpu.VMEM)
    flat = jax.ShapeDtypeStruct(noisy.shape, F32)
    return call(
        final_kernel,
        (jax.ShapeDtypeStruct((cap, width), BF16), flat, flat),
        tuple(scalars) + (modulation, mid, part, noisy, weight) + tuple(firsts) + tuple(seconds),
        scratch=[pltpu.VMEM((cap, width), F32)],
        specs=[smem] * 3 + [vmem] * 9,
        flops=2 * cap * width * weight.shape[0],
        name="finish",
    )


def shards(
    hidden_in,
    noisy_latent,
    piece_rows,
    modulation,
    qkv_weight,
    proj_weight,
    up_weight,
    down_weight,
    final_weight,
    guidance,
    solver_coef,
):
    cap, width = hidden_in.shape
    half = cap // 2
    large, small = 2 * half // 3, half // 3
    core, _, _ = place()
    modulation = modulation[0]
    qkv_rows_t, proj_t, up_t, down_t = (
        w[0].T for w in (qkv_weight, proj_weight, up_weight, down_weight)
    )

    large_rows = lax.dynamic_slice_in_dim(hidden_in, core * half, large)
    small_rows = lax.dynamic_slice_in_dim(hidden_in, core * half + large, small)
    large_rows, small_rows = lax.optimization_barrier((large_rows, small_rows))
    hidden = up_t.shape[0]
    cuts = (0, FAR_EARLY, hidden)
    got, away = [], []
    for step in range(3):
        got_large = permute_by(large_rows, [order[step] for order in LARGE])
        got_small = permute_by(small_rows, [SMALL[step]] * 2)
        if step < 2:
            got_large, got_small = lax.optimization_barrier((got_large, got_small))
            large_rows = jnp.concatenate([large_rows, got_large])
            small_rows = jnp.concatenate([small_rows, got_small])
        if step == 0:
            up_t, down_t, proj_own, _ = lax.optimization_barrier((up_t, down_t, proj_t, got_large))
            sent = [
                jnp.where(core == 0, up_t[low:high], down_t[low:high])
                for low, high in zip(cuts[:-1], cuts[1:])
            ]
            proj_rows = lax.dynamic_slice_in_dim(proj_own, core * HEAD_DIM, HEAD_DIM)
            proj_other = lax.dynamic_slice_in_dim(proj_own, (1 - core) * HEAD_DIM, HEAD_DIM)
        if step == 1:
            proj_rows = after(proj_rows, got_large)
        if step == 2:
            early = qkv_rows(
                modulation,
                qkv_rows_t,
                (hidden_in, got[0][0], got[1][0], got[0][1], got[1][1])
                + (away[0][0], away[1][0], away[0][1], away[1][1]),
                "qkv_early",
            )
            got_large, got_small, early, *sent = lax.optimization_barrier(
                (got_large, got_small, early, *sent)
            )
        got.append((got_large, got_small))
        away.append((from_other_half(got_large), from_other_half(got_small)))
    far = [permute_by(sent[0], [GROUP // 2] * 2)]

    proj_parts = [proj_rows]
    late = qkv_rows(modulation, qkv_rows_t, got[2] + away[2], "qkv_late")
    for step in range(3):
        if step:
            proj_rows = after(proj_rows, *(away[2] if step == 1 else (late,)))
        proj_parts.append(permute_by(proj_rows, [order[step] for order in PROJ]))
        if step < 2:
            proj_rows = jnp.concatenate([proj_rows, proj_parts[-1]])
    proj_parts += [proj_other] + [from_other_half(rows) for rows in proj_parts[1:4]]
    mine, sent_heads = attention(piece_rows, early, late, cap)
    mate = permute_by(sent_heads, [order[2] for order in HEADS_TO])
    mate, far[0] = lax.optimization_barrier((mate, far[0]))
    far.append(permute_by(after(sent[1], mate), [GROUP // 2] * 2))
    far += [from_other_half(rows) for rows in far]
    plane = []
    for j in range(1, GROUP // 2):
        both = jnp.concatenate([a[:, j * cap : (j + 1) * cap] for a in (mine, mate)], axis=1)
        plane.append(permute_by(both, [spread(order, j) for order in HEADS_TO]))
    mid, low_rows, high_rows = project(modulation, hidden_in, proj_parts, mine, mate, plane)

    chunks = (low_rows, high_rows)
    side = [permute_by(rows, (1, 2)) for rows in chunks]
    across = [permute_by(jnp.concatenate([o, s]), (2, 1)) for o, s in zip(chunks, side)]
    packed = pack(up_t, down_t, far)
    sums = [
        mlp_rows((rows,), packed, (cap,), BF16, f"mlp_far{i}")[0] for i, rows in enumerate(across)
    ]
    firsts = [permute_by(rows, (2, 1)) for rows in sums]
    part, *side_parts = mlp_rows(
        (after(chunks[0], *sums), chunks[1]) + tuple(side), packed, (cap, half, half), F32, "mlp_near"
    )
    seconds = [
        permute_by((rows + first[half:].astype(F32)).astype(BF16), (1, 2))
        for rows, first in zip(side_parts, firsts)
    ]
    block_rows, pred, base = final(
        (piece_rows, guidance, solver_coef),
        modulation,
        mid,
        part,
        noisy_latent.T,
        final_weight.T,
        firsts,
        seconds,
    )
    next_latent = base + (pred + from_other_half(pred))
    return (next_latent.T, block_rows[None])


def solution(mesh):
    placed = (
        P("tok", None),
        P("tok", None),
        P(),
        P("cfg", None, None, None),
        P("tok", None, None),
        P("tok", None, None),
        P("tok", None, None),
        P("tok", None, None),
        P(),
        P(),
        P(),
    )
    return jax.shard_map(
        shards,
        mesh=mesh,
        in_specs=placed,
        out_specs=(P("tok", None), P("cfg", "tok", None)),
        check_vma=False,
    )
```

```python
import functools
import math

import jax
import jax.numpy as jnp
from jax import lax
from jax.experimental import pallas as pl
from jax.experimental.pallas import tpu as pltpu
from jax.sharding import PartitionSpec as P

HEAD_DIM = 72
GROUP = 8
LEN = 1024
LANES = 128
ALIGN = 16
LARGE = ((1, 2, 4), (2, 4, 1))
SMALL = (4, 1, 2)
PROJ = ((2, 4, 1), (4, 1, 2))
HEADS_TO = ((2, 4, 1), (4, 1, 2))
FAR_EARLY = (96, 208)
F32 = jnp.float32
BF16 = jnp.bfloat16


def permute_by(block, offsets):
    count = lax.axis_size("tok")
    route = [
        (half * count + i, half * count + (i ^ offset))
        for half, offset in enumerate(offsets)
        for i in range(count)
    ]
    return lax.ppermute(block, ("cfg", "tok"), route)


def from_other_half(block):
    return lax.ppermute(block, "cfg", [(0, 1), (1, 0)])


def after(value, *earlier):
    return lax.optimization_barrier((value,) + earlier)[0]


def place():
    pos = lax.axis_index("tok")
    return lax.axis_index("cfg"), pos // GROUP, pos % GROUP


def normalized(values):
    center = values - jnp.mean(values, axis=-1, keepdims=True)
    spread = jnp.mean(center * center, axis=-1, keepdims=True)
    return center * lax.rsqrt(spread + 1e-06)


def mod_row(mod_ref, latent, k):
    return mod_ref[latent, k : k + 1, :]


def call(kernel, out_shape, operands, scratch=(), specs=None, flops=0, name=None, vmem=40):
    whole = pl.BlockSpec(memory_space=pltpu.VMEM)
    moved = sum(math.prod(o.shape) * o.dtype.itemsize for o in operands)
    return pl.pallas_call(
        kernel,
        out_shape=out_shape,
        in_specs=specs or [whole] * len(operands),
        out_specs=jax.tree.map(lambda _: whole, out_shape),
        scratch_shapes=list(scratch),
        compiler_params=pltpu.CompilerParams(vmem_limit_bytes=vmem << 20),
        cost_estimate=pl.CostEstimate(flops=flops, bytes_accessed=moved, transcendentals=0),
        name=name,
    )(*operands)


def qkv_kernel(row_counts, mod_ref, weight_ref, *refs):
    row_refs, out_ref, normed, padded = refs[:-3], refs[-3], refs[-2], refs[-1]
    _, latent, _ = place()
    shift, scale = mod_row(mod_ref, latent, 0), 1.0 + mod_row(mod_ref, latent, 1)
    chunk = 32
    at = 0
    for ref, count in zip(row_refs, row_counts):
        for low in range(0, count, chunk):
            rows = ref[low : low + chunk, :].astype(F32)
            normed[at : at + chunk, :] = (normalized(rows) * scale + shift).astype(BF16)
            at += chunk
    weight = weight_ref[...].astype(F32)
    unused = jnp.zeros((LANES - HEAD_DIM, weight.shape[1]), F32)
    for part in range(weight.shape[0] // HEAD_DIM):
        rows = jnp.concatenate([weight[part * HEAD_DIM : (part + 1) * HEAD_DIM], unused])
        padded[part * LANES : (part + 1) * LANES, :] = rows.astype(BF16)
    lane = lax.broadcasted_iota(jnp.int32, (1, padded.shape[0]), 1)
    width = padded.shape[0] // 3
    factor = jnp.where(lane < width, HEAD_DIM ** (-0.5) * math.log2(math.e), 1.0)
    ones = jnp.where((lane >= 2 * width) & (lane % LANES == HEAD_DIM), 1.0, 0.0)
    block = at // 2
    for low in range(0, at, block):
        out = lax.dot_general(
            normed[low : low + block, :], padded[...], (((1,), (1,)), ((), ())), preferred_element_type=F32
        )
        out_ref[low : low + block, :] = (out * factor + ones).astype(BF16)


def qkv_rows(modulation, weight, pieces, row_counts, name):
    count = sum(row_counts)
    parts, width = weight.shape[0] // HEAD_DIM, weight.shape[1]
    return call(
        functools.partial(qkv_kernel, row_counts),
        jax.ShapeDtypeStruct((count, parts * LANES), BF16),
        (modulation, weight) + tuple(pieces),
        scratch=[pltpu.VMEM((count, width), BF16), pltpu.VMEM((parts * LANES, width), BF16)],
        flops=2 * count * width * parts * LANES,
        name=name,
    )


def position(order, offset):
    return sum(1 << i for i, bit in enumerate(order) if offset & bit)


def spread(order, index):
    return sum(bit for i, bit in enumerate(order) if index >> i & 1)


def attention_kernel(cap, packed_rows, counts_ref, early_ref, late_ref, near_ref, far_ref, packed, out):
    core, latent, member = place()
    half = cap // 2
    large, small = 2 * half // 3, half // 3
    width = early_ref.shape[1] // 3
    heads = width // LANES
    counts = [counts_ref[latent, member ^ d] for d in range(GROUP)]
    starts = [jnp.int32(0)]
    for d in range(GROUP):
        starts.append(starts[-1] + (counts[d] + ALIGN - 1) // ALIGN * ALIGN)
    total_rows = packed.shape[0]
    spare = total_rows - LEN
    packed[LEN:, :] = jnp.zeros((spare, packed.shape[1]), BF16)
    for d in range(GROUP):
        for k in range(2):
            away = (core != k).astype(jnp.int32)
            for is_small in range(2):
                size = small if is_small else large
                first = k * half + is_small * large
                where = position(SMALL if is_small else LARGE[k], d)
                if where == 0:
                    rows = early_ref[first : first + size, :]
                elif where < 4:
                    base = cap + is_small * 3 * large + (where - 1) * size
                    base = pl.multiple_of(base + away * (3 * half), 32)
                    rows = early_ref[pl.ds(base, size), :]
                else:
                    base = is_small * 4 * large + (where - 4) * size
                    base = pl.multiple_of(base + away * (4 * half), 32)
                    rows = late_ref[pl.ds(base, size), :]
                packed[pl.ds(pl.multiple_of(starts[d] + first, ALIGN), size), :] = rows
    slot = lax.broadcasted_iota(jnp.int32, (1, packed_rows), 1)
    valid = jnp.zeros((1, packed_rows), jnp.bool_)
    for d in range(GROUP):
        valid = valid | ((slot >= starts[d]) & (slot < starts[d] + counts[d]))
    bias = jnp.where(valid, 0.0, -1e30)
    out[LEN:, :] = jnp.zeros((spare, out.shape[1]), F32)
    block = packed_rows // 3
    for low in range(0, packed_rows, block):
        for head in range(heads):
            lanes = head * LANES
            queries = packed[low : low + block, lanes : lanes + LANES]
            keys = packed[:packed_rows, width + lanes : width + lanes + LANES]
            values = packed[:packed_rows, 2 * width + lanes : 2 * width + lanes + LANES]
            scores = lax.dot_general(
                queries, keys, (((1,), (1,)), ((), ())), preferred_element_type=F32
            )
            scores = scores + bias
            peak = jnp.max(scores, axis=-1, keepdims=True)
            probs = jnp.exp2(scores - peak).astype(BF16)
            mixed = jnp.dot(probs, values, preferred_element_type=F32)
            mixed = mixed / mixed[:, HEAD_DIM : HEAD_DIM + 1]
            out[low : low + block, lanes : lanes + LANES] = mixed
    targets = [
        jnp.where(core == 0, starts[spread(HEADS_TO[0], j)], starts[spread(HEADS_TO[1], j)])
        for j in range(GROUP)
    ]
    for pair in range(0, GROUP, 2):
        columns = []
        for head in range(heads):
            rows = [
                out[pl.ds(pl.multiple_of(targets[j], ALIGN), cap), head * LANES : (head + 1) * LANES]
                for j in (pair, pair + 1)
            ]
            columns.append(jnp.concatenate(rows).T[:HEAD_DIM])
        dest = near_ref if pair < GROUP // 2 else far_ref
        at = pair % (GROUP // 2) * cap
        dest[:, at : at + 2 * cap] = jnp.concatenate(columns).astype(BF16)


def attention(piece_rows, early, late, cap):
    packed_rows = LEN + GROUP * ALIGN
    total = -(-(packed_rows + cap) // 32) * 32
    width = early.shape[1] // 3
    heads = width // LANES
    shape = jax.ShapeDtypeStruct((heads * HEAD_DIM, GROUP // 2 * cap), BF16)
    return call(
        functools.partial(attention_kernel, cap, packed_rows),
        (shape, shape),
        (piece_rows, early, late),
        scratch=[pltpu.VMEM((total, 3 * width), BF16), pltpu.VMEM((total, width), F32)],
        specs=[pl.BlockSpec(memory_space=pltpu.SMEM)] + [pl.BlockSpec(memory_space=pltpu.VMEM)] * 2,
        flops=4 * heads * packed_rows * packed_rows * LANES,
        name="attend",
    )


def project_kernel(cap, mod_ref, hidden_ref, mine_ref, mate_ref, *refs):
    proj_refs, plane_refs = refs[:8], refs[8 : 8 + GROUP // 2 - 1]
    mid_ref, low_ref, high_ref, flat, weights = refs[8 + GROUP // 2 - 1 :]
    core, latent, member = place()
    heads = mine_ref.shape[0] // HEAD_DIM

    def put(block, j):
        offset = jnp.where(core == 0, spread(HEADS_TO[0], j), spread(HEADS_TO[1], j))
        for head in range(heads):
            rows = block[head * HEAD_DIM : (head + 1) * HEAD_DIM]
            flat[head * GROUP + offset] = rows

    put(mine_ref[...][:, :cap].astype(F32), 0)
    put(mate_ref[...][:, :cap].astype(F32), GROUP // 2)
    for j, ref in enumerate(plane_refs):
        both = ref[...].astype(F32)
        put(both[:, :cap], j + 1)
        put(both[:, cap:], (j + 1) ^ (GROUP // 2))
    for away in range(2):
        head = core if away == 0 else 1 - core
        at = 0
        for blocks, ref in zip((1, 1, 2, 4), proj_refs[4 * away : 4 * away + 4]):
            block = ref[ref.shape[0] - blocks * HEAD_DIM :, :].astype(F32)
            for row in range(0, block.shape[0], HEAD_DIM):
                offset = jnp.where(head == 0, spread(PROJ[0], at), spread(PROJ[1], at))
                weights[head * GROUP + offset] = block[row : row + HEAD_DIM]
                at += 1
    stacked = flat[...].reshape(heads * GROUP * HEAD_DIM, cap).astype(BF16)
    proj = weights[...].reshape(heads * GROUP * HEAD_DIM, weights.shape[2]).astype(BF16)
    attn_out = lax.dot_general(stacked, proj, (((0,), (0,)), ((), ())), preferred_element_type=F32)
    mid = hidden_ref[...].astype(F32) + mod_row(mod_ref, latent, 2) * attn_out
    mid_ref[...] = mid
    scale, shift = 1.0 + mod_row(mod_ref, latent, 4), mod_row(mod_ref, latent, 3)
    mlp_in = (normalized(mid) * scale + shift).astype(BF16)
    low_ref[...] = mlp_in[: cap // 2]
    high_ref[...] = mlp_in[cap // 2 :]


def project(modulation, hidden_in, proj_parts, mine, mate, plane):
    cap, width = hidden_in.shape
    heads = mine.shape[0] // HEAD_DIM
    half = jax.ShapeDtypeStruct((cap // 2, width), BF16)
    return call(
        functools.partial(project_kernel, cap),
        (jax.ShapeDtypeStruct((cap, width), F32), half, half),
        (modulation, hidden_in, mine, mate) + tuple(proj_parts) + tuple(plane),
        scratch=[
            pltpu.VMEM((heads * GROUP, HEAD_DIM, cap), F32),
            pltpu.VMEM((heads * GROUP, HEAD_DIM, width), F32),
        ],
        flops=2 * cap * width * width,
        name="project",
    )


def pack_kernel(up_ref, down_ref, *refs):
    far_refs, (up_all, down_all, sems) = refs[:-3], refs[-3:]
    core, _, _ = place()
    hidden, parts = up_ref.shape[0], len(far_refs) // 2
    own = [
        pltpu.make_async_copy(up_ref, up_all.at[pl.ds(0, hidden)], sems.at[2 * parts]),
        pltpu.make_async_copy(down_ref, down_all.at[pl.ds(0, hidden)], sems.at[2 * parts + 1]),
    ]
    for copy in own:
        copy.start()

    def fetch(dests):
        copies = []
        for d, dest in enumerate(dests):
            at = hidden
            for ref in far_refs[parts * d : parts * (d + 1)]:
                rows = ref.shape[0]
                copies.append(
                    pltpu.make_async_copy(ref, dest.at[pl.ds(at, rows)], sems.at[len(copies)])
                )
                at += rows
        for copy in copies:
            copy.start()
        for copy in copies:
            copy.wait()

    pl.when(core == 0)(lambda: fetch((up_all, down_all)))
    pl.when(core == 1)(lambda: fetch((down_all, up_all)))
    for copy in own:
        copy.wait()


def pack(up, down, far):
    hidden, width = up.shape
    both = jax.ShapeDtypeStruct((2 * hidden, width), BF16)
    return call(
        pack_kernel,
        (both, both),
        (up, down) + tuple(far),
        scratch=[pltpu.SemaphoreType.DMA((2 + len(far),))],
        specs=[pl.BlockSpec(memory_space=pl.ANY)] * (2 + len(far)),
        name="pack",
    )


def mlp_kernel(row_count, out_count, up_ref, down_ref, *refs):
    row_refs, out_refs, rows = refs[:row_count], refs[row_count:-1], refs[-1]
    at = 0
    for ref in row_refs:
        rows[at : at + ref.shape[0], :] = ref[...]
        at += ref.shape[0]
    units = lax.dot_general(
        rows[...], up_ref[...], (((1,), (1,)), ((), ())), preferred_element_type=F32
    )
    units = 0.5 * units * (1.0 + jnp.tanh(0.7978845608 * (units + 0.044715 * (units * units * units))))
    partial = jnp.dot(units.astype(BF16), down_ref[...], preferred_element_type=F32)
    at = 0
    for ref in out_refs:
        ref[...] = partial[at : at + ref.shape[0]].astype(ref.dtype)
        at += ref.shape[0]


def mlp_rows(pieces, packed, out_rows, dtype, name):
    count = sum(p.shape[0] for p in pieces)
    hidden, width = packed[0].shape
    outs = tuple(jax.ShapeDtypeStruct((rows, width), dtype) for rows in out_rows)
    return call(
        functools.partial(mlp_kernel, len(pieces), len(outs)),
        outs,
        tuple(packed) + tuple(pieces),
        scratch=[pltpu.VMEM((count, width), BF16)],
        flops=4 * count * width * hidden,
        name=name,
    )


def final_kernel(
    counts_ref, guide_ref, coef_ref, mod_ref, mid_ref, part_ref, noisy_ref, weight_ref,
    first_low, first_high, second_low, second_high, block_ref, pred_ref, base_ref, total,
):
    core, latent, member = place()
    cap = mid_ref.shape[0]
    half = cap // 2
    for low, first, second in ((0, first_low, second_low), (half, first_high, second_high)):
        total[low : low + half, :] = (
            part_ref[low : low + half, :] + first[:half, :].astype(F32) + second[...].astype(F32)
        )
    rows = (mid_ref[...] + mod_row(mod_ref, latent, 5) * total[...]).astype(BF16).astype(F32)
    count = counts_ref[latent, member]
    rows = jnp.where(lax.broadcasted_iota(jnp.int32, (cap, 1), 0) < count, rows, 0.0)
    block_ref[...] = rows.astype(BF16)
    scale, shift = 1.0 + mod_row(mod_ref, latent, 7), mod_row(mod_ref, latent, 6)
    final_in = (normalized(rows) * scale + shift).astype(BF16)
    pred = lax.dot_general(
        weight_ref[...], final_in, (((1,), (1,)), ((), ())), preferred_element_type=F32
    )
    guide = guide_ref[latent]
    valid = lax.broadcasted_iota(jnp.int32, (1, cap), 1) < count
    weighted = (-coef_ref[latent, 1] * jnp.where(core == 0, guide, 1.0 - guide)) * pred
    pred_ref[...] = jnp.where(valid, weighted, 0.0)
    base_ref[...] = jnp.where(valid, coef_ref[latent, 0] * noisy_ref[...], 0.0)


def final(scalars, modulation, mid, part, noisy, weight, firsts, seconds):
    cap, width = mid.shape
    smem, vmem = pl.BlockSpec(memory_space=pltpu.SMEM), pl.BlockSpec(memory_space=pltpu.VMEM)
    flat = jax.ShapeDtypeStruct(noisy.shape, F32)
    return call(
        final_kernel,
        (jax.ShapeDtypeStruct((cap, width), BF16), flat, flat),
        tuple(scalars) + (modulation, mid, part, noisy, weight) + tuple(firsts) + tuple(seconds),
        scratch=[pltpu.VMEM((cap, width), F32)],
        specs=[smem] * 3 + [vmem] * 9,
        flops=2 * cap * width * weight.shape[0],
        name="finish",
    )


def shards(
    hidden_in,
    noisy_latent,
    piece_rows,
    modulation,
    qkv_weight,
    proj_weight,
    up_weight,
    down_weight,
    final_weight,
    guidance,
    solver_coef,
):
    cap, width = hidden_in.shape
    half = cap // 2
    large, small = 2 * half // 3, half // 3
    core, _, _ = place()
    modulation = modulation[0]
    qkv_rows_t, proj_t, up_t, down_t = (
        w[0].T for w in (qkv_weight, proj_weight, up_weight, down_weight)
    )

    large_rows = lax.dynamic_slice_in_dim(hidden_in, core * half, large)
    small_rows = lax.dynamic_slice_in_dim(hidden_in, core * half + large, small)
    large_rows, small_rows = lax.optimization_barrier((large_rows, small_rows))
    hidden = up_t.shape[0]
    cuts = (0, FAR_EARLY[0], sum(FAR_EARLY), hidden)
    proj_rows = None
    got, away = [], []
    for step in range(3):
        payload = large_rows if step == 0 else jnp.concatenate([large_rows, proj_rows])
        got_large = permute_by(payload, [order[step] for order in LARGE])
        got_small = permute_by(small_rows, [SMALL[step]] * 2)
        if step == 0:
            up_t, down_t, _ = lax.optimization_barrier((up_t, down_t, got_large))
            sent = [
                jnp.where(core == 0, up_t[low:high], down_t[low:high])
                for low, high in zip(cuts[:-1], cuts[1:])
            ]
            proj_own = [
                lax.dynamic_slice_in_dim(proj_t, head * HEAD_DIM, HEAD_DIM) for head in (core, 1 - core)
            ]
            proj_rows = proj_own[0]
        elif step == 1:
            got_large, got_small = lax.optimization_barrier((got_large, got_small))
            proj_rows = jnp.concatenate([proj_rows, got_large[2 * large :]])
        else:
            early = qkv_rows(
                modulation,
                qkv_rows_t,
                (hidden_in, got[0][0], got[1][0], got[0][1], got[1][1])
                + (away[0][0], away[1][0], away[0][1], away[1][1]),
                (cap, large, 2 * large, small, 2 * small) + (large, 2 * large, small, 2 * small),
                "qkv_early",
            )
            got_large, got_small, early, *sent = lax.optimization_barrier(
                (got_large, got_small, early, *sent)
            )
            proj_rows = jnp.concatenate([proj_rows, got_large[4 * large :]])
        if step < 2:
            large_rows = jnp.concatenate([large_rows, got_large[: large << step]])
            small_rows = jnp.concatenate([small_rows, got_small])
        got.append((got_large, got_small))
        away.append((from_other_half(got_large), from_other_half(got_small)))
    proj_last = permute_by(proj_rows, [order[2] for order in PROJ])
    far = [permute_by(sent[0], [GROUP // 2] * 2)]
    late = qkv_rows(
        modulation,
        qkv_rows_t,
        got[2] + away[2],
        (4 * large, 4 * small) * 2,
        "qkv_late",
    )
    far.append(permute_by(after(sent[1], far[0], late), [GROUP // 2] * 2))
    mine, sent_heads = attention(piece_rows, early, late, cap)
    mate = permute_by(sent_heads, [order[2] for order in HEADS_TO])
    mate, far[1], proj_last = lax.optimization_barrier((mate, far[1], proj_last))
    proj_parts = [proj_own[0], got[1][0], got[2][0], proj_last]
    proj_parts += [proj_own[1], away[1][0], away[2][0], from_other_half(proj_last)]
    plane = []
    for j in range(1, GROUP // 2):
        both = jnp.concatenate([a[:, j * cap : (j + 1) * cap] for a in (mine, mate)], axis=1)
        plane.append(permute_by(both, [spread(order, j) for order in HEADS_TO]))
    far.append(permute_by(after(sent[2], *plane), [GROUP // 2] * 2))
    mid, low_rows, high_rows = project(modulation, hidden_in, proj_parts, mine, mate, plane)

    chunks = (low_rows, high_rows)
    side = [permute_by(rows, (1, 2)) for rows in chunks]
    both = [jnp.concatenate([o, s]) for o, s in zip(chunks, side)]
    across = [permute_by(rows, (2, 1)) for rows in both]
    far[2] = after(far[2], *both)
    far += [from_other_half(rows) for rows in far]
    packed = pack(up_t, down_t, far)
    sums = [
        mlp_rows((rows,), packed, (cap,), BF16, f"mlp_far{i}")[0] for i, rows in enumerate(across)
    ]
    firsts = [permute_by(rows, (2, 1)) for rows in sums]
    part, *side_parts = mlp_rows(
        (after(chunks[0], *sums), chunks[1]) + tuple(side), packed, (cap, half, half), F32, "mlp_near"
    )
    seconds = [
        permute_by((rows + first[half:].astype(F32)).astype(BF16), (1, 2))
        for rows, first in zip(side_parts, firsts)
    ]
    block_rows, pred, base = final(
        (piece_rows, guidance, solver_coef),
        modulation,
        mid,
        part,
        noisy_latent.T,
        final_weight.T,
        firsts,
        seconds,
    )
    next_latent = base + (pred + from_other_half(pred))
    return (next_latent.T, block_rows[None])


def solution(mesh):
    placed = (
        P("tok", None),
        P("tok", None),
        P(),
        P("cfg", None, None, None),
        P("tok", None, None),
        P("tok", None, None),
        P("tok", None, None),
        P("tok", None, None),
        P(),
        P(),
        P(),
    )
    return jax.shard_map(
        shards,
        mesh=mesh,
        in_specs=placed,
        out_specs=(P("tok", None), P("cfg", "tok", None)),
        check_vma=False,
    )
```

```python
import functools
import math

import jax
import jax.numpy as jnp
from jax import lax
from jax.experimental import pallas as pl
from jax.experimental.pallas import tpu as pltpu
from jax.sharding import PartitionSpec as P

HEAD_DIM = 72
GROUP = 8
LEN = 1024
LANES = 128
ALIGN = 16
LARGE = ((1, 2, 4), (2, 4, 1))
SMALL = (4, 1, 2)
PROJ = ((2, 4, 1), (4, 1, 2))
HEADS_TO = ((2, 4, 1), (4, 1, 2))
FAR_EARLY = (64, 240, 160)
F32 = jnp.float32
BF16 = jnp.bfloat16


def permute_by(block, offsets):
    count = lax.axis_size("tok")
    route = [
        (half * count + i, half * count + (i ^ offset))
        for half, offset in enumerate(offsets)
        for i in range(count)
    ]
    return lax.ppermute(block, ("cfg", "tok"), route)


def from_other_half(block):
    return lax.ppermute(block, "cfg", [(0, 1), (1, 0)])


def after(value, *earlier):
    return lax.optimization_barrier((value,) + earlier)[0]


def place():
    pos = lax.axis_index("tok")
    return lax.axis_index("cfg"), pos // GROUP, pos % GROUP


def normalized(values):
    center = values - jnp.mean(values, axis=-1, keepdims=True)
    spread = jnp.mean(center * center, axis=-1, keepdims=True)
    return center * lax.rsqrt(spread + 1e-06)


def mod_row(mod_ref, latent, k):
    return mod_ref[latent, k : k + 1, :]


def call(kernel, out_shape, operands, scratch=(), specs=None, flops=0, name=None, vmem=40):
    whole = pl.BlockSpec(memory_space=pltpu.VMEM)
    moved = sum(math.prod(o.shape) * o.dtype.itemsize for o in operands)
    return pl.pallas_call(
        kernel,
        out_shape=out_shape,
        in_specs=specs or [whole] * len(operands),
        out_specs=jax.tree.map(lambda _: whole, out_shape),
        scratch_shapes=list(scratch),
        compiler_params=pltpu.CompilerParams(vmem_limit_bytes=vmem << 20),
        cost_estimate=pl.CostEstimate(flops=flops, bytes_accessed=moved, transcendentals=0),
        name=name,
    )(*operands)


def qkv_kernel(row_counts, mod_ref, weight_ref, *refs):
    row_refs, out_ref, normed, padded = refs[:-3], refs[-3], refs[-2], refs[-1]
    _, latent, _ = place()
    shift, scale = mod_row(mod_ref, latent, 0), 1.0 + mod_row(mod_ref, latent, 1)
    chunk = 32
    at = 0
    for ref, count in zip(row_refs, row_counts):
        for low in range(0, count, chunk):
            rows = ref[low : low + chunk, :].astype(F32)
            normed[at : at + chunk, :] = (normalized(rows) * scale + shift).astype(BF16)
            at += chunk
    weight = weight_ref[...].astype(F32)
    unused = jnp.zeros((LANES - HEAD_DIM, weight.shape[1]), F32)
    for part in range(weight.shape[0] // HEAD_DIM):
        rows = jnp.concatenate([weight[part * HEAD_DIM : (part + 1) * HEAD_DIM], unused])
        padded[part * LANES : (part + 1) * LANES, :] = rows.astype(BF16)
    lane = lax.broadcasted_iota(jnp.int32, (1, padded.shape[0]), 1)
    width = padded.shape[0] // 3
    factor = jnp.where(lane < width, HEAD_DIM ** (-0.5) * math.log2(math.e), 1.0)
    ones = jnp.where((lane >= 2 * width) & (lane % LANES == HEAD_DIM), 1.0, 0.0)
    block = at // 2
    for low in range(0, at, block):
        out = lax.dot_general(
            normed[low : low + block, :], padded[...], (((1,), (1,)), ((), ())), preferred_element_type=F32
        )
        out_ref[low : low + block, :] = (out * factor + ones).astype(BF16)


def qkv_rows(modulation, weight, pieces, row_counts, name):
    count = sum(row_counts)
    parts, width = weight.shape[0] // HEAD_DIM, weight.shape[1]
    return call(
        functools.partial(qkv_kernel, row_counts),
        jax.ShapeDtypeStruct((count, parts * LANES), BF16),
        (modulation, weight) + tuple(pieces),
        scratch=[pltpu.VMEM((count, width), BF16), pltpu.VMEM((parts * LANES, width), BF16)],
        flops=2 * count * width * parts * LANES,
        name=name,
    )


def position(order, offset):
    return sum(1 << i for i, bit in enumerate(order) if offset & bit)


def spread(order, index):
    return sum(bit for i, bit in enumerate(order) if index >> i & 1)


def attention_kernel(cap, packed_rows, counts_ref, early_ref, late_ref, near_ref, far_ref, packed, out):
    core, latent, member = place()
    half = cap // 2
    large, small = 2 * half // 3, half // 3
    width = early_ref.shape[1] // 3
    heads = width // LANES
    counts = [counts_ref[latent, member ^ d] for d in range(GROUP)]
    starts = [jnp.int32(0)]
    for d in range(GROUP):
        starts.append(starts[-1] + (counts[d] + ALIGN - 1) // ALIGN * ALIGN)
    total_rows = packed.shape[0]
    spare = total_rows - LEN
    packed[LEN:, :] = jnp.zeros((spare, packed.shape[1]), BF16)
    for d in range(GROUP):
        for k in range(2):
            away = (core != k).astype(jnp.int32)
            for is_small in range(2):
                size = small if is_small else large
                first = k * half + is_small * large
                where = position(SMALL if is_small else LARGE[k], d)
                if where == 0:
                    rows = early_ref[first : first + size, :]
                elif where < 4:
                    base = cap + is_small * 3 * large + (where - 1) * size
                    base = pl.multiple_of(base + away * (3 * half), 32)
                    rows = early_ref[pl.ds(base, size), :]
                else:
                    base = is_small * 4 * large + (where - 4) * size
                    base = pl.multiple_of(base + away * (4 * half), 32)
                    rows = late_ref[pl.ds(base, size), :]
                packed[pl.ds(pl.multiple_of(starts[d] + first, ALIGN), size), :] = rows
    slot = lax.broadcasted_iota(jnp.int32, (1, packed_rows), 1)
    valid = jnp.zeros((1, packed_rows), jnp.bool_)
    for d in range(GROUP):
        valid = valid | ((slot >= starts[d]) & (slot < starts[d] + counts[d]))
    bias = jnp.where(valid, 0.0, -1e30)
    out[LEN:, :] = jnp.zeros((spare, out.shape[1]), F32)
    block = packed_rows // 3
    for low in range(0, packed_rows, block):
        for head in range(heads):
            lanes = head * LANES
            queries = packed[low : low + block, lanes : lanes + LANES]
            keys = packed[:packed_rows, width + lanes : width + lanes + LANES]
            values = packed[:packed_rows, 2 * width + lanes : 2 * width + lanes + LANES]
            scores = lax.dot_general(
                queries, keys, (((1,), (1,)), ((), ())), preferred_element_type=F32
            )
            scores = scores + bias
            peak = jnp.max(scores, axis=-1, keepdims=True)
            probs = jnp.exp2(scores - peak).astype(BF16)
            mixed = jnp.dot(probs, values, preferred_element_type=F32)
            mixed = mixed / mixed[:, HEAD_DIM : HEAD_DIM + 1]
            out[low : low + block, lanes : lanes + LANES] = mixed
    targets = [
        jnp.where(core == 0, starts[spread(HEADS_TO[0], j)], starts[spread(HEADS_TO[1], j)])
        for j in range(GROUP)
    ]
    for pair in range(0, GROUP, 2):
        columns = []
        for head in range(heads):
            rows = [
                out[pl.ds(pl.multiple_of(targets[j], ALIGN), cap), head * LANES : (head + 1) * LANES]
                for j in (pair, pair + 1)
            ]
            columns.append(jnp.concatenate(rows).T[:HEAD_DIM])
        dest = near_ref if pair < GROUP // 2 else far_ref
        at = pair % (GROUP // 2) * cap
        dest[:, at : at + 2 * cap] = jnp.concatenate(columns).astype(BF16)


def attention(piece_rows, early, late, cap):
    packed_rows = LEN + GROUP * ALIGN
    total = -(-(packed_rows + cap) // 32) * 32
    width = early.shape[1] // 3
    heads = width // LANES
    shape = jax.ShapeDtypeStruct((heads * HEAD_DIM, GROUP // 2 * cap), BF16)
    return call(
        functools.partial(attention_kernel, cap, packed_rows),
        (shape, shape),
        (piece_rows, early, late),
        scratch=[pltpu.VMEM((total, 3 * width), BF16), pltpu.VMEM((total, width), F32)],
        specs=[pl.BlockSpec(memory_space=pltpu.SMEM)] + [pl.BlockSpec(memory_space=pltpu.VMEM)] * 2,
        flops=4 * heads * packed_rows * packed_rows * LANES,
        name="attend",
    )


def project_kernel(cap, mod_ref, hidden_ref, mine_ref, mate_ref, *refs):
    proj_refs, plane_refs = refs[:8], refs[8 : 8 + GROUP // 2 - 1]
    mid_ref, mlp_ref, flat, weights = refs[8 + GROUP // 2 - 1 :]
    core, latent, member = place()
    heads = mine_ref.shape[0] // HEAD_DIM

    def put(block, j):
        offset = jnp.where(core == 0, spread(HEADS_TO[0], j), spread(HEADS_TO[1], j))
        for head in range(heads):
            rows = block[head * HEAD_DIM : (head + 1) * HEAD_DIM]
            flat[head * GROUP + offset] = rows

    put(mine_ref[...][:, :cap].astype(F32), 0)
    put(mate_ref[...][:, :cap].astype(F32), GROUP // 2)
    for j, ref in enumerate(plane_refs):
        both = ref[...].astype(F32)
        put(both[:, :cap], j + 1)
        put(both[:, cap:], (j + 1) ^ (GROUP // 2))
    for away in range(2):
        head = core if away == 0 else 1 - core
        at = 0
        for blocks, ref in zip((1, 1, 2, 4), proj_refs[4 * away : 4 * away + 4]):
            block = ref[ref.shape[0] - blocks * HEAD_DIM :, :].astype(F32)
            for row in range(0, block.shape[0], HEAD_DIM):
                offset = jnp.where(head == 0, spread(PROJ[0], at), spread(PROJ[1], at))
                weights[head * GROUP + offset] = block[row : row + HEAD_DIM]
                at += 1
    stacked = flat[...].reshape(heads * GROUP * HEAD_DIM, cap).astype(BF16)
    proj = weights[...].reshape(heads * GROUP * HEAD_DIM, weights.shape[2]).astype(BF16)
    attn_out = lax.dot_general(stacked, proj, (((0,), (0,)), ((), ())), preferred_element_type=F32)
    mid = hidden_ref[...].astype(F32) + mod_row(mod_ref, latent, 2) * attn_out
    mid_ref[...] = mid
    scale, shift = 1.0 + mod_row(mod_ref, latent, 4), mod_row(mod_ref, latent, 3)
    mlp_ref[...] = (normalized(mid) * scale + shift).astype(BF16)


def project(modulation, hidden_in, proj_parts, mine, mate, plane):
    cap, width = hidden_in.shape
    heads = mine.shape[0] // HEAD_DIM
    return call(
        functools.partial(project_kernel, cap),
        (jax.ShapeDtypeStruct((cap, width), F32), jax.ShapeDtypeStruct((cap, width), BF16)),
        (modulation, hidden_in, mine, mate) + tuple(proj_parts) + tuple(plane),
        scratch=[
            pltpu.VMEM((heads * GROUP, HEAD_DIM, cap), F32),
            pltpu.VMEM((heads * GROUP, HEAD_DIM, width), F32),
        ],
        flops=2 * cap * width * width,
        name="project",
    )


def pack_kernel(up_ref, down_ref, *refs):
    far_refs, (up_all, down_all, sems) = refs[:-3], refs[-3:]
    core, _, _ = place()
    hidden, parts = up_ref.shape[0], len(far_refs) // 2
    own = [
        pltpu.make_async_copy(up_ref, up_all.at[pl.ds(0, hidden)], sems.at[2 * parts]),
        pltpu.make_async_copy(down_ref, down_all.at[pl.ds(0, hidden)], sems.at[2 * parts + 1]),
    ]
    for copy in own:
        copy.start()

    def fetch(dests):
        copies = []
        for d, dest in enumerate(dests):
            at = hidden
            for ref in far_refs[parts * d : parts * (d + 1)]:
                rows = ref.shape[0]
                copies.append(
                    pltpu.make_async_copy(ref, dest.at[pl.ds(at, rows)], sems.at[len(copies)])
                )
                at += rows
        for copy in copies:
            copy.start()
        for copy in copies:
            copy.wait()

    pl.when(core == 0)(lambda: fetch((up_all, down_all)))
    pl.when(core == 1)(lambda: fetch((down_all, up_all)))
    for copy in own:
        copy.wait()


def pack(up, down, far):
    hidden, width = up.shape
    both = jax.ShapeDtypeStruct((2 * hidden, width), BF16)
    return call(
        pack_kernel,
        (both, both),
        (up, down) + tuple(far),
        scratch=[pltpu.SemaphoreType.DMA((2 + len(far),))],
        specs=[pl.BlockSpec(memory_space=pl.ANY)] * (2 + len(far)),
        name="pack",
    )


def mlp_kernel(row_count, out_count, up_ref, down_ref, *refs):
    row_refs, out_refs, rows = refs[:row_count], refs[row_count:-1], refs[-1]
    at = 0
    for ref in row_refs:
        rows[at : at + ref.shape[0], :] = ref[...]
        at += ref.shape[0]
    units = lax.dot_general(
        rows[...], up_ref[...], (((1,), (1,)), ((), ())), preferred_element_type=F32
    )
    units = 0.5 * units * (1.0 + jnp.tanh(0.7978845608 * (units + 0.044715 * (units * units * units))))
    partial = jnp.dot(units.astype(BF16), down_ref[...], preferred_element_type=F32)
    at = 0
    for ref in out_refs:
        ref[...] = partial[at : at + ref.shape[0]].astype(ref.dtype)
        at += ref.shape[0]


def mlp_rows(pieces, packed, out_rows, dtype, name):
    count = sum(p.shape[0] for p in pieces)
    hidden, width = packed[0].shape
    outs = tuple(jax.ShapeDtypeStruct((rows, width), dtype) for rows in out_rows)
    return call(
        functools.partial(mlp_kernel, len(pieces), len(outs)),
        outs,
        tuple(packed) + tuple(pieces),
        scratch=[pltpu.VMEM((count, width), BF16)],
        flops=4 * count * width * hidden,
        name=name,
    )


def final_kernel(
    counts_ref, guide_ref, coef_ref, mod_ref, mid_ref, part_ref, noisy_ref, weight_ref,
    first_low, first_high, second_low, second_high, block_ref, pred_ref, base_ref, total,
):
    core, latent, member = place()
    cap = mid_ref.shape[0]
    half = cap // 2
    for low, first, second in ((0, first_low, second_low), (half, first_high, second_high)):
        total[low : low + half, :] = (
            part_ref[low : low + half, :] + first[:half, :].astype(F32) + second[...].astype(F32)
        )
    rows = (mid_ref[...] + mod_row(mod_ref, latent, 5) * total[...]).astype(BF16).astype(F32)
    count = counts_ref[latent, member]
    rows = jnp.where(lax.broadcasted_iota(jnp.int32, (cap, 1), 0) < count, rows, 0.0)
    block_ref[...] = rows.astype(BF16)
    scale, shift = 1.0 + mod_row(mod_ref, latent, 7), mod_row(mod_ref, latent, 6)
    final_in = (normalized(rows) * scale + shift).astype(BF16)
    pred = lax.dot_general(
        weight_ref[...], final_in, (((1,), (1,)), ((), ())), preferred_element_type=F32
    )
    guide = guide_ref[latent]
    valid = lax.broadcasted_iota(jnp.int32, (1, cap), 1) < count
    weighted = (-coef_ref[latent, 1] * jnp.where(core == 0, guide, 1.0 - guide)) * pred
    pred_ref[...] = jnp.where(valid, weighted, 0.0)
    base_ref[...] = jnp.where(valid, coef_ref[latent, 0] * noisy_ref[...], 0.0)


def final(scalars, modulation, mid, part, noisy, weight, firsts, seconds):
    cap, width = mid.shape
    smem, vmem = pl.BlockSpec(memory_space=pltpu.SMEM), pl.BlockSpec(memory_space=pltpu.VMEM)
    flat = jax.ShapeDtypeStruct(noisy.shape, F32)
    return call(
        final_kernel,
        (jax.ShapeDtypeStruct((cap, width), BF16), flat, flat),
        tuple(scalars) + (modulation, mid, part, noisy, weight) + tuple(firsts) + tuple(seconds),
        scratch=[pltpu.VMEM((cap, width), F32)],
        specs=[smem] * 3 + [vmem] * 9,
        flops=2 * cap * width * weight.shape[0],
        name="finish",
    )


def shards(
    hidden_in,
    noisy_latent,
    piece_rows,
    modulation,
    qkv_weight,
    proj_weight,
    up_weight,
    down_weight,
    final_weight,
    guidance,
    solver_coef,
):
    cap, width = hidden_in.shape
    half = cap // 2
    large, small = 2 * half // 3, half // 3
    core, _, _ = place()
    modulation = modulation[0]
    qkv_rows_t, proj_t, up_t, down_t = (
        w[0].T for w in (qkv_weight, proj_weight, up_weight, down_weight)
    )

    own_rows = after(lax.dynamic_slice_in_dim(hidden_in, core * half, half))
    large_rows, small_rows = own_rows[:large], own_rows[large:]
    hidden = up_t.shape[0]
    cuts = [sum(FAR_EARLY[:i]) for i in range(len(FAR_EARLY) + 1)] + [hidden]
    proj_rows = None
    got, away = [], []
    for step in range(3):
        payload = large_rows if step == 0 else jnp.concatenate([large_rows, proj_rows])
        got_large = permute_by(payload, [order[step] for order in LARGE])
        got_small = permute_by(small_rows, [SMALL[step]] * 2)
        if step == 0:
            up_t, down_t, _ = lax.optimization_barrier((up_t, down_t, got_large))
            sent = [
                jnp.where(core == 0, up_t[low:high], down_t[low:high])
                for low, high in zip(cuts[:-1], cuts[1:])
            ]
            proj_own = [
                lax.dynamic_slice_in_dim(proj_t, head * HEAD_DIM, HEAD_DIM) for head in (core, 1 - core)
            ]
            proj_rows = proj_own[0]
        elif step == 1:
            got_large, got_small = lax.optimization_barrier((got_large, got_small))
            proj_rows = jnp.concatenate([proj_rows, got_large[2 * large :]])
        else:
            early = qkv_rows(
                modulation,
                qkv_rows_t,
                (hidden_in, got[0][0], got[1][0], got[0][1], got[1][1])
                + (away[0][0], away[1][0], away[0][1], away[1][1]),
                (cap, large, 2 * large, small, 2 * small) + (large, 2 * large, small, 2 * small),
                "qkv_early",
            )
            got_large, got_small, early, *sent = lax.optimization_barrier(
                (got_large, got_small, early, *sent)
            )
            proj_rows = jnp.concatenate([proj_rows, got_large[4 * large :]])
        if step < 2:
            large_rows = jnp.concatenate([large_rows, got_large[: large << step]])
            small_rows = jnp.concatenate([small_rows, got_small])
        got.append((got_large, got_small))
        away.append((from_other_half(got_large), from_other_half(got_small)))
    proj_last = permute_by(proj_rows, [order[2] for order in PROJ])
    far = [permute_by(sent[0], [GROUP // 2] * 2)]
    late = qkv_rows(
        modulation,
        qkv_rows_t,
        got[2] + away[2],
        (4 * large, 4 * small) * 2,
        "qkv_late",
    )
    far.append(permute_by(after(sent[1], far[0], late), [GROUP // 2] * 2))
    far.append(permute_by(after(sent[2], far[0], late), [GROUP // 2] * 2))
    mine, sent_heads = attention(piece_rows, early, late, cap)
    mate = permute_by(sent_heads, [order[2] for order in HEADS_TO])
    mate, far[1], proj_last = lax.optimization_barrier((mate, far[1], proj_last))
    proj_parts = [proj_own[0], got[1][0], got[2][0], proj_last]
    proj_parts += [proj_own[1], away[1][0], away[2][0], from_other_half(proj_last)]
    plane = []
    for j in range(1, GROUP // 2):
        both = jnp.concatenate([a[:, j * cap : (j + 1) * cap] for a in (mine, mate)], axis=1)
        plane.append(permute_by(both, [spread(order, j) for order in HEADS_TO]))
    far[2], *plane = lax.optimization_barrier((far[2], *plane))
    far.append(permute_by(after(sent[3], *plane), [GROUP // 2] * 2))
    mid, mlp_in = project(modulation, hidden_in, proj_parts, mine, mate, plane)

    side = permute_by(mlp_in, (1, 2))
    both = [
        jnp.concatenate([rows[low : low + half] for rows in (mlp_in, side)]) for low in (0, half)
    ]
    across = [permute_by(rows, (2, 1)) for rows in both]
    far[3] = after(far[3], *both)
    far += [from_other_half(rows) for rows in far]
    packed = pack(up_t, down_t, far)
    sums = [
        mlp_rows((rows,), packed, (cap,), BF16, f"mlp_far{i}")[0] for i, rows in enumerate(across)
    ]
    firsts = [permute_by(rows, (2, 1)) for rows in sums]
    part, *side_parts = mlp_rows(
        (after(mlp_in, *sums), side), packed, (cap, half, half), F32, "mlp_near"
    )
    seconds = [
        permute_by((rows + first[half:].astype(F32)).astype(BF16), (1, 2))
        for rows, first in zip(side_parts, firsts)
    ]
    block_rows, pred, base = final(
        (piece_rows, guidance, solver_coef),
        modulation,
        mid,
        part,
        noisy_latent.T,
        final_weight.T,
        firsts,
        seconds,
    )
    next_latent = base + (pred + from_other_half(pred))
    return (next_latent.T, block_rows[None])


def solution(mesh):
    placed = (
        P("tok", None),
        P("tok", None),
        P(),
        P("cfg", None, None, None),
        P("tok", None, None),
        P("tok", None, None),
        P("tok", None, None),
        P("tok", None, None),
        P(),
        P(),
        P(),
    )
    return jax.shard_map(
        shards,
        mesh=mesh,
        in_specs=placed,
        out_specs=(P("tok", None), P("cfg", "tok", None)),
        check_vma=False,
    )
```

```python
import functools
import math

import jax
import jax.numpy as jnp
from jax import lax
from jax.experimental import pallas as pl
from jax.experimental.pallas import tpu as pltpu
from jax.sharding import PartitionSpec as P

HEAD_DIM = 72
GROUP = 8
LEN = 1024
LANES = 128
ALIGN = 16
LARGE = ((1, 2, 4), (2, 4, 1))
SMALL = (4, 1, 2)
PROJ = ((2, 4, 1), (4, 1, 2))
HEADS_TO = ((2, 4, 1), (4, 1, 2))
FAR_EARLY = (80, 64, 176, 128)
CHUNKS = 3
F32 = jnp.float32
BF16 = jnp.bfloat16


def permute_by(block, offsets):
    count = lax.axis_size("tok")
    route = [
        (half * count + i, half * count + (i ^ offset))
        for half, offset in enumerate(offsets)
        for i in range(count)
    ]
    return lax.ppermute(block, ("cfg", "tok"), route)


def from_other_half(block):
    return lax.ppermute(block, "cfg", [(0, 1), (1, 0)])


def after(value, *earlier):
    return lax.optimization_barrier((value,) + earlier)[0]


def place():
    pos = lax.axis_index("tok")
    return lax.axis_index("cfg"), pos // GROUP, pos % GROUP


def normalized(values):
    center = values - jnp.mean(values, axis=-1, keepdims=True)
    spread = jnp.mean(center * center, axis=-1, keepdims=True)
    return center * lax.rsqrt(spread + 1e-06)


def mod_row(mod_ref, latent, k):
    return mod_ref[latent, k : k + 1, :]


def call(kernel, out_shape, operands, scratch=(), specs=None, flops=0, name=None, vmem=40):
    whole = pl.BlockSpec(memory_space=pltpu.VMEM)
    moved = sum(math.prod(o.shape) * o.dtype.itemsize for o in operands)
    return pl.pallas_call(
        kernel,
        out_shape=out_shape,
        in_specs=specs or [whole] * len(operands),
        out_specs=jax.tree.map(lambda _: whole, out_shape),
        scratch_shapes=list(scratch),
        compiler_params=pltpu.CompilerParams(vmem_limit_bytes=vmem << 20),
        cost_estimate=pl.CostEstimate(flops=flops, bytes_accessed=moved, transcendentals=0),
        name=name,
    )(*operands)


def qkv_kernel(row_counts, mod_ref, weight_ref, *refs):
    row_refs, out_ref, normed, padded = refs[:-3], refs[-3], refs[-2], refs[-1]
    _, latent, _ = place()
    shift, scale = mod_row(mod_ref, latent, 0), 1.0 + mod_row(mod_ref, latent, 1)
    chunk = 32
    at = 0
    for ref, count in zip(row_refs, row_counts):
        for low in range(0, count, chunk):
            rows = ref[low : low + chunk, :].astype(F32)
            normed[at : at + chunk, :] = (normalized(rows) * scale + shift).astype(BF16)
            at += chunk
    weight = weight_ref[...].astype(F32)
    unused = jnp.zeros((LANES - HEAD_DIM, weight.shape[1]), F32)
    for part in range(weight.shape[0] // HEAD_DIM):
        rows = jnp.concatenate([weight[part * HEAD_DIM : (part + 1) * HEAD_DIM], unused])
        padded[part * LANES : (part + 1) * LANES, :] = rows.astype(BF16)
    lane = lax.broadcasted_iota(jnp.int32, (1, padded.shape[0]), 1)
    width = padded.shape[0] // 3
    factor = jnp.where(lane < width, HEAD_DIM ** (-0.5) * math.log2(math.e), 1.0)
    ones = jnp.where((lane >= 2 * width) & (lane % LANES == HEAD_DIM), 1.0, 0.0)
    block = at // 2
    for low in range(0, at, block):
        out = lax.dot_general(
            normed[low : low + block, :], padded[...], (((1,), (1,)), ((), ())), preferred_element_type=F32
        )
        out_ref[low : low + block, :] = (out * factor + ones).astype(BF16)


def qkv_rows(modulation, weight, pieces, row_counts, name):
    count = sum(row_counts)
    parts, width = weight.shape[0] // HEAD_DIM, weight.shape[1]
    return call(
        functools.partial(qkv_kernel, row_counts),
        jax.ShapeDtypeStruct((count, parts * LANES), BF16),
        (modulation, weight) + tuple(pieces),
        scratch=[pltpu.VMEM((count, width), BF16), pltpu.VMEM((parts * LANES, width), BF16)],
        flops=2 * count * width * parts * LANES,
        name=name,
    )


def position(order, offset):
    return sum(1 << i for i, bit in enumerate(order) if offset & bit)


def spread(order, index):
    return sum(bit for i, bit in enumerate(order) if index >> i & 1)


def attention_kernel(cap, packed_rows, counts_ref, early_ref, late_ref, near_ref, far_ref, packed, out):
    core, latent, member = place()
    half = cap // 2
    large, small = 2 * half // 3, half // 3
    width = early_ref.shape[1] // 3
    heads = width // LANES
    counts = [counts_ref[latent, member ^ d] for d in range(GROUP)]
    starts = [jnp.int32(0)]
    for d in range(GROUP):
        starts.append(starts[-1] + (counts[d] + ALIGN - 1) // ALIGN * ALIGN)
    total_rows = packed.shape[0]
    spare = total_rows - LEN
    packed[LEN:, :] = jnp.zeros((spare, packed.shape[1]), BF16)
    for d in range(GROUP):
        for k in range(2):
            away = (core != k).astype(jnp.int32)
            for is_small in range(2):
                size = small if is_small else large
                first = k * half + is_small * large
                where = position(SMALL if is_small else LARGE[k], d)
                if where == 0:
                    rows = early_ref[first : first + size, :]
                elif where < 4:
                    base = cap + is_small * 3 * large + (where - 1) * size
                    base = pl.multiple_of(base + away * (3 * half), 32)
                    rows = early_ref[pl.ds(base, size), :]
                else:
                    base = is_small * 4 * large + (where - 4) * size
                    base = pl.multiple_of(base + away * (4 * half), 32)
                    rows = late_ref[pl.ds(base, size), :]
                packed[pl.ds(pl.multiple_of(starts[d] + first, ALIGN), size), :] = rows
    slot = lax.broadcasted_iota(jnp.int32, (1, packed_rows), 1)
    valid = jnp.zeros((1, packed_rows), jnp.bool_)
    for d in range(GROUP):
        valid = valid | ((slot >= starts[d]) & (slot < starts[d] + counts[d]))
    bias = jnp.where(valid, 0.0, -1e30)
    out[LEN:, :] = jnp.zeros((spare, out.shape[1]), F32)
    block = packed_rows // 3
    for low in range(0, packed_rows, block):
        for head in range(heads):
            lanes = head * LANES
            queries = packed[low : low + block, lanes : lanes + LANES]
            keys = packed[:packed_rows, width + lanes : width + lanes + LANES]
            values = packed[:packed_rows, 2 * width + lanes : 2 * width + lanes + LANES]
            scores = lax.dot_general(
                queries, keys, (((1,), (1,)), ((), ())), preferred_element_type=F32
            )
            scores = scores + bias
            peak = jnp.max(scores, axis=-1, keepdims=True)
            probs = jnp.exp2(scores - peak).astype(BF16)
            mixed = jnp.dot(probs, values, preferred_element_type=F32)
            mixed = mixed / mixed[:, HEAD_DIM : HEAD_DIM + 1]
            out[low : low + block, lanes : lanes + LANES] = mixed
    targets = [
        jnp.where(core == 0, starts[spread(HEADS_TO[0], j)], starts[spread(HEADS_TO[1], j)])
        for j in range(GROUP)
    ]
    for pair in range(0, GROUP, 2):
        columns = []
        for head in range(heads):
            rows = [
                out[pl.ds(pl.multiple_of(targets[j], ALIGN), cap), head * LANES : (head + 1) * LANES]
                for j in (pair, pair + 1)
            ]
            columns.append(jnp.concatenate(rows).T[:HEAD_DIM])
        dest = near_ref if pair < GROUP // 2 else far_ref
        at = pair % (GROUP // 2) * cap
        dest[:, at : at + 2 * cap] = jnp.concatenate(columns).astype(BF16)


def attention(piece_rows, early, late, cap):
    packed_rows = LEN + GROUP * ALIGN
    total = -(-(packed_rows + cap) // 32) * 32
    width = early.shape[1] // 3
    heads = width // LANES
    shape = jax.ShapeDtypeStruct((heads * HEAD_DIM, GROUP // 2 * cap), BF16)
    return call(
        functools.partial(attention_kernel, cap, packed_rows),
        (shape, shape),
        (piece_rows, early, late),
        scratch=[pltpu.VMEM((total, 3 * width), BF16), pltpu.VMEM((total, width), F32)],
        specs=[pl.BlockSpec(memory_space=pltpu.SMEM)] + [pl.BlockSpec(memory_space=pltpu.VMEM)] * 2,
        flops=4 * heads * packed_rows * packed_rows * LANES,
        name="attend",
    )


def project_kernel(cap, mod_ref, hidden_ref, mine_ref, mate_ref, *refs):
    proj_refs, plane_refs = refs[:8], refs[8 : 8 + GROUP // 2 - 1]
    mid_ref, mlp_ref, flat, weights = refs[8 + GROUP // 2 - 1 :]
    core, latent, member = place()
    heads = mine_ref.shape[0] // HEAD_DIM

    def put(block, j):
        offset = jnp.where(core == 0, spread(HEADS_TO[0], j), spread(HEADS_TO[1], j))
        for head in range(heads):
            rows = block[head * HEAD_DIM : (head + 1) * HEAD_DIM]
            flat[head * GROUP + offset] = rows

    put(mine_ref[...][:, :cap].astype(F32), 0)
    put(mate_ref[...][:, :cap].astype(F32), GROUP // 2)
    for j, ref in enumerate(plane_refs):
        both = ref[...].astype(F32)
        put(both[:, :cap], j + 1)
        put(both[:, cap:], (j + 1) ^ (GROUP // 2))
    for away in range(2):
        head = core if away == 0 else 1 - core
        at = 0
        for blocks, ref in zip((1, 1, 2, 4), proj_refs[4 * away : 4 * away + 4]):
            block = ref[ref.shape[0] - blocks * HEAD_DIM :, :].astype(F32)
            for row in range(0, block.shape[0], HEAD_DIM):
                offset = jnp.where(head == 0, spread(PROJ[0], at), spread(PROJ[1], at))
                weights[head * GROUP + offset] = block[row : row + HEAD_DIM]
                at += 1
    stacked = flat[...].reshape(heads * GROUP * HEAD_DIM, cap).astype(BF16)
    proj = weights[...].reshape(heads * GROUP * HEAD_DIM, weights.shape[2]).astype(BF16)
    attn_out = lax.dot_general(stacked, proj, (((0,), (0,)), ((), ())), preferred_element_type=F32)
    mid = hidden_ref[...].astype(F32) + mod_row(mod_ref, latent, 2) * attn_out
    mid_ref[...] = mid
    scale, shift = 1.0 + mod_row(mod_ref, latent, 4), mod_row(mod_ref, latent, 3)
    mlp_ref[...] = (normalized(mid) * scale + shift).astype(BF16)


def project(modulation, hidden_in, proj_parts, mine, mate, plane):
    cap, width = hidden_in.shape
    heads = mine.shape[0] // HEAD_DIM
    return call(
        functools.partial(project_kernel, cap),
        (jax.ShapeDtypeStruct((cap, width), F32), jax.ShapeDtypeStruct((cap, width), BF16)),
        (modulation, hidden_in, mine, mate) + tuple(proj_parts) + tuple(plane),
        scratch=[
            pltpu.VMEM((heads * GROUP, HEAD_DIM, cap), F32),
            pltpu.VMEM((heads * GROUP, HEAD_DIM, width), F32),
        ],
        flops=2 * cap * width * width,
        name="project",
    )


def pack_kernel(row_counts, up_ref, down_ref, *refs):
    far_refs, (up_all, down_all, sems) = refs[:-3], refs[-3:]
    core, _, _ = place()
    hidden, parts = up_ref.shape[0], len(far_refs) // 2
    own = [
        pltpu.make_async_copy(up_ref, up_all.at[pl.ds(0, hidden)], sems.at[2 * parts]),
        pltpu.make_async_copy(down_ref, down_all.at[pl.ds(0, hidden)], sems.at[2 * parts + 1]),
    ]
    for copy in own:
        copy.start()

    def fetch(dests):
        copies = []
        for d, dest in enumerate(dests):
            at = hidden
            for rows, ref in zip(row_counts, far_refs[parts * d : parts * (d + 1)]):
                source = ref.at[pl.ds(ref.shape[0] - rows, rows)]
                copies.append(
                    pltpu.make_async_copy(source, dest.at[pl.ds(at, rows)], sems.at[len(copies)])
                )
                at += rows
        for copy in copies:
            copy.start()
        for copy in copies:
            copy.wait()

    pl.when(core == 0)(lambda: fetch((up_all, down_all)))
    pl.when(core == 1)(lambda: fetch((down_all, up_all)))
    for copy in own:
        copy.wait()


def pack(up, down, far, row_counts):
    hidden, width = up.shape
    both = jax.ShapeDtypeStruct((2 * hidden, width), BF16)
    return call(
        functools.partial(pack_kernel, row_counts),
        (both, both),
        (up, down) + tuple(far),
        scratch=[pltpu.SemaphoreType.DMA((2 + len(far),))],
        specs=[pl.BlockSpec(memory_space=pl.ANY)] * (2 + len(far)),
        name="pack",
    )


def mlp_kernel(row_count, out_count, up_ref, down_ref, *refs):
    row_refs, out_refs, rows = refs[:row_count], refs[row_count:-1], refs[-1]
    at = 0
    for ref in row_refs:
        rows[at : at + ref.shape[0], :] = ref[...]
        at += ref.shape[0]
    units = lax.dot_general(
        rows[...], up_ref[...], (((1,), (1,)), ((), ())), preferred_element_type=F32
    )
    units = 0.5 * units * (1.0 + jnp.tanh(0.7978845608 * (units + 0.044715 * (units * units * units))))
    partial = jnp.dot(units.astype(BF16), down_ref[...], preferred_element_type=F32)
    at = 0
    for ref in out_refs:
        ref[...] = partial[at : at + ref.shape[0]].astype(ref.dtype)
        at += ref.shape[0]


def mlp_rows(pieces, packed, out_rows, dtype, name):
    count = sum(p.shape[0] for p in pieces)
    hidden, width = packed[0].shape
    outs = tuple(jax.ShapeDtypeStruct((rows, width), dtype) for rows in out_rows)
    return call(
        functools.partial(mlp_kernel, len(pieces), len(outs)),
        outs,
        tuple(packed) + tuple(pieces),
        scratch=[pltpu.VMEM((count, width), BF16)],
        flops=4 * count * width * hidden,
        name=name,
    )


def final_kernel(
    counts_ref, guide_ref, coef_ref, mod_ref, mid_ref, part_ref, noisy_ref, weight_ref,
    *refs,
):
    core, latent, member = place()
    cap = mid_ref.shape[0]
    sum_refs, (block_ref, pred_ref, base_ref, total) = refs[:-4], refs[-4:]
    chunk = cap // CHUNKS
    for i, (first, second) in enumerate(zip(sum_refs[:CHUNKS], sum_refs[CHUNKS:])):
        rows = slice(i * chunk, (i + 1) * chunk)
        total[rows, :] = part_ref[rows, :] + first[:chunk, :].astype(F32) + second[...].astype(F32)
    rows = (mid_ref[...] + mod_row(mod_ref, latent, 5) * total[...]).astype(BF16).astype(F32)
    count = counts_ref[latent, member]
    rows = jnp.where(lax.broadcasted_iota(jnp.int32, (cap, 1), 0) < count, rows, 0.0)
    block_ref[...] = rows.astype(BF16)
    scale, shift = 1.0 + mod_row(mod_ref, latent, 7), mod_row(mod_ref, latent, 6)
    final_in = (normalized(rows) * scale + shift).astype(BF16)
    pred = lax.dot_general(
        weight_ref[...], final_in, (((1,), (1,)), ((), ())), preferred_element_type=F32
    )
    guide = guide_ref[latent]
    valid = lax.broadcasted_iota(jnp.int32, (1, cap), 1) < count
    weighted = (-coef_ref[latent, 1] * jnp.where(core == 0, guide, 1.0 - guide)) * pred
    pred_ref[...] = jnp.where(valid, weighted, 0.0)
    base_ref[...] = jnp.where(valid, coef_ref[latent, 0] * noisy_ref[...], 0.0)


def final(scalars, modulation, mid, part, noisy, weight, firsts, seconds):
    cap, width = mid.shape
    smem, vmem = pl.BlockSpec(memory_space=pltpu.SMEM), pl.BlockSpec(memory_space=pltpu.VMEM)
    flat = jax.ShapeDtypeStruct(noisy.shape, F32)
    return call(
        final_kernel,
        (jax.ShapeDtypeStruct((cap, width), BF16), flat, flat),
        tuple(scalars) + (modulation, mid, part, noisy, weight) + tuple(firsts) + tuple(seconds),
        scratch=[pltpu.VMEM((cap, width), F32)],
        specs=[smem] * 3 + [vmem] * (5 + 2 * CHUNKS),
        flops=2 * cap * width * weight.shape[0],
        name="finish",
    )


def shards(
    hidden_in,
    noisy_latent,
    piece_rows,
    modulation,
    qkv_weight,
    proj_weight,
    up_weight,
    down_weight,
    final_weight,
    guidance,
    solver_coef,
):
    cap, width = hidden_in.shape
    half = cap // 2
    large, small = 2 * half // 3, half // 3
    core, _, _ = place()
    modulation = modulation[0]
    qkv_rows_t, proj_t, up_t, down_t = (
        w[0].T for w in (qkv_weight, proj_weight, up_weight, down_weight)
    )

    own_rows = after(lax.dynamic_slice_in_dim(hidden_in, core * half, half))
    large_rows, small_rows = own_rows[:large], own_rows[large:]
    hidden = up_t.shape[0]
    cuts = [sum(FAR_EARLY[:i]) for i in range(len(FAR_EARLY) + 1)] + [hidden]
    sent = [jnp.where(core == 0, up_t[: cuts[1]], down_t[: cuts[1]])]
    proj_rows = None
    got, away = [], []
    for step in range(3):
        payload = large_rows if step == 0 else jnp.concatenate([large_rows, proj_rows])
        got_large = permute_by(payload, [order[step] for order in LARGE])
        small_payload = jnp.concatenate([small_rows, sent[0]]) if step == 0 else small_rows
        got_small = permute_by(small_payload, [SMALL[step]] * 2)
        if step == 0:
            up_t, down_t, _ = lax.optimization_barrier((up_t, down_t, got_large))
            sent = [
                jnp.where(core == 0, up_t[low:high], down_t[low:high])
                for low, high in zip(cuts[1:-1], cuts[2:])
            ]
            proj_own = [
                lax.dynamic_slice_in_dim(proj_t, head * HEAD_DIM, HEAD_DIM) for head in (core, 1 - core)
            ]
            proj_rows = proj_own[0]
        elif step == 1:
            got_large, got_small = lax.optimization_barrier((got_large, got_small))
            proj_rows = jnp.concatenate([proj_rows, got_large[2 * large :]])
        else:
            early = qkv_rows(
                modulation,
                qkv_rows_t,
                (hidden_in, got[0][0], got[1][0], got[0][1], got[1][1])
                + (away[0][0], away[1][0], away[0][1], away[1][1]),
                (cap, large, 2 * large, small, 2 * small) + (large, 2 * large, small, 2 * small),
                "qkv_early",
            )
            got_large, got_small, early, *sent = lax.optimization_barrier(
                (got_large, got_small, early, *sent)
            )
            proj_rows = jnp.concatenate([proj_rows, got_large[4 * large :]])
        if step < 2:
            large_rows = jnp.concatenate([large_rows, got_large[: large << step]])
            small_rows = jnp.concatenate([small_rows, got_small[: small << step]])
        got.append((got_large, got_small))
        away.append((from_other_half(got_large), from_other_half(got_small)))
    proj_last = permute_by(proj_rows, [order[2] for order in PROJ])
    far = [got[0][1], permute_by(sent[0], [GROUP // 2] * 2)]
    late = qkv_rows(
        modulation,
        qkv_rows_t,
        got[2] + away[2],
        (4 * large, 4 * small) * 2,
        "qkv_late",
    )
    far.append(permute_by(after(sent[1], far[1], late), [GROUP // 2] * 2))
    far.append(permute_by(after(sent[2], far[1], late), [GROUP // 2] * 2))
    mine, sent_heads = attention(piece_rows, early, late, cap)
    mate = permute_by(sent_heads, [order[2] for order in HEADS_TO])
    mate, far[2], proj_last = lax.optimization_barrier((mate, far[2], proj_last))
    proj_parts = [proj_own[0], got[1][0], got[2][0], proj_last]
    proj_parts += [proj_own[1], away[1][0], away[2][0], from_other_half(proj_last)]
    plane = []
    for j in range(1, GROUP // 2):
        both = jnp.concatenate([a[:, j * cap : (j + 1) * cap] for a in (mine, mate)], axis=1)
        plane.append(permute_by(both, [spread(order, j) for order in HEADS_TO]))
    far[3], *plane = lax.optimization_barrier((far[3], *plane))
    far.append(permute_by(after(sent[3], *plane), [GROUP // 2] * 2))
    mid, mlp_in = project(modulation, hidden_in, proj_parts, mine, mate, plane)

    side = permute_by(mlp_in, (1, 2))
    chunk = cap // CHUNKS
    both = [
        jnp.concatenate([rows[low : low + chunk] for rows in (mlp_in, side)])
        for low in range(0, cap, chunk)
    ]
    across = [permute_by(rows, (2, 1)) for rows in both]
    far[4] = after(far[4], *both)
    far += [away[0][1]] + [from_other_half(rows) for rows in far[1:]]
    packed = pack(up_t, down_t, far, [high - low for low, high in zip(cuts[:-1], cuts[1:])])
    sums = [
        mlp_rows((rows,), packed, (2 * chunk,), BF16, f"mlp_far{i}")[0] for i, rows in enumerate(across)
    ]
    firsts = [permute_by(rows, (2, 1)) for rows in sums]
    part, *side_parts = mlp_rows(
        (after(mlp_in, *sums), side), packed, (cap,) + (chunk,) * CHUNKS, F32, "mlp_near"
    )
    seconds = [
        permute_by((rows + first[chunk:].astype(F32)).astype(BF16), (1, 2))
        for rows, first in zip(side_parts, firsts)
    ]
    block_rows, pred, base = final(
        (piece_rows, guidance, solver_coef),
        modulation,
        mid,
        part,
        noisy_latent.T,
        final_weight.T,
        firsts,
        seconds,
    )
    next_latent = base + (pred + from_other_half(pred))
    return (next_latent.T, block_rows[None])


def solution(mesh):
    placed = (
        P("tok", None),
        P("tok", None),
        P(),
        P("cfg", None, None, None),
        P("tok", None, None),
        P("tok", None, None),
        P("tok", None, None),
        P("tok", None, None),
        P(),
        P(),
        P(),
    )
    return jax.shard_map(
        shards,
        mesh=mesh,
        in_specs=placed,
        out_specs=(P("tok", None), P("cfg", "tok", None)),
        check_vma=False,
    )
```

```python
import functools
import math

import jax
import jax.numpy as jnp
from jax import lax
from jax.experimental import pallas as pl
from jax.experimental.pallas import tpu as pltpu
from jax.sharding import PartitionSpec as P

HEAD_DIM = 72
GROUP = 8
LEN = 1024
LANES = 128
ALIGN = 16
LARGE = ((1, 2, 4), (2, 4, 1))
SMALL = (4, 1, 2)
PROJ = ((2, 4, 1), (4, 1, 2))
HEADS_TO = ((2, 4, 1), (4, 1, 2))
FAR_EARLY = 416
CHUNKS = 3
F32 = jnp.float32
BF16 = jnp.bfloat16


def permute_by(block, offsets):
    count = lax.axis_size("tok")
    route = [
        (half * count + i, half * count + (i ^ offset))
        for half, offset in enumerate(offsets)
        for i in range(count)
    ]
    return lax.ppermute(block, ("cfg", "tok"), route)


def from_other_half(block):
    return lax.ppermute(block, "cfg", [(0, 1), (1, 0)])


def after(value, *earlier):
    return lax.optimization_barrier((value,) + earlier)[0]


def place():
    pos = lax.axis_index("tok")
    return lax.axis_index("cfg"), pos // GROUP, pos % GROUP


def normalized(values):
    center = values - jnp.mean(values, axis=-1, keepdims=True)
    spread = jnp.mean(center * center, axis=-1, keepdims=True)
    return center * lax.rsqrt(spread + 1e-06)


def mod_row(mod_ref, latent, k):
    return mod_ref[latent, k : k + 1, :]


def call(kernel, out_shape, operands, scratch=(), specs=None, flops=0, name=None, vmem=40):
    whole = pl.BlockSpec(memory_space=pltpu.VMEM)
    moved = sum(math.prod(o.shape) * o.dtype.itemsize for o in operands)
    return pl.pallas_call(
        kernel,
        out_shape=out_shape,
        in_specs=specs or [whole] * len(operands),
        out_specs=jax.tree.map(lambda _: whole, out_shape),
        scratch_shapes=list(scratch),
        compiler_params=pltpu.CompilerParams(vmem_limit_bytes=vmem << 20),
        cost_estimate=pl.CostEstimate(flops=flops, bytes_accessed=moved, transcendentals=0),
        name=name,
    )(*operands)


def qkv_kernel(row_counts, mod_ref, weight_ref, *refs):
    row_refs, out_ref, normed, padded = refs[:-3], refs[-3], refs[-2], refs[-1]
    _, latent, _ = place()
    shift, scale = mod_row(mod_ref, latent, 0), 1.0 + mod_row(mod_ref, latent, 1)
    chunk = 32
    at = 0
    for ref, count in zip(row_refs, row_counts):
        for low in range(0, count, chunk):
            rows = ref[low : low + chunk, :].astype(F32)
            normed[at : at + chunk, :] = (normalized(rows) * scale + shift).astype(BF16)
            at += chunk
    weight = weight_ref[...].astype(F32)
    unused = jnp.zeros((LANES - HEAD_DIM, weight.shape[1]), F32)
    for part in range(weight.shape[0] // HEAD_DIM):
        rows = jnp.concatenate([weight[part * HEAD_DIM : (part + 1) * HEAD_DIM], unused])
        padded[part * LANES : (part + 1) * LANES, :] = rows.astype(BF16)
    lane = lax.broadcasted_iota(jnp.int32, (1, padded.shape[0]), 1)
    width = padded.shape[0] // 3
    factor = jnp.where(lane < width, HEAD_DIM ** (-0.5) * math.log2(math.e), 1.0)
    ones = jnp.where((lane >= 2 * width) & (lane % LANES == HEAD_DIM), 1.0, 0.0)
    block = at // 2
    for low in range(0, at, block):
        out = lax.dot_general(
            normed[low : low + block, :], padded[...], (((1,), (1,)), ((), ())), preferred_element_type=F32
        )
        out_ref[low : low + block, :] = (out * factor + ones).astype(BF16)


def qkv_rows(modulation, weight, pieces, row_counts, name):
    count = sum(row_counts)
    parts, width = weight.shape[0] // HEAD_DIM, weight.shape[1]
    return call(
        functools.partial(qkv_kernel, row_counts),
        jax.ShapeDtypeStruct((count, parts * LANES), BF16),
        (modulation, weight) + tuple(pieces),
        scratch=[pltpu.VMEM((count, width), BF16), pltpu.VMEM((parts * LANES, width), BF16)],
        flops=2 * count * width * parts * LANES,
        name=name,
    )


def position(order, offset):
    return sum(1 << i for i, bit in enumerate(order) if offset & bit)


def spread(order, index):
    return sum(bit for i, bit in enumerate(order) if index >> i & 1)


def attention_kernel(cap, packed_rows, counts_ref, early_ref, *refs):
    late_refs, (near_ref, far_ref, packed, out) = refs[:2], refs[2:]
    core, latent, member = place()
    half = cap // 2
    large, small = 2 * half // 3, half // 3
    width = early_ref.shape[1] // 3
    heads = width // LANES
    counts = [counts_ref[latent, member ^ d] for d in range(GROUP)]
    starts = [jnp.int32(0)]
    for d in range(GROUP):
        starts.append(starts[-1] + (counts[d] + ALIGN - 1) // ALIGN * ALIGN)
    total_rows = packed.shape[0]
    spare = total_rows - LEN
    packed[LEN:, :] = jnp.zeros((spare, packed.shape[1]), BF16)
    def lay(own_core):
        for d in range(GROUP):
            for k in range(2):
                away = own_core != k
                for is_small in range(2):
                    size = small if is_small else large
                    first = k * half + is_small * large
                    where = position(SMALL if is_small else LARGE[k], d)
                    source = early_ref
                    if where == 0:
                        base = first
                    elif where < 4:
                        base = cap + is_small * 3 * large + (where - 1) * size + away * 3 * half
                    else:
                        source = late_refs[away]
                        base = is_small * 4 * large + (where - 4) * size
                    packed[pl.ds(pl.multiple_of(starts[d] + first, ALIGN), size), :] = source[
                        base : base + size, :
                    ]

    pl.when(core == 0)(lambda: lay(0))
    pl.when(core == 1)(lambda: lay(1))
    slot = lax.broadcasted_iota(jnp.int32, (1, packed_rows), 1)
    valid = jnp.zeros((1, packed_rows), jnp.bool_)
    for d in range(GROUP):
        valid = valid | ((slot >= starts[d]) & (slot < starts[d] + counts[d]))
    bias = jnp.where(valid, 0.0, -1e30)
    out[LEN:, :] = jnp.zeros((spare, out.shape[1]), F32)
    block = packed_rows // 3
    for low in range(0, packed_rows, block):
        for head in range(heads):
            lanes = head * LANES
            queries = packed[low : low + block, lanes : lanes + LANES]
            keys = packed[:packed_rows, width + lanes : width + lanes + LANES]
            values = packed[:packed_rows, 2 * width + lanes : 2 * width + lanes + LANES]
            scores = lax.dot_general(
                queries, keys, (((1,), (1,)), ((), ())), preferred_element_type=F32
            )
            scores = scores + bias
            peak = jnp.max(scores, axis=-1, keepdims=True)
            probs = jnp.exp2(scores - peak).astype(BF16)
            mixed = jnp.dot(probs, values, preferred_element_type=F32)
            mixed = mixed / mixed[:, HEAD_DIM : HEAD_DIM + 1]
            out[low : low + block, lanes : lanes + LANES] = mixed
    targets = [
        jnp.where(core == 0, starts[spread(HEADS_TO[0], j)], starts[spread(HEADS_TO[1], j)])
        for j in range(GROUP)
    ]
    for pair in range(0, GROUP, 2):
        columns = []
        for head in range(heads):
            rows = [
                out[pl.ds(pl.multiple_of(targets[j], ALIGN), cap), head * LANES : (head + 1) * LANES]
                for j in (pair, pair + 1)
            ]
            columns.append(jnp.concatenate(rows).T[:HEAD_DIM])
        dest = near_ref if pair < GROUP // 2 else far_ref
        at = pair % (GROUP // 2) * cap
        dest[:, at : at + 2 * cap] = jnp.concatenate(columns).astype(BF16)


def attention(piece_rows, early, late, cap):
    packed_rows = LEN + GROUP * ALIGN
    total = -(-(packed_rows + cap) // 32) * 32
    width = early.shape[1] // 3
    heads = width // LANES
    shape = jax.ShapeDtypeStruct((heads * HEAD_DIM, GROUP // 2 * cap), BF16)
    return call(
        functools.partial(attention_kernel, cap, packed_rows),
        (shape, shape),
        (piece_rows, early) + tuple(late),
        scratch=[pltpu.VMEM((total, 3 * width), BF16), pltpu.VMEM((total, width), F32)],
        specs=[pl.BlockSpec(memory_space=pltpu.SMEM)] + [pl.BlockSpec(memory_space=pltpu.VMEM)] * 3,
        flops=4 * heads * packed_rows * packed_rows * LANES,
        name="attend",
    )


def project_kernel(cap, mod_ref, hidden_ref, mine_ref, mate_ref, *refs):
    proj_refs, plane_refs = refs[:8], refs[8 : 8 + GROUP // 2 - 1]
    mid_ref, mlp_ref, flat, weights = refs[8 + GROUP // 2 - 1 :]
    core, latent, member = place()
    heads = mine_ref.shape[0] // HEAD_DIM

    def put(block, j):
        offset = jnp.where(core == 0, spread(HEADS_TO[0], j), spread(HEADS_TO[1], j))
        for head in range(heads):
            rows = block[head * HEAD_DIM : (head + 1) * HEAD_DIM]
            flat[head * GROUP + offset] = rows

    put(mine_ref[...][:, :cap].astype(F32), 0)
    put(mate_ref[...][:, :cap].astype(F32), GROUP // 2)
    for j, ref in enumerate(plane_refs):
        both = ref[...].astype(F32)
        put(both[:, :cap], j + 1)
        put(both[:, cap:], (j + 1) ^ (GROUP // 2))
    for away in range(2):
        head = core if away == 0 else 1 - core
        at = 0
        for blocks, ref in zip((1, 1, 2, 4), proj_refs[4 * away : 4 * away + 4]):
            block = ref[ref.shape[0] - blocks * HEAD_DIM :, :].astype(F32)
            for row in range(0, block.shape[0], HEAD_DIM):
                offset = jnp.where(head == 0, spread(PROJ[0], at), spread(PROJ[1], at))
                weights[head * GROUP + offset] = block[row : row + HEAD_DIM]
                at += 1
    stacked = flat[...].reshape(heads * GROUP * HEAD_DIM, cap).astype(BF16)
    proj = weights[...].reshape(heads * GROUP * HEAD_DIM, weights.shape[2]).astype(BF16)
    attn_out = lax.dot_general(stacked, proj, (((0,), (0,)), ((), ())), preferred_element_type=F32)
    mid = hidden_ref[...].astype(F32) + mod_row(mod_ref, latent, 2) * attn_out
    mid_ref[...] = mid
    scale, shift = 1.0 + mod_row(mod_ref, latent, 4), mod_row(mod_ref, latent, 3)
    mlp_ref[...] = (normalized(mid) * scale + shift).astype(BF16)


def project(modulation, hidden_in, proj_parts, mine, mate, plane):
    cap, width = hidden_in.shape
    heads = mine.shape[0] // HEAD_DIM
    return call(
        functools.partial(project_kernel, cap),
        (jax.ShapeDtypeStruct((cap, width), F32), jax.ShapeDtypeStruct((cap, width), BF16)),
        (modulation, hidden_in, mine, mate) + tuple(proj_parts) + tuple(plane),
        scratch=[
            pltpu.VMEM((heads * GROUP, HEAD_DIM, cap), F32),
            pltpu.VMEM((heads * GROUP, HEAD_DIM, width), F32),
        ],
        flops=2 * cap * width * width,
        name="project",
    )


def pack_kernel(row_counts, up_ref, down_ref, *refs):
    far_refs, (up_all, down_all, sems) = refs[:-3], refs[-3:]
    core, _, _ = place()
    hidden, parts = up_ref.shape[0], len(far_refs) // 2
    own = [
        pltpu.make_async_copy(up_ref, up_all.at[pl.ds(0, hidden)], sems.at[2 * parts]),
        pltpu.make_async_copy(down_ref, down_all.at[pl.ds(0, hidden)], sems.at[2 * parts + 1]),
    ]
    for copy in own:
        copy.start()

    def fetch(dests):
        copies = []
        for d, dest in enumerate(dests):
            at = hidden
            for rows, ref in zip(row_counts, far_refs[parts * d : parts * (d + 1)]):
                source = ref.at[pl.ds(ref.shape[0] - rows, rows)]
                copies.append(
                    pltpu.make_async_copy(source, dest.at[pl.ds(at, rows)], sems.at[len(copies)])
                )
                at += rows
        for copy in copies:
            copy.start()
        for copy in copies:
            copy.wait()

    pl.when(core == 0)(lambda: fetch((up_all, down_all)))
    pl.when(core == 1)(lambda: fetch((down_all, up_all)))
    for copy in own:
        copy.wait()


def pack(up, down, far, row_counts):
    hidden, width = up.shape
    both = jax.ShapeDtypeStruct((2 * hidden, width), BF16)
    return call(
        functools.partial(pack_kernel, row_counts),
        (both, both),
        (up, down) + tuple(far),
        scratch=[pltpu.SemaphoreType.DMA((2 + len(far),))],
        specs=[pl.BlockSpec(memory_space=pl.ANY)] * (2 + len(far)),
        name="pack",
    )


def mlp_kernel(row_count, out_count, up_ref, down_ref, *refs):
    row_refs, out_refs, rows = refs[:row_count], refs[row_count:-1], refs[-1]
    at = 0
    for ref in row_refs:
        rows[at : at + ref.shape[0], :] = ref[...]
        at += ref.shape[0]
    units = lax.dot_general(
        rows[...], up_ref[...], (((1,), (1,)), ((), ())), preferred_element_type=F32
    )
    units = 0.5 * units * (1.0 + jnp.tanh(0.7978845608 * (units + 0.044715 * (units * units * units))))
    partial = jnp.dot(units.astype(BF16), down_ref[...], preferred_element_type=F32)
    at = 0
    for ref in out_refs:
        ref[...] = partial[at : at + ref.shape[0]].astype(ref.dtype)
        at += ref.shape[0]


def mlp_rows(pieces, packed, out_rows, dtype, name):
    count = sum(p.shape[0] for p in pieces)
    hidden, width = packed[0].shape
    outs = tuple(jax.ShapeDtypeStruct((rows, width), dtype) for rows in out_rows)
    return call(
        functools.partial(mlp_kernel, len(pieces), len(outs)),
        outs,
        tuple(packed) + tuple(pieces),
        scratch=[pltpu.VMEM((count, width), BF16)],
        flops=4 * count * width * hidden,
        name=name,
    )


def final_kernel(
    counts_ref, guide_ref, coef_ref, mod_ref, mid_ref, part_ref, noisy_ref, weight_ref,
    *refs,
):
    core, latent, member = place()
    cap = mid_ref.shape[0]
    sum_refs, (block_ref, pred_ref, base_ref, total) = refs[:-4], refs[-4:]
    chunk = cap // CHUNKS
    for i, (first, second) in enumerate(zip(sum_refs[:CHUNKS], sum_refs[CHUNKS:])):
        rows = slice(i * chunk, (i + 1) * chunk)
        total[rows, :] = part_ref[rows, :] + first[:chunk, :].astype(F32) + second[...].astype(F32)
    rows = (mid_ref[...] + mod_row(mod_ref, latent, 5) * total[...]).astype(BF16).astype(F32)
    count = counts_ref[latent, member]
    rows = jnp.where(lax.broadcasted_iota(jnp.int32, (cap, 1), 0) < count, rows, 0.0)
    block_ref[...] = rows.astype(BF16)
    scale, shift = 1.0 + mod_row(mod_ref, latent, 7), mod_row(mod_ref, latent, 6)
    final_in = (normalized(rows) * scale + shift).astype(BF16)
    pred = lax.dot_general(
        weight_ref[...], final_in, (((1,), (1,)), ((), ())), preferred_element_type=F32
    )
    guide = guide_ref[latent]
    valid = lax.broadcasted_iota(jnp.int32, (1, cap), 1) < count
    weighted = (-coef_ref[latent, 1] * jnp.where(core == 0, guide, 1.0 - guide)) * pred
    pred_ref[...] = jnp.where(valid, weighted, 0.0)
    base_ref[...] = jnp.where(valid, coef_ref[latent, 0] * noisy_ref[...], 0.0)


def final(scalars, modulation, mid, part, noisy, weight, firsts, seconds):
    cap, width = mid.shape
    smem, vmem = pl.BlockSpec(memory_space=pltpu.SMEM), pl.BlockSpec(memory_space=pltpu.VMEM)
    flat = jax.ShapeDtypeStruct(noisy.shape, F32)
    return call(
        final_kernel,
        (jax.ShapeDtypeStruct((cap, width), BF16), flat, flat),
        tuple(scalars) + (modulation, mid, part, noisy, weight) + tuple(firsts) + tuple(seconds),
        scratch=[pltpu.VMEM((cap, width), F32)],
        specs=[smem] * 3 + [vmem] * (5 + 2 * CHUNKS),
        flops=2 * cap * width * weight.shape[0],
        name="finish",
    )


def shards(
    hidden_in,
    noisy_latent,
    piece_rows,
    modulation,
    qkv_weight,
    proj_weight,
    up_weight,
    down_weight,
    final_weight,
    guidance,
    solver_coef,
):
    cap, width = hidden_in.shape
    half = cap // 2
    large, small = 2 * half // 3, half // 3
    core, _, _ = place()
    modulation = modulation[0]
    qkv_rows_t, proj_t, up_t, down_t = (
        w[0].T for w in (qkv_weight, proj_weight, up_weight, down_weight)
    )

    own_rows = after(lax.dynamic_slice_in_dim(hidden_in, core * half, half))
    large_rows, small_rows = own_rows[:large], own_rows[large:]
    hidden = up_t.shape[0]
    cuts = (0, FAR_EARLY, hidden)
    proj_rows = None
    got, away = [], []
    for step in range(3):
        payload = large_rows if step == 0 else jnp.concatenate([large_rows, proj_rows])
        got_large = permute_by(payload, [order[step] for order in LARGE])
        got_small = permute_by(small_rows, [SMALL[step]] * 2)
        if step == 0:
            up_t, down_t, _ = lax.optimization_barrier((up_t, down_t, got_large))
            sent = [
                jnp.where(core == 0, up_t[low:high], down_t[low:high])
                for low, high in zip(cuts[:-1], cuts[1:])
            ]
            proj_own = [
                lax.dynamic_slice_in_dim(proj_t, head * HEAD_DIM, HEAD_DIM) for head in (core, 1 - core)
            ]
            proj_rows = proj_own[0]
        elif step == 1:
            got_large, got_small = lax.optimization_barrier((got_large, got_small))
            proj_rows = jnp.concatenate([proj_rows, got_large[2 * large :]])
        else:
            early = qkv_rows(
                modulation,
                qkv_rows_t,
                (hidden_in, got[0][0], got[1][0], got[0][1], got[1][1])
                + (away[0][0], away[1][0], away[0][1], away[1][1]),
                (cap, large, 2 * large, small, 2 * small) + (large, 2 * large, small, 2 * small),
                "qkv_early",
            )
            got_large, got_small, early, *sent = lax.optimization_barrier(
                (got_large, got_small, early, *sent)
            )
            proj_rows = jnp.concatenate([proj_rows, got_large[4 * large :]])
        if step < 2:
            large_rows = jnp.concatenate([large_rows, got_large[: large << step]])
            small_rows = jnp.concatenate([small_rows, got_small])
        got.append((got_large, got_small))
        away.append((from_other_half(got_large), from_other_half(got_small)))
    proj_last = permute_by(proj_rows, [order[2] for order in PROJ])
    far = [permute_by(sent[0], [GROUP // 2] * 2)]
    late = [qkv_rows(modulation, qkv_rows_t, got[2], (4 * large, 4 * small), "qkv_late_own")]
    *other, late[0] = lax.optimization_barrier((*away[2], late[0]))
    late.append(qkv_rows(modulation, qkv_rows_t, other, (4 * large, 4 * small), "qkv_late_other"))
    mine, sent_heads = attention(piece_rows, early, late, cap)
    mate = permute_by(sent_heads, [order[2] for order in HEADS_TO])
    mate, proj_last = lax.optimization_barrier((mate, proj_last))
    proj_parts = [proj_own[0], got[1][0], got[2][0], proj_last]
    proj_parts += [proj_own[1], away[1][0], away[2][0], from_other_half(proj_last)]
    plane = []
    for j in range(1, GROUP // 2):
        both = jnp.concatenate([a[:, j * cap : (j + 1) * cap] for a in (mine, mate)], axis=1)
        plane.append(permute_by(both, [spread(order, j) for order in HEADS_TO]))
    far[0], *plane = lax.optimization_barrier((far[0], *plane))
    far.append(permute_by(after(sent[1], *plane), [GROUP // 2] * 2))
    mid, mlp_in = project(modulation, hidden_in, proj_parts, mine, mate, plane)

    chunk = cap // CHUNKS
    side = permute_by(mlp_in, (1, 2))
    both = [
        jnp.concatenate([rows[low : low + chunk] for rows in (mlp_in, side)])
        for low in range(0, cap, chunk)
    ]
    across = [permute_by(rows, (2, 1)) for rows in both]
    far[1] = after(far[1], *both)
    far += [from_other_half(rows) for rows in far]
    packed = pack(up_t, down_t, far, [high - low for low, high in zip(cuts[:-1], cuts[1:])])
    sums = [
        mlp_rows((rows,), packed, (2 * chunk,), BF16, f"mlp_far{i}")[0] for i, rows in enumerate(across)
    ]
    firsts = [permute_by(rows, (2, 1)) for rows in sums]
    part, *side_parts = mlp_rows(
        (after(mlp_in, *sums), side), packed, (cap,) + (chunk,) * CHUNKS, F32, "mlp_near"
    )
    seconds = [
        permute_by((rows + first[chunk:].astype(F32)).astype(BF16), (1, 2))
        for rows, first in zip(side_parts, firsts)
    ]
    block_rows, pred, base = final(
        (piece_rows, guidance, solver_coef),
        modulation,
        mid,
        part,
        noisy_latent.T,
        final_weight.T,
        firsts,
        seconds,
    )
    next_latent = base + (pred + from_other_half(pred))
    return (next_latent.T, block_rows[None])


def solution(mesh):
    placed = (
        P("tok", None),
        P("tok", None),
        P(),
        P("cfg", None, None, None),
        P("tok", None, None),
        P("tok", None, None),
        P("tok", None, None),
        P("tok", None, None),
        P(),
        P(),
        P(),
    )
    return jax.shard_map(
        shards,
        mesh=mesh,
        in_specs=placed,
        out_specs=(P("tok", None), P("cfg", "tok", None)),
        check_vma=False,
    )
```

```python
import functools
import math

import jax
import jax.numpy as jnp
from jax import lax
from jax.experimental import pallas as pl
from jax.experimental.pallas import tpu as pltpu
from jax.sharding import PartitionSpec as P

HEAD_DIM = 72
GROUP = 8
LEN = 1024
LANES = 128
ALIGN = 16
LARGE = ((1, 2, 4), (2, 4, 1))
SMALL = (4, 1, 2)
PROJ = ((2, 4, 1), (4, 1, 2))
HEADS_TO = ((2, 4, 1), (4, 1, 2))
FAR_EARLY = 384
CHUNKS = 3
F32 = jnp.float32
BF16 = jnp.bfloat16


def permute_by(block, offsets):
    count = lax.axis_size("tok")
    route = [
        (half * count + i, half * count + (i ^ offset))
        for half, offset in enumerate(offsets)
        for i in range(count)
    ]
    return lax.ppermute(block, ("cfg", "tok"), route)


def from_other_half(block):
    return lax.ppermute(block, "cfg", [(0, 1), (1, 0)])


def after(value, *earlier):
    return lax.optimization_barrier((value,) + earlier)[0]


def place():
    pos = lax.axis_index("tok")
    return lax.axis_index("cfg"), pos // GROUP, pos % GROUP


def normalized(values):
    center = values - jnp.mean(values, axis=-1, keepdims=True)
    spread = jnp.mean(center * center, axis=-1, keepdims=True)
    return center * lax.rsqrt(spread + 1e-06)


def mod_row(mod_ref, latent, k):
    return mod_ref[latent, k : k + 1, :]


def call(kernel, out_shape, operands, scratch=(), specs=None, flops=0, name=None, vmem=40):
    whole = pl.BlockSpec(memory_space=pltpu.VMEM)
    moved = sum(math.prod(o.shape) * o.dtype.itemsize for o in operands)
    return pl.pallas_call(
        kernel,
        out_shape=out_shape,
        in_specs=specs or [whole] * len(operands),
        out_specs=jax.tree.map(lambda _: whole, out_shape),
        scratch_shapes=list(scratch),
        compiler_params=pltpu.CompilerParams(vmem_limit_bytes=vmem << 20),
        cost_estimate=pl.CostEstimate(flops=flops, bytes_accessed=moved, transcendentals=0),
        name=name,
    )(*operands)


def pad_weight(weight_ref, padded):
    weight = weight_ref[...].astype(F32)
    unused = jnp.zeros((LANES - HEAD_DIM, weight.shape[1]), F32)
    for part in range(weight.shape[0] // HEAD_DIM):
        rows = jnp.concatenate([weight[part * HEAD_DIM : (part + 1) * HEAD_DIM], unused])
        padded[part * LANES : (part + 1) * LANES, :] = rows.astype(BF16)


def qkv_kernel(row_counts, mod_ref, weight_ref, *refs):
    row_refs, (out_ref, *made, normed) = refs[: len(row_counts)], refs[len(row_counts) :]
    _, latent, _ = place()
    shift, scale = mod_row(mod_ref, latent, 0), 1.0 + mod_row(mod_ref, latent, 1)
    chunk = 32
    at = 0
    for ref, count in zip(row_refs, row_counts):
        for low in range(0, count, chunk):
            rows = ref[low : low + chunk, :].astype(F32)
            normed[at : at + chunk, :] = (normalized(rows) * scale + shift).astype(BF16)
            at += chunk
    padded = weight_ref
    if made:
        padded = made[0]
        pad_weight(weight_ref, padded)
    lane = lax.broadcasted_iota(jnp.int32, (1, padded.shape[0]), 1)
    width = padded.shape[0] // 3
    factor = jnp.where(lane < width, HEAD_DIM ** (-0.5) * math.log2(math.e), 1.0)
    ones = jnp.where((lane >= 2 * width) & (lane % LANES == HEAD_DIM), 1.0, 0.0)
    block = at // 2
    for low in range(0, at, block):
        out = lax.dot_general(
            normed[low : low + block, :], padded[...], (((1,), (1,)), ((), ())), preferred_element_type=F32
        )
        out_ref[low : low + block, :] = (out * factor + ones).astype(BF16)


def qkv_rows(modulation, weight, pieces, row_counts, make_padded, name):
    count, width = sum(row_counts), weight.shape[1]
    padded_rows = weight.shape[0] // HEAD_DIM * LANES if make_padded else weight.shape[0]
    outs = [jax.ShapeDtypeStruct((count, padded_rows), BF16)]
    if make_padded:
        outs.append(jax.ShapeDtypeStruct((padded_rows, width), BF16))
    return call(
        functools.partial(qkv_kernel, row_counts),
        tuple(outs),
        (modulation, weight) + tuple(pieces),
        scratch=[pltpu.VMEM((count, width), BF16)],
        flops=2 * count * width * padded_rows,
        name=name,
    )


def position(order, offset):
    return sum(1 << i for i, bit in enumerate(order) if offset & bit)


def spread(order, index):
    return sum(bit for i, bit in enumerate(order) if index >> i & 1)


def attention_kernel(cap, packed_rows, counts_ref, early_ref, *refs):
    late_refs, (near_ref, far_ref, packed, out) = refs[:2], refs[2:]
    core, latent, member = place()
    half = cap // 2
    large, small = 2 * half // 3, half // 3
    width = early_ref.shape[1] // 3
    heads = width // LANES
    counts = [counts_ref[latent, member ^ d] for d in range(GROUP)]
    starts = [jnp.int32(0)]
    for d in range(GROUP):
        starts.append(starts[-1] + (counts[d] + ALIGN - 1) // ALIGN * ALIGN)
    total_rows = packed.shape[0]
    spare = total_rows - LEN
    packed[LEN:, :] = jnp.zeros((spare, packed.shape[1]), BF16)
    def lay(own_core):
        for d in range(GROUP):
            for k in range(2):
                away = own_core != k
                for is_small in range(2):
                    size = small if is_small else large
                    first = k * half + is_small * large
                    where = position(SMALL if is_small else LARGE[k], d)
                    source = early_ref
                    if where == 0:
                        base = first
                    elif where < 4:
                        base = cap + is_small * 3 * large + (where - 1) * size + away * 3 * half
                    else:
                        source = late_refs[away]
                        base = is_small * 4 * large + (where - 4) * size
                    packed[pl.ds(pl.multiple_of(starts[d] + first, ALIGN), size), :] = source[
                        base : base + size, :
                    ]

    pl.when(core == 0)(lambda: lay(0))
    pl.when(core == 1)(lambda: lay(1))
    slot = lax.broadcasted_iota(jnp.int32, (1, packed_rows), 1)
    valid = jnp.zeros((1, packed_rows), jnp.bool_)
    for d in range(GROUP):
        valid = valid | ((slot >= starts[d]) & (slot < starts[d] + counts[d]))
    bias = jnp.where(valid, 0.0, -1e30)
    out[LEN:, :] = jnp.zeros((spare, out.shape[1]), F32)
    block = packed_rows // 3
    for low in range(0, packed_rows, block):
        for head in range(heads):
            lanes = head * LANES
            queries = packed[low : low + block, lanes : lanes + LANES]
            keys = packed[:packed_rows, width + lanes : width + lanes + LANES]
            values = packed[:packed_rows, 2 * width + lanes : 2 * width + lanes + LANES]
            scores = lax.dot_general(
                queries, keys, (((1,), (1,)), ((), ())), preferred_element_type=F32
            )
            scores = scores + bias
            peak = jnp.max(scores, axis=-1, keepdims=True)
            probs = jnp.exp2(scores - peak).astype(BF16)
            mixed = jnp.dot(probs, values, preferred_element_type=F32)
            mixed = mixed / mixed[:, HEAD_DIM : HEAD_DIM + 1]
            out[low : low + block, lanes : lanes + LANES] = mixed
    targets = [
        jnp.where(core == 0, starts[spread(HEADS_TO[0], j)], starts[spread(HEADS_TO[1], j)])
        for j in range(GROUP)
    ]
    for pair in range(0, GROUP, 2):
        columns = []
        for head in range(heads):
            rows = [
                out[pl.ds(pl.multiple_of(targets[j], ALIGN), cap), head * LANES : (head + 1) * LANES]
                for j in (pair, pair + 1)
            ]
            columns.append(jnp.concatenate(rows).T[:HEAD_DIM])
        dest = near_ref if pair < GROUP // 2 else far_ref
        at = pair % (GROUP // 2) * cap
        dest[:, at : at + 2 * cap] = jnp.concatenate(columns).astype(BF16)


def attention(piece_rows, early, late, cap):
    packed_rows = LEN + GROUP * ALIGN
    total = -(-(packed_rows + cap) // 32) * 32
    width = early.shape[1] // 3
    heads = width // LANES
    shape = jax.ShapeDtypeStruct((heads * HEAD_DIM, GROUP // 2 * cap), BF16)
    return call(
        functools.partial(attention_kernel, cap, packed_rows),
        (shape, shape),
        (piece_rows, early) + tuple(late),
        scratch=[pltpu.VMEM((total, 3 * width), BF16), pltpu.VMEM((total, width), F32)],
        specs=[pl.BlockSpec(memory_space=pltpu.SMEM)] + [pl.BlockSpec(memory_space=pltpu.VMEM)] * 3,
        flops=4 * heads * packed_rows * packed_rows * LANES,
        name="attend",
    )


def project_kernel(cap, mod_ref, hidden_ref, mine_ref, mate_ref, *refs):
    proj_refs, plane_refs = refs[:8], refs[8 : 8 + GROUP // 2 - 1]
    mid_ref, mlp_ref, flat, weights = refs[8 + GROUP // 2 - 1 :]
    core, latent, member = place()
    heads = mine_ref.shape[0] // HEAD_DIM

    def put(block, j):
        offset = jnp.where(core == 0, spread(HEADS_TO[0], j), spread(HEADS_TO[1], j))
        for head in range(heads):
            rows = block[head * HEAD_DIM : (head + 1) * HEAD_DIM]
            flat[head * GROUP + offset] = rows

    put(mine_ref[...][:, :cap].astype(F32), 0)
    put(mate_ref[...][:, :cap].astype(F32), GROUP // 2)
    for j, ref in enumerate(plane_refs):
        both = ref[...].astype(F32)
        put(both[:, :cap], j + 1)
        put(both[:, cap:], (j + 1) ^ (GROUP // 2))
    for away in range(2):
        head = core if away == 0 else 1 - core
        at = 0
        for blocks, ref in zip((1, 1, 2, 4), proj_refs[4 * away : 4 * away + 4]):
            block = ref[ref.shape[0] - blocks * HEAD_DIM :, :].astype(F32)
            for row in range(0, block.shape[0], HEAD_DIM):
                offset = jnp.where(head == 0, spread(PROJ[0], at), spread(PROJ[1], at))
                weights[head * GROUP + offset] = block[row : row + HEAD_DIM]
                at += 1
    stacked = flat[...].reshape(heads * GROUP * HEAD_DIM, cap).astype(BF16)
    proj = weights[...].reshape(heads * GROUP * HEAD_DIM, weights.shape[2]).astype(BF16)
    attn_out = lax.dot_general(stacked, proj, (((0,), (0,)), ((), ())), preferred_element_type=F32)
    mid = hidden_ref[...].astype(F32) + mod_row(mod_ref, latent, 2) * attn_out
    mid_ref[...] = mid
    scale, shift = 1.0 + mod_row(mod_ref, latent, 4), mod_row(mod_ref, latent, 3)
    mlp_ref[...] = (normalized(mid) * scale + shift).astype(BF16)


def project(modulation, hidden_in, proj_parts, mine, mate, plane):
    cap, width = hidden_in.shape
    heads = mine.shape[0] // HEAD_DIM
    return call(
        functools.partial(project_kernel, cap),
        (jax.ShapeDtypeStruct((cap, width), F32), jax.ShapeDtypeStruct((cap, width), BF16)),
        (modulation, hidden_in, mine, mate) + tuple(proj_parts) + tuple(plane),
        scratch=[
            pltpu.VMEM((heads * GROUP, HEAD_DIM, cap), F32),
            pltpu.VMEM((heads * GROUP, HEAD_DIM, width), F32),
        ],
        flops=2 * cap * width * width,
        name="project",
    )


def pack_kernel(row_counts, up_ref, down_ref, *refs):
    far_refs, (up_all, down_all, sems) = refs[:-3], refs[-3:]
    core, _, _ = place()
    hidden, parts = up_ref.shape[0], len(far_refs) // 2
    own = [
        pltpu.make_async_copy(up_ref, up_all.at[pl.ds(0, hidden)], sems.at[2 * parts]),
        pltpu.make_async_copy(down_ref, down_all.at[pl.ds(0, hidden)], sems.at[2 * parts + 1]),
    ]
    for copy in own:
        copy.start()

    def fetch(dests):
        copies = []
        for d, dest in enumerate(dests):
            at = hidden
            for rows, ref in zip(row_counts, far_refs[parts * d : parts * (d + 1)]):
                source = ref.at[pl.ds(ref.shape[0] - rows, rows)]
                copies.append(
                    pltpu.make_async_copy(source, dest.at[pl.ds(at, rows)], sems.at[len(copies)])
                )
                at += rows
        for copy in copies:
            copy.start()
        for copy in copies:
            copy.wait()

    pl.when(core == 0)(lambda: fetch((up_all, down_all)))
    pl.when(core == 1)(lambda: fetch((down_all, up_all)))
    for copy in own:
        copy.wait()


def pack(up, down, far, row_counts):
    hidden, width = up.shape
    both = jax.ShapeDtypeStruct((2 * hidden, width), BF16)
    return call(
        functools.partial(pack_kernel, row_counts),
        (both, both),
        (up, down) + tuple(far),
        scratch=[pltpu.SemaphoreType.DMA((2 + len(far),))],
        specs=[pl.BlockSpec(memory_space=pl.ANY)] * (2 + len(far)),
        name="pack",
    )


def mlp_kernel(row_count, out_count, up_ref, down_ref, *refs):
    row_refs, out_refs, rows = refs[:row_count], refs[row_count:-1], refs[-1]
    at = 0
    for ref in row_refs:
        rows[at : at + ref.shape[0], :] = ref[...]
        at += ref.shape[0]
    units = lax.dot_general(
        rows[...], up_ref[...], (((1,), (1,)), ((), ())), preferred_element_type=F32
    )
    units = 0.5 * units * (1.0 + jnp.tanh(0.7978845608 * (units + 0.044715 * (units * units * units))))
    partial = jnp.dot(units.astype(BF16), down_ref[...], preferred_element_type=F32)
    at = 0
    for ref in out_refs:
        ref[...] = partial[at : at + ref.shape[0]].astype(ref.dtype)
        at += ref.shape[0]


def mlp_rows(pieces, packed, out_rows, dtype, name):
    count = sum(p.shape[0] for p in pieces)
    hidden, width = packed[0].shape
    outs = tuple(jax.ShapeDtypeStruct((rows, width), dtype) for rows in out_rows)
    return call(
        functools.partial(mlp_kernel, len(pieces), len(outs)),
        outs,
        tuple(packed) + tuple(pieces),
        scratch=[pltpu.VMEM((count, width), BF16)],
        flops=4 * count * width * hidden,
        name=name,
    )


def final_kernel(
    counts_ref, guide_ref, coef_ref, mod_ref, mid_ref, part_ref, noisy_ref, weight_ref,
    *refs,
):
    core, latent, member = place()
    cap = mid_ref.shape[0]
    sum_refs, (block_ref, pred_ref, base_ref, total) = refs[:-4], refs[-4:]
    chunk = cap // CHUNKS
    for i, (first, second) in enumerate(zip(sum_refs[:CHUNKS], sum_refs[CHUNKS:])):
        rows = slice(i * chunk, (i + 1) * chunk)
        total[rows, :] = part_ref[rows, :] + first[:chunk, :].astype(F32) + second[...].astype(F32)
    rows = (mid_ref[...] + mod_row(mod_ref, latent, 5) * total[...]).astype(BF16).astype(F32)
    count = counts_ref[latent, member]
    rows = jnp.where(lax.broadcasted_iota(jnp.int32, (cap, 1), 0) < count, rows, 0.0)
    block_ref[...] = rows.astype(BF16)
    scale, shift = 1.0 + mod_row(mod_ref, latent, 7), mod_row(mod_ref, latent, 6)
    final_in = (normalized(rows) * scale + shift).astype(BF16)
    pred = lax.dot_general(
        weight_ref[...], final_in, (((1,), (1,)), ((), ())), preferred_element_type=F32
    )
    guide = guide_ref[latent]
    valid = lax.broadcasted_iota(jnp.int32, (1, cap), 1) < count
    weighted = (-coef_ref[latent, 1] * jnp.where(core == 0, guide, 1.0 - guide)) * pred
    pred_ref[...] = jnp.where(valid, weighted, 0.0)
    base_ref[...] = jnp.where(valid, coef_ref[latent, 0] * noisy_ref[...], 0.0)


def final(scalars, modulation, mid, part, noisy, weight, firsts, seconds):
    cap, width = mid.shape
    smem, vmem = pl.BlockSpec(memory_space=pltpu.SMEM), pl.BlockSpec(memory_space=pltpu.VMEM)
    flat = jax.ShapeDtypeStruct(noisy.shape, F32)
    return call(
        final_kernel,
        (jax.ShapeDtypeStruct((cap, width), BF16), flat, flat),
        tuple(scalars) + (modulation, mid, part, noisy, weight) + tuple(firsts) + tuple(seconds),
        scratch=[pltpu.VMEM((cap, width), F32)],
        specs=[smem] * 3 + [vmem] * (5 + 2 * CHUNKS),
        flops=2 * cap * width * weight.shape[0],
        name="finish",
    )


def shards(
    hidden_in,
    noisy_latent,
    piece_rows,
    modulation,
    qkv_weight,
    proj_weight,
    up_weight,
    down_weight,
    final_weight,
    guidance,
    solver_coef,
):
    cap, width = hidden_in.shape
    half = cap // 2
    large, small = 2 * half // 3, half // 3
    core, _, _ = place()
    modulation = modulation[0]
    qkv_rows_t, proj_t, up_t, down_t = (
        w[0].T for w in (qkv_weight, proj_weight, up_weight, down_weight)
    )

    own_rows = after(lax.dynamic_slice_in_dim(hidden_in, core * half, half))
    large_rows, small_rows = own_rows[:large], own_rows[large:]
    hidden = up_t.shape[0]
    cuts = (0, FAR_EARLY, hidden)
    proj_rows = None
    got, away = [], []
    for step in range(3):
        payload = large_rows if step == 0 else jnp.concatenate([large_rows, proj_rows])
        got_large = permute_by(payload, [order[step] for order in LARGE])
        got_small = permute_by(small_rows, [SMALL[step]] * 2)
        if step == 0:
            up_t, down_t, _ = lax.optimization_barrier((up_t, down_t, got_large))
            sent = [
                jnp.where(core == 0, up_t[low:high], down_t[low:high])
                for low, high in zip(cuts[:-1], cuts[1:])
            ]
            proj_own = [
                lax.dynamic_slice_in_dim(proj_t, head * HEAD_DIM, HEAD_DIM) for head in (core, 1 - core)
            ]
            proj_rows = proj_own[0]
        elif step == 1:
            proj_rows = jnp.concatenate([proj_rows, got_large[2 * large :]])
        else:
            early, qkv_padded = qkv_rows(
                modulation,
                qkv_rows_t,
                (hidden_in, got[0][0], got[1][0], got[0][1], got[1][1])
                + (away[0][0], away[1][0], away[0][1], away[1][1]),
                (cap, large, 2 * large, small, 2 * small) + (large, 2 * large, small, 2 * small),
                True,
                "qkv_early",
            )
            got_large, got_small, early, *sent = lax.optimization_barrier(
                (got_large, got_small, early, *sent)
            )
            proj_rows = jnp.concatenate([proj_rows, got_large[4 * large :]])
        if step < 2:
            large_rows = jnp.concatenate([large_rows, got_large[: large << step]])
            small_rows = jnp.concatenate([small_rows, got_small])
        got.append((got_large, got_small))
        away.append((from_other_half(got_large), from_other_half(got_small)))
    proj_last = permute_by(proj_rows, [order[2] for order in PROJ])
    far = [permute_by(sent[0], [GROUP // 2] * 2)]
    counts = (4 * large, 4 * small)
    late = list(qkv_rows(modulation, qkv_padded, got[2], counts, False, "qkv_late_own"))
    *other, late[0] = lax.optimization_barrier((*away[2], late[0]))
    late += qkv_rows(modulation, qkv_padded, other, counts, False, "qkv_late_other")
    mine, sent_heads = attention(piece_rows, early, late, cap)
    mate = permute_by(sent_heads, [order[2] for order in HEADS_TO])
    mate, proj_last = lax.optimization_barrier((mate, proj_last))
    proj_parts = [proj_own[0], got[1][0], got[2][0], proj_last]
    proj_parts += [proj_own[1], away[1][0], away[2][0], from_other_half(proj_last)]
    plane = []
    for j in range(1, GROUP // 2):
        both = jnp.concatenate([a[:, j * cap : (j + 1) * cap] for a in (mine, mate)], axis=1)
        plane.append(permute_by(both, [spread(order, j) for order in HEADS_TO]))
    far[0], *plane = lax.optimization_barrier((far[0], *plane))
    far.append(permute_by(after(sent[1], *plane), [GROUP // 2] * 2))
    mid, mlp_in = project(modulation, hidden_in, proj_parts, mine, mate, plane)

    chunk = cap // CHUNKS
    side = permute_by(mlp_in, (1, 2))
    both = [
        jnp.concatenate([rows[low : low + chunk] for rows in (mlp_in, side)])
        for low in range(0, cap, chunk)
    ]
    across = [permute_by(rows, (2, 1)) for rows in both]
    far[1] = after(far[1], *both)
    far += [from_other_half(rows) for rows in far]
    packed = pack(up_t, down_t, far, [high - low for low, high in zip(cuts[:-1], cuts[1:])])
    sums = [
        mlp_rows((rows,), packed, (2 * chunk,), BF16, f"mlp_far{i}")[0] for i, rows in enumerate(across)
    ]
    firsts = [permute_by(rows, (2, 1)) for rows in sums]
    part, *side_parts = mlp_rows(
        (after(mlp_in, *sums), side), packed, (cap,) + (chunk,) * CHUNKS, F32, "mlp_near"
    )
    seconds = [
        permute_by((rows + first[chunk:].astype(F32)).astype(BF16), (1, 2))
        for rows, first in zip(side_parts, firsts)
    ]
    block_rows, pred, base = final(
        (piece_rows, guidance, solver_coef),
        modulation,
        mid,
        part,
        noisy_latent.T,
        final_weight.T,
        firsts,
        seconds,
    )
    next_latent = base + (pred + from_other_half(pred))
    return (next_latent.T, block_rows[None])


def solution(mesh):
    placed = (
        P("tok", None),
        P("tok", None),
        P(),
        P("cfg", None, None, None),
        P("tok", None, None),
        P("tok", None, None),
        P("tok", None, None),
        P("tok", None, None),
        P(),
        P(),
        P(),
    )
    return jax.shard_map(
        shards,
        mesh=mesh,
        in_specs=placed,
        out_specs=(P("tok", None), P("cfg", "tok", None)),
        check_vma=False,
    )
```

```python
import functools
import math

import jax
import jax.numpy as jnp
from jax import lax
from jax.experimental import pallas as pl
from jax.experimental.pallas import tpu as pltpu
from jax.sharding import PartitionSpec as P

HEAD_DIM = 72
GROUP = 8
LEN = 1024
LANES = 128
ALIGN = 16
LARGE = ((1, 2, 4), (2, 4, 1))
SMALL = (4, 1, 2)
PROJ = ((2, 4, 1), (4, 1, 2))
HEADS_TO = ((2, 4, 1), (4, 1, 2))
FAR_EARLY = (80, 320)
CHUNKS = 3
F32 = jnp.float32
BF16 = jnp.bfloat16


def permute_by(block, offsets):
    count = lax.axis_size("tok")
    route = [
        (half * count + i, half * count + (i ^ offset))
        for half, offset in enumerate(offsets)
        for i in range(count)
    ]
    return lax.ppermute(block, ("cfg", "tok"), route)


def from_other_half(block):
    return lax.ppermute(block, "cfg", [(0, 1), (1, 0)])


def after(value, *earlier):
    return lax.optimization_barrier((value,) + earlier)[0]


def place():
    pos = lax.axis_index("tok")
    return lax.axis_index("cfg"), pos // GROUP, pos % GROUP


def normalized(values):
    center = values - jnp.mean(values, axis=-1, keepdims=True)
    spread = jnp.mean(center * center, axis=-1, keepdims=True)
    return center * lax.rsqrt(spread + 1e-06)


def mod_row(mod_ref, latent, k):
    return mod_ref[latent, k : k + 1, :]


def call(kernel, out_shape, operands, scratch=(), specs=None, flops=0, name=None, vmem=40):
    whole = pl.BlockSpec(memory_space=pltpu.VMEM)
    moved = sum(math.prod(o.shape) * o.dtype.itemsize for o in operands)
    return pl.pallas_call(
        kernel,
        out_shape=out_shape,
        in_specs=specs or [whole] * len(operands),
        out_specs=jax.tree.map(lambda _: whole, out_shape),
        scratch_shapes=list(scratch),
        compiler_params=pltpu.CompilerParams(vmem_limit_bytes=vmem << 20),
        cost_estimate=pl.CostEstimate(flops=flops, bytes_accessed=moved, transcendentals=0),
        name=name,
    )(*operands)


def first_kernel(hidden_ref, up_ref, down_ref, large_ref, small_ref, sems):
    core, _, _ = place()
    half = hidden_ref.shape[0] // 2
    large, small = large_ref.shape[0], half - large_ref.shape[0]
    first = pl.multiple_of(core * half, 32)
    copies = [
        pltpu.make_async_copy(hidden_ref.at[pl.ds(first, large)], large_ref, sems.at[0]),
        pltpu.make_async_copy(
            hidden_ref.at[pl.ds(first + large, small)], small_ref.at[pl.ds(0, small)], sems.at[1]
        ),
    ]
    for copy in copies:
        copy.start()
    rest = small_ref.shape[0] - small

    def bring(weight_ref):
        copy = pltpu.make_async_copy(
            weight_ref.at[pl.ds(0, rest)], small_ref.at[pl.ds(small, rest)], sems.at[2]
        )
        copy.start()
        copy.wait()

    pl.when(core == 0)(lambda: bring(up_ref))
    pl.when(core == 1)(lambda: bring(down_ref))
    for copy in copies:
        copy.wait()


def first_payloads(hidden_in, up, down, large, small, weight_rows):
    width = hidden_in.shape[1]
    return call(
        first_kernel,
        (
            jax.ShapeDtypeStruct((large, width), BF16),
            jax.ShapeDtypeStruct((small + weight_rows, width), BF16),
        ),
        (hidden_in, up, down),
        scratch=[pltpu.SemaphoreType.DMA((3,))],
        specs=[pl.BlockSpec(memory_space=pl.ANY)] * 3,
        name="first",
    )


def pad_weight(weight_ref, padded):
    weight = weight_ref[...].astype(F32)
    unused = jnp.zeros((LANES - HEAD_DIM, weight.shape[1]), F32)
    for part in range(weight.shape[0] // HEAD_DIM):
        rows = jnp.concatenate([weight[part * HEAD_DIM : (part + 1) * HEAD_DIM], unused])
        padded[part * LANES : (part + 1) * LANES, :] = rows.astype(BF16)


def qkv_kernel(row_counts, mod_ref, weight_ref, *refs):
    row_refs, (out_ref, *made, normed) = refs[: len(row_counts)], refs[len(row_counts) :]
    _, latent, _ = place()
    shift, scale = mod_row(mod_ref, latent, 0), 1.0 + mod_row(mod_ref, latent, 1)
    chunk = 32
    at = 0
    for ref, count in zip(row_refs, row_counts):
        for low in range(0, count, chunk):
            rows = ref[low : low + chunk, :].astype(F32)
            normed[at : at + chunk, :] = (normalized(rows) * scale + shift).astype(BF16)
            at += chunk
    padded = weight_ref
    if made:
        padded = made[0]
        pad_weight(weight_ref, padded)
    lane = lax.broadcasted_iota(jnp.int32, (1, padded.shape[0]), 1)
    width = padded.shape[0] // 3
    factor = jnp.where(lane < width, HEAD_DIM ** (-0.5) * math.log2(math.e), 1.0)
    ones = jnp.where((lane >= 2 * width) & (lane % LANES == HEAD_DIM), 1.0, 0.0)
    block = at // 2
    for low in range(0, at, block):
        out = lax.dot_general(
            normed[low : low + block, :], padded[...], (((1,), (1,)), ((), ())), preferred_element_type=F32
        )
        out_ref[low : low + block, :] = (out * factor + ones).astype(BF16)


def qkv_rows(modulation, weight, pieces, row_counts, make_padded, name):
    count, width = sum(row_counts), weight.shape[1]
    padded_rows = weight.shape[0] // HEAD_DIM * LANES if make_padded else weight.shape[0]
    outs = [jax.ShapeDtypeStruct((count, padded_rows), BF16)]
    if make_padded:
        outs.append(jax.ShapeDtypeStruct((padded_rows, width), BF16))
    return call(
        functools.partial(qkv_kernel, row_counts),
        tuple(outs),
        (modulation, weight) + tuple(pieces),
        scratch=[pltpu.VMEM((count, width), BF16)],
        flops=2 * count * width * padded_rows,
        name=name,
    )


def position(order, offset):
    return sum(1 << i for i, bit in enumerate(order) if offset & bit)


def spread(order, index):
    return sum(bit for i, bit in enumerate(order) if index >> i & 1)


def attention_kernel(cap, packed_rows, counts_ref, early_ref, *refs):
    late_refs, (near_ref, far_ref, packed, out) = refs[:2], refs[2:]
    core, latent, member = place()
    half = cap // 2
    large, small = 2 * half // 3, half // 3
    width = early_ref.shape[1] // 3
    heads = width // LANES
    counts = [counts_ref[latent, member ^ d] for d in range(GROUP)]
    starts = [jnp.int32(0)]
    for d in range(GROUP):
        starts.append(starts[-1] + (counts[d] + ALIGN - 1) // ALIGN * ALIGN)
    total_rows = packed.shape[0]
    spare = total_rows - LEN
    packed[LEN:, :] = jnp.zeros((spare, packed.shape[1]), BF16)
    def lay(own_core):
        for d in range(GROUP):
            for k in range(2):
                away = own_core != k
                for is_small in range(2):
                    size = small if is_small else large
                    first = k * half + is_small * large
                    where = position(SMALL if is_small else LARGE[k], d)
                    source = early_ref
                    if where == 0:
                        base = first
                    elif where < 4:
                        base = cap + is_small * 3 * large + (where - 1) * size + away * 3 * half
                    else:
                        source = late_refs[away]
                        base = is_small * 4 * large + (where - 4) * size
                    packed[pl.ds(pl.multiple_of(starts[d] + first, ALIGN), size), :] = source[
                        base : base + size, :
                    ]

    pl.when(core == 0)(lambda: lay(0))
    pl.when(core == 1)(lambda: lay(1))
    slot = lax.broadcasted_iota(jnp.int32, (1, packed_rows), 1)
    valid = jnp.zeros((1, packed_rows), jnp.bool_)
    for d in range(GROUP):
        valid = valid | ((slot >= starts[d]) & (slot < starts[d] + counts[d]))
    bias = jnp.where(valid, 0.0, -1e30)
    out[LEN:, :] = jnp.zeros((spare, out.shape[1]), F32)
    block = packed_rows // 3
    for low in range(0, packed_rows, block):
        for head in range(heads):
            lanes = head * LANES
            queries = packed[low : low + block, lanes : lanes + LANES]
            keys = packed[:packed_rows, width + lanes : width + lanes + LANES]
            values = packed[:packed_rows, 2 * width + lanes : 2 * width + lanes + LANES]
            scores = lax.dot_general(
                queries, keys, (((1,), (1,)), ((), ())), preferred_element_type=F32
            )
            scores = scores + bias
            peak = jnp.max(scores, axis=-1, keepdims=True)
            probs = jnp.exp2(scores - peak).astype(BF16)
            mixed = jnp.dot(probs, values, preferred_element_type=F32)
            mixed = mixed / mixed[:, HEAD_DIM : HEAD_DIM + 1]
            out[low : low + block, lanes : lanes + LANES] = mixed
    targets = [
        jnp.where(core == 0, starts[spread(HEADS_TO[0], j)], starts[spread(HEADS_TO[1], j)])
        for j in range(GROUP)
    ]
    for pair in range(0, GROUP, 2):
        columns = []
        for head in range(heads):
            rows = [
                out[pl.ds(pl.multiple_of(targets[j], ALIGN), cap), head * LANES : (head + 1) * LANES]
                for j in (pair, pair + 1)
            ]
            columns.append(jnp.concatenate(rows).T[:HEAD_DIM])
        dest = near_ref if pair < GROUP // 2 else far_ref
        at = pair % (GROUP // 2) * cap
        dest[:, at : at + 2 * cap] = jnp.concatenate(columns).astype(BF16)


def attention(piece_rows, early, late, cap):
    packed_rows = LEN + GROUP * ALIGN
    total = -(-(packed_rows + cap) // 32) * 32
    width = early.shape[1] // 3
    heads = width // LANES
    shape = jax.ShapeDtypeStruct((heads * HEAD_DIM, GROUP // 2 * cap), BF16)
    return call(
        functools.partial(attention_kernel, cap, packed_rows),
        (shape, shape),
        (piece_rows, early) + tuple(late),
        scratch=[pltpu.VMEM((total, 3 * width), BF16), pltpu.VMEM((total, width), F32)],
        specs=[pl.BlockSpec(memory_space=pltpu.SMEM)] + [pl.BlockSpec(memory_space=pltpu.VMEM)] * 3,
        flops=4 * heads * packed_rows * packed_rows * LANES,
        name="attend",
    )


def project_kernel(cap, mod_ref, hidden_ref, mine_ref, mate_ref, *refs):
    proj_refs, plane_refs = refs[:8], refs[8 : 8 + GROUP // 2 - 1]
    mid_ref, mlp_ref, flat, weights = refs[8 + GROUP // 2 - 1 :]
    core, latent, member = place()
    heads = mine_ref.shape[0] // HEAD_DIM

    def put(block, j):
        offset = jnp.where(core == 0, spread(HEADS_TO[0], j), spread(HEADS_TO[1], j))
        for head in range(heads):
            rows = block[head * HEAD_DIM : (head + 1) * HEAD_DIM]
            flat[head * GROUP + offset] = rows

    put(mine_ref[...][:, :cap].astype(F32), 0)
    put(mate_ref[...][:, :cap].astype(F32), GROUP // 2)
    for j, ref in enumerate(plane_refs):
        both = ref[...].astype(F32)
        put(both[:, :cap], j + 1)
        put(both[:, cap:], (j + 1) ^ (GROUP // 2))
    for away in range(2):
        head = core if away == 0 else 1 - core
        at = 0
        for blocks, ref in zip((1, 1, 2, 4), proj_refs[4 * away : 4 * away + 4]):
            block = ref[ref.shape[0] - blocks * HEAD_DIM :, :].astype(F32)
            for row in range(0, block.shape[0], HEAD_DIM):
                offset = jnp.where(head == 0, spread(PROJ[0], at), spread(PROJ[1], at))
                weights[head * GROUP + offset] = block[row : row + HEAD_DIM]
                at += 1
    stacked = flat[...].reshape(heads * GROUP * HEAD_DIM, cap).astype(BF16)
    proj = weights[...].reshape(heads * GROUP * HEAD_DIM, weights.shape[2]).astype(BF16)
    attn_out = lax.dot_general(stacked, proj, (((0,), (0,)), ((), ())), preferred_element_type=F32)
    mid = hidden_ref[...].astype(F32) + mod_row(mod_ref, latent, 2) * attn_out
    mid_ref[...] = mid
    scale, shift = 1.0 + mod_row(mod_ref, latent, 4), mod_row(mod_ref, latent, 3)
    mlp_ref[...] = (normalized(mid) * scale + shift).astype(BF16)


def project(modulation, hidden_in, proj_parts, mine, mate, plane):
    cap, width = hidden_in.shape
    heads = mine.shape[0] // HEAD_DIM
    return call(
        functools.partial(project_kernel, cap),
        (jax.ShapeDtypeStruct((cap, width), F32), jax.ShapeDtypeStruct((cap, width), BF16)),
        (modulation, hidden_in, mine, mate) + tuple(proj_parts) + tuple(plane),
        scratch=[
            pltpu.VMEM((heads * GROUP, HEAD_DIM, cap), F32),
            pltpu.VMEM((heads * GROUP, HEAD_DIM, width), F32),
        ],
        flops=2 * cap * width * width,
        name="project",
    )


def pack_kernel(row_counts, up_ref, down_ref, *refs):
    far_refs, (up_all, down_all, sems) = refs[:-3], refs[-3:]
    core, _, _ = place()
    hidden, parts = up_ref.shape[0], len(far_refs) // 2
    own = [
        pltpu.make_async_copy(up_ref, up_all.at[pl.ds(0, hidden)], sems.at[2 * parts]),
        pltpu.make_async_copy(down_ref, down_all.at[pl.ds(0, hidden)], sems.at[2 * parts + 1]),
    ]
    for copy in own:
        copy.start()

    def fetch(dests):
        copies = []
        for d, dest in enumerate(dests):
            at = hidden
            for rows, ref in zip(row_counts, far_refs[parts * d : parts * (d + 1)]):
                source = ref.at[pl.ds(ref.shape[0] - rows, rows)]
                copies.append(
                    pltpu.make_async_copy(source, dest.at[pl.ds(at, rows)], sems.at[len(copies)])
                )
                at += rows
        for copy in copies:
            copy.start()
        for copy in copies:
            copy.wait()

    pl.when(core == 0)(lambda: fetch((up_all, down_all)))
    pl.when(core == 1)(lambda: fetch((down_all, up_all)))
    for copy in own:
        copy.wait()


def pack(up, down, far, row_counts):
    hidden, width = up.shape
    both = jax.ShapeDtypeStruct((2 * hidden, width), BF16)
    return call(
        functools.partial(pack_kernel, row_counts),
        (both, both),
        (up, down) + tuple(far),
        scratch=[pltpu.SemaphoreType.DMA((2 + len(far),))],
        specs=[pl.BlockSpec(memory_space=pl.ANY)] * (2 + len(far)),
        name="pack",
    )


def mlp_kernel(row_count, out_count, up_ref, down_ref, *refs):
    row_refs, out_refs, rows = refs[:row_count], refs[row_count:-1], refs[-1]
    at = 0
    for ref in row_refs:
        rows[at : at + ref.shape[0], :] = ref[...]
        at += ref.shape[0]
    units = lax.dot_general(
        rows[...], up_ref[...], (((1,), (1,)), ((), ())), preferred_element_type=F32
    )
    units = 0.5 * units * (1.0 + jnp.tanh(0.7978845608 * (units + 0.044715 * (units * units * units))))
    partial = jnp.dot(units.astype(BF16), down_ref[...], preferred_element_type=F32)
    at = 0
    for ref in out_refs:
        ref[...] = partial[at : at + ref.shape[0]].astype(ref.dtype)
        at += ref.shape[0]


def mlp_rows(pieces, packed, out_rows, dtype, name):
    count = sum(p.shape[0] for p in pieces)
    hidden, width = packed[0].shape
    outs = tuple(jax.ShapeDtypeStruct((rows, width), dtype) for rows in out_rows)
    return call(
        functools.partial(mlp_kernel, len(pieces), len(outs)),
        outs,
        tuple(packed) + tuple(pieces),
        scratch=[pltpu.VMEM((count, width), BF16)],
        flops=4 * count * width * hidden,
        name=name,
    )


def final_kernel(
    counts_ref, guide_ref, coef_ref, mod_ref, mid_ref, part_ref, noisy_ref, weight_ref,
    *refs,
):
    core, latent, member = place()
    cap = mid_ref.shape[0]
    sum_refs, (block_ref, pred_ref, base_ref, total) = refs[:-4], refs[-4:]
    chunk = cap // CHUNKS
    for i, (first, second) in enumerate(zip(sum_refs[:CHUNKS], sum_refs[CHUNKS:])):
        rows = slice(i * chunk, (i + 1) * chunk)
        total[rows, :] = part_ref[rows, :] + first[:chunk, :].astype(F32) + second[...].astype(F32)
    rows = (mid_ref[...] + mod_row(mod_ref, latent, 5) * total[...]).astype(BF16).astype(F32)
    count = counts_ref[latent, member]
    rows = jnp.where(lax.broadcasted_iota(jnp.int32, (cap, 1), 0) < count, rows, 0.0)
    block_ref[...] = rows.astype(BF16)
    scale, shift = 1.0 + mod_row(mod_ref, latent, 7), mod_row(mod_ref, latent, 6)
    final_in = (normalized(rows) * scale + shift).astype(BF16)
    pred = lax.dot_general(
        weight_ref[...], final_in, (((1,), (1,)), ((), ())), preferred_element_type=F32
    )
    guide = guide_ref[latent]
    valid = lax.broadcasted_iota(jnp.int32, (1, cap), 1) < count
    weighted = (-coef_ref[latent, 1] * jnp.where(core == 0, guide, 1.0 - guide)) * pred
    pred_ref[...] = jnp.where(valid, weighted, 0.0)
    base_ref[...] = jnp.where(valid, coef_ref[latent, 0] * noisy_ref[...], 0.0)


def final(scalars, modulation, mid, part, noisy, weight, firsts, seconds):
    cap, width = mid.shape
    smem, vmem = pl.BlockSpec(memory_space=pltpu.SMEM), pl.BlockSpec(memory_space=pltpu.VMEM)
    flat = jax.ShapeDtypeStruct(noisy.shape, F32)
    return call(
        final_kernel,
        (jax.ShapeDtypeStruct((cap, width), BF16), flat, flat),
        tuple(scalars) + (modulation, mid, part, noisy, weight) + tuple(firsts) + tuple(seconds),
        scratch=[pltpu.VMEM((cap, width), F32)],
        specs=[smem] * 3 + [vmem] * (5 + 2 * CHUNKS),
        flops=2 * cap * width * weight.shape[0],
        name="finish",
    )


def shards(
    hidden_in,
    noisy_latent,
    piece_rows,
    modulation,
    qkv_weight,
    proj_weight,
    up_weight,
    down_weight,
    final_weight,
    guidance,
    solver_coef,
):
    cap, width = hidden_in.shape
    half = cap // 2
    large, small = 2 * half // 3, half // 3
    core, _, _ = place()
    modulation = modulation[0]
    qkv_rows_t, proj_t, up_t, down_t = (
        w[0].T for w in (qkv_weight, proj_weight, up_weight, down_weight)
    )

    hidden = up_t.shape[0]
    cuts = (0, FAR_EARLY[0], sum(FAR_EARLY), hidden)
    large_rows, small_rows = first_payloads(hidden_in, up_t, down_t, large, small, cuts[1])
    proj_rows = None
    got, away = [], []
    for step in range(3):
        payload = large_rows if step == 0 else jnp.concatenate([large_rows, proj_rows])
        got_large = permute_by(payload, [order[step] for order in LARGE])
        got_small = permute_by(small_rows, [SMALL[step]] * 2)
        if step == 0:
            up_t, down_t, _ = lax.optimization_barrier((up_t, down_t, got_large))
            sent = [
                jnp.where(core == 0, up_t[low:high], down_t[low:high])
                for low, high in zip(cuts[1:-1], cuts[2:])
            ]
            proj_own = [
                lax.dynamic_slice_in_dim(proj_t, head * HEAD_DIM, HEAD_DIM) for head in (core, 1 - core)
            ]
            proj_rows = proj_own[0]
        elif step == 1:
            proj_rows = jnp.concatenate([proj_rows, got_large[2 * large :]])
        else:
            early, qkv_padded = qkv_rows(
                modulation,
                qkv_rows_t,
                (hidden_in, got[0][0], got[1][0], got[0][1], got[1][1])
                + (away[0][0], away[1][0], away[0][1], away[1][1]),
                (cap, large, 2 * large, small, 2 * small) + (large, 2 * large, small, 2 * small),
                True,
                "qkv_early",
            )
            got_large, got_small, early, *sent = lax.optimization_barrier(
                (got_large, got_small, early, *sent)
            )
            proj_rows = jnp.concatenate([proj_rows, got_large[4 * large :]])
        if step < 2:
            large_rows = jnp.concatenate([large_rows, got_large[: large << step]])
            small_rows = jnp.concatenate([rows[: small << step] for rows in (small_rows, got_small)])
        got.append((got_large, got_small))
        away.append((from_other_half(got_large), from_other_half(got_small)))
    proj_last = permute_by(proj_rows, [order[2] for order in PROJ])
    far = [got[0][1], permute_by(sent[0], [GROUP // 2] * 2)]
    counts = (4 * large, 4 * small)
    late = list(qkv_rows(modulation, qkv_padded, got[2], counts, False, "qkv_late_own"))
    *other, late[0] = lax.optimization_barrier((*away[2], late[0]))
    late += qkv_rows(modulation, qkv_padded, other, counts, False, "qkv_late_other")
    mine, sent_heads = attention(piece_rows, early, late, cap)
    mate = permute_by(sent_heads, [order[2] for order in HEADS_TO])
    mate, proj_last = lax.optimization_barrier((mate, proj_last))
    proj_parts = [proj_own[0], got[1][0], got[2][0], proj_last]
    proj_parts += [proj_own[1], away[1][0], away[2][0], from_other_half(proj_last)]
    plane = []
    for j in range(1, GROUP // 2):
        both = jnp.concatenate([a[:, j * cap : (j + 1) * cap] for a in (mine, mate)], axis=1)
        plane.append(permute_by(both, [spread(order, j) for order in HEADS_TO]))
    far[1], *plane = lax.optimization_barrier((far[1], *plane))
    far.append(permute_by(after(sent[1], *plane), [GROUP // 2] * 2))
    mid, mlp_in = project(modulation, hidden_in, proj_parts, mine, mate, plane)

    chunk = cap // CHUNKS
    side = permute_by(mlp_in, (1, 2))
    both = [
        jnp.concatenate([rows[low : low + chunk] for rows in (mlp_in, side)])
        for low in range(0, cap, chunk)
    ]
    across = [permute_by(rows, (2, 1)) for rows in both]
    far[2] = after(far[2], *both)
    far += [away[0][1]] + [from_other_half(rows) for rows in far[1:]]
    packed = pack(up_t, down_t, far, [high - low for low, high in zip(cuts[:-1], cuts[1:])])
    sums = [
        mlp_rows((rows,), packed, (2 * chunk,), BF16, f"mlp_far{i}")[0] for i, rows in enumerate(across)
    ]
    firsts = [permute_by(rows, (2, 1)) for rows in sums]
    part, *side_parts = mlp_rows(
        (after(mlp_in, *sums), side), packed, (cap,) + (chunk,) * CHUNKS, F32, "mlp_near"
    )
    seconds = [
        permute_by((rows + first[chunk:].astype(F32)).astype(BF16), (1, 2))
        for rows, first in zip(side_parts, firsts)
    ]
    block_rows, pred, base = final(
        (piece_rows, guidance, solver_coef),
        modulation,
        mid,
        part,
        noisy_latent.T,
        final_weight.T,
        firsts,
        seconds,
    )
    next_latent = base + (pred + from_other_half(pred))
    return (next_latent.T, block_rows[None])


def solution(mesh):
    placed = (
        P("tok", None),
        P("tok", None),
        P(),
        P("cfg", None, None, None),
        P("tok", None, None),
        P("tok", None, None),
        P("tok", None, None),
        P("tok", None, None),
        P(),
        P(),
        P(),
    )
    return jax.shard_map(
        shards,
        mesh=mesh,
        in_specs=placed,
        out_specs=(P("tok", None), P("cfg", "tok", None)),
        check_vma=False,
    )
```

```python
import functools
import math

import jax
import jax.numpy as jnp
from jax import lax
from jax.experimental import pallas as pl
from jax.experimental.pallas import tpu as pltpu
from jax.sharding import PartitionSpec as P

HEAD_DIM = 72
GROUP = 8
LEN = 1024
LANES = 128
ALIGN = 16
LARGE = ((1, 2, 4), (2, 4, 1))
SMALL = (4, 1, 2)
PROJ = ((2, 4, 1), (4, 1, 2))
HEADS_TO = ((2, 4, 1), (4, 1, 2))
FAR_EARLY = (80, 320)
CHUNKS = 3
F32 = jnp.float32
BF16 = jnp.bfloat16


def permute_by(block, offsets):
    count = lax.axis_size("tok")
    route = [
        (half * count + i, half * count + (i ^ offset))
        for half, offset in enumerate(offsets)
        for i in range(count)
    ]
    return lax.ppermute(block, ("cfg", "tok"), route)


def from_other_half(block):
    return lax.ppermute(block, "cfg", [(0, 1), (1, 0)])


def after(value, *earlier):
    return lax.optimization_barrier((value,) + earlier)[0]


def place():
    pos = lax.axis_index("tok")
    return lax.axis_index("cfg"), pos // GROUP, pos % GROUP


def normalized(values):
    center = values - jnp.mean(values, axis=-1, keepdims=True)
    spread = jnp.mean(center * center, axis=-1, keepdims=True)
    return center * lax.rsqrt(spread + 1e-06)


def mod_row(mod_ref, latent, k):
    return mod_ref[latent, k : k + 1, :]


def call(kernel, out_shape, operands, scratch=(), specs=None, flops=0, name=None, vmem=40):
    whole = pl.BlockSpec(memory_space=pltpu.VMEM)
    moved = sum(math.prod(o.shape) * o.dtype.itemsize for o in operands)
    return pl.pallas_call(
        kernel,
        out_shape=out_shape,
        in_specs=specs or [whole] * len(operands),
        out_specs=jax.tree.map(lambda _: whole, out_shape),
        scratch_shapes=list(scratch),
        compiler_params=pltpu.CompilerParams(vmem_limit_bytes=vmem << 20),
        cost_estimate=pl.CostEstimate(flops=flops, bytes_accessed=moved, transcendentals=0),
        name=name,
    )(*operands)


def first_kernel(hidden_ref, up_ref, down_ref, large_ref, small_ref, sems):
    core, _, _ = place()
    half = hidden_ref.shape[0] // 2
    large, small = large_ref.shape[0], half - large_ref.shape[0]
    first = pl.multiple_of(core * half, 32)
    copies = [
        pltpu.make_async_copy(hidden_ref.at[pl.ds(first, large)], large_ref, sems.at[0]),
        pltpu.make_async_copy(
            hidden_ref.at[pl.ds(first + large, small)], small_ref.at[pl.ds(0, small)], sems.at[1]
        ),
    ]
    for copy in copies:
        copy.start()
    rest = small_ref.shape[0] - small

    def bring(weight_ref):
        copy = pltpu.make_async_copy(
            weight_ref.at[pl.ds(0, rest)], small_ref.at[pl.ds(small, rest)], sems.at[2]
        )
        copy.start()
        copy.wait()

    pl.when(core == 0)(lambda: bring(up_ref))
    pl.when(core == 1)(lambda: bring(down_ref))
    for copy in copies:
        copy.wait()


def first_payloads(hidden_in, up, down, large, small, weight_rows):
    width = hidden_in.shape[1]
    return call(
        first_kernel,
        (
            jax.ShapeDtypeStruct((large, width), BF16),
            jax.ShapeDtypeStruct((small + weight_rows, width), BF16),
        ),
        (hidden_in, up, down),
        scratch=[pltpu.SemaphoreType.DMA((3,))],
        specs=[pl.BlockSpec(memory_space=pl.ANY)] * 3,
        name="first",
        vmem=63,
    )


def pad_weight(weight_ref, padded):
    weight = weight_ref[...].astype(F32)
    unused = jnp.zeros((LANES - HEAD_DIM, weight.shape[1]), F32)
    for part in range(weight.shape[0] // HEAD_DIM):
        rows = jnp.concatenate([weight[part * HEAD_DIM : (part + 1) * HEAD_DIM], unused])
        padded[part * LANES : (part + 1) * LANES, :] = rows.astype(BF16)


def qkv_kernel(row_counts, mod_ref, weight_ref, *refs):
    row_refs, (out_ref, *made, normed) = refs[: len(row_counts)], refs[len(row_counts) :]
    _, latent, _ = place()
    shift, scale = mod_row(mod_ref, latent, 0), 1.0 + mod_row(mod_ref, latent, 1)
    chunk = 32
    at = 0
    for ref, count in zip(row_refs, row_counts):
        for low in range(0, count, chunk):
            rows = ref[low : low + chunk, :].astype(F32)
            normed[at : at + chunk, :] = (normalized(rows) * scale + shift).astype(BF16)
            at += chunk
    padded = weight_ref
    if made:
        padded = made[0]
        pad_weight(weight_ref, padded)
    lane = lax.broadcasted_iota(jnp.int32, (1, padded.shape[0]), 1)
    width = padded.shape[0] // 3
    factor = jnp.where(lane < width, HEAD_DIM ** (-0.5) * math.log2(math.e), 1.0)
    ones = jnp.where((lane >= 2 * width) & (lane % LANES == HEAD_DIM), 1.0, 0.0)
    block = at // 2
    for low in range(0, at, block):
        out = lax.dot_general(
            normed[low : low + block, :], padded[...], (((1,), (1,)), ((), ())), preferred_element_type=F32
        )
        out_ref[low : low + block, :] = (out * factor + ones).astype(BF16)


def qkv_rows(modulation, weight, pieces, row_counts, make_padded, name):
    count, width = sum(row_counts), weight.shape[1]
    padded_rows = weight.shape[0] // HEAD_DIM * LANES if make_padded else weight.shape[0]
    outs = [jax.ShapeDtypeStruct((count, padded_rows), BF16)]
    if make_padded:
        outs.append(jax.ShapeDtypeStruct((padded_rows, width), BF16))
    return call(
        functools.partial(qkv_kernel, row_counts),
        tuple(outs),
        (modulation, weight) + tuple(pieces),
        scratch=[pltpu.VMEM((count, width), BF16)],
        flops=2 * count * width * padded_rows,
        name=name,
    )


def position(order, offset):
    return sum(1 << i for i, bit in enumerate(order) if offset & bit)


def spread(order, index):
    return sum(bit for i, bit in enumerate(order) if index >> i & 1)


def attention_kernel(cap, packed_rows, counts_ref, early_ref, *refs):
    late_refs, (near_ref, far_ref, packed, out) = refs[:2], refs[2:]
    core, latent, member = place()
    half = cap // 2
    large, small = 2 * half // 3, half // 3
    width = early_ref.shape[1] // 3
    heads = width // LANES
    counts = [counts_ref[latent, member ^ d] for d in range(GROUP)]
    starts = [jnp.int32(0)]
    for d in range(GROUP):
        starts.append(starts[-1] + (counts[d] + ALIGN - 1) // ALIGN * ALIGN)
    total_rows = packed.shape[0]
    spare = total_rows - LEN
    packed[LEN:, :] = jnp.zeros((spare, packed.shape[1]), BF16)
    def lay(own_core):
        for d in range(GROUP):
            for k in range(2):
                away = own_core != k
                for is_small in range(2):
                    size = small if is_small else large
                    first = k * half + is_small * large
                    where = position(SMALL if is_small else LARGE[k], d)
                    source = early_ref
                    if where == 0:
                        base = first
                    elif where < 4:
                        base = cap + is_small * 3 * large + (where - 1) * size + away * 3 * half
                    else:
                        source = late_refs[away]
                        base = is_small * 4 * large + (where - 4) * size
                    packed[pl.ds(pl.multiple_of(starts[d] + first, ALIGN), size), :] = source[
                        base : base + size, :
                    ]

    pl.when(core == 0)(lambda: lay(0))
    pl.when(core == 1)(lambda: lay(1))
    slot = lax.broadcasted_iota(jnp.int32, (1, packed_rows), 1)
    valid = jnp.zeros((1, packed_rows), jnp.bool_)
    for d in range(GROUP):
        valid = valid | ((slot >= starts[d]) & (slot < starts[d] + counts[d]))
    bias = jnp.where(valid, 0.0, -1e30)
    out[LEN:, :] = jnp.zeros((spare, out.shape[1]), F32)
    block = packed_rows // 3
    for low in range(0, packed_rows, block):
        for head in range(heads):
            lanes = head * LANES
            queries = packed[low : low + block, lanes : lanes + LANES]
            keys = packed[:packed_rows, width + lanes : width + lanes + LANES]
            values = packed[:packed_rows, 2 * width + lanes : 2 * width + lanes + LANES]
            scores = lax.dot_general(
                queries, keys, (((1,), (1,)), ((), ())), preferred_element_type=F32
            )
            scores = scores + bias
            peak = jnp.max(scores, axis=-1, keepdims=True)
            probs = jnp.exp2(scores - peak).astype(BF16)
            mixed = jnp.dot(probs, values, preferred_element_type=F32)
            mixed = mixed / mixed[:, HEAD_DIM : HEAD_DIM + 1]
            out[low : low + block, lanes : lanes + LANES] = mixed
    targets = [
        jnp.where(core == 0, starts[spread(HEADS_TO[0], j)], starts[spread(HEADS_TO[1], j)])
        for j in range(GROUP)
    ]
    for pair in range(0, GROUP, 2):
        columns = []
        for head in range(heads):
            rows = [
                out[pl.ds(pl.multiple_of(targets[j], ALIGN), cap), head * LANES : (head + 1) * LANES]
                for j in (pair, pair + 1)
            ]
            columns.append(jnp.concatenate(rows).T[:HEAD_DIM])
        dest = near_ref if pair < GROUP // 2 else far_ref
        at = pair % (GROUP // 2) * cap
        dest[:, at : at + 2 * cap] = jnp.concatenate(columns).astype(BF16)


def attention(piece_rows, early, late, cap):
    packed_rows = LEN + GROUP * ALIGN
    total = -(-(packed_rows + cap) // 32) * 32
    width = early.shape[1] // 3
    heads = width // LANES
    shape = jax.ShapeDtypeStruct((heads * HEAD_DIM, GROUP // 2 * cap), BF16)
    return call(
        functools.partial(attention_kernel, cap, packed_rows),
        (shape, shape),
        (piece_rows, early) + tuple(late),
        scratch=[pltpu.VMEM((total, 3 * width), BF16), pltpu.VMEM((total, width), F32)],
        specs=[pl.BlockSpec(memory_space=pltpu.SMEM)] + [pl.BlockSpec(memory_space=pltpu.VMEM)] * 3,
        flops=4 * heads * packed_rows * packed_rows * LANES,
        name="attend",
    )


def project_kernel(cap, mod_ref, hidden_ref, mine_ref, mate_ref, *refs):
    proj_refs, plane_refs = refs[:8], refs[8 : 8 + GROUP // 2 - 1]
    mid_ref, mlp_ref, flat, weights = refs[8 + GROUP // 2 - 1 :]
    core, latent, member = place()
    heads = mine_ref.shape[0] // HEAD_DIM

    def put(block, j):
        offset = jnp.where(core == 0, spread(HEADS_TO[0], j), spread(HEADS_TO[1], j))
        for head in range(heads):
            rows = block[head * HEAD_DIM : (head + 1) * HEAD_DIM]
            flat[head * GROUP + offset] = rows

    put(mine_ref[...][:, :cap].astype(F32), 0)
    put(mate_ref[...][:, :cap].astype(F32), GROUP // 2)
    for j, ref in enumerate(plane_refs):
        both = ref[...].astype(F32)
        put(both[:, :cap], j + 1)
        put(both[:, cap:], (j + 1) ^ (GROUP // 2))
    for away in range(2):
        head = core if away == 0 else 1 - core
        at = 0
        for blocks, ref in zip((1, 1, 2, 4), proj_refs[4 * away : 4 * away + 4]):
            block = ref[ref.shape[0] - blocks * HEAD_DIM :, :].astype(F32)
            for row in range(0, block.shape[0], HEAD_DIM):
                offset = jnp.where(head == 0, spread(PROJ[0], at), spread(PROJ[1], at))
                weights[head * GROUP + offset] = block[row : row + HEAD_DIM]
                at += 1
    stacked = flat[...].reshape(heads * GROUP * HEAD_DIM, cap).astype(BF16)
    proj = weights[...].reshape(heads * GROUP * HEAD_DIM, weights.shape[2]).astype(BF16)
    attn_out = lax.dot_general(stacked, proj, (((0,), (0,)), ((), ())), preferred_element_type=F32)
    mid = hidden_ref[...].astype(F32) + mod_row(mod_ref, latent, 2) * attn_out
    mid_ref[...] = mid
    scale, shift = 1.0 + mod_row(mod_ref, latent, 4), mod_row(mod_ref, latent, 3)
    mlp_ref[...] = (normalized(mid) * scale + shift).astype(BF16)


def project(modulation, hidden_in, proj_parts, mine, mate, plane):
    cap, width = hidden_in.shape
    heads = mine.shape[0] // HEAD_DIM
    return call(
        functools.partial(project_kernel, cap),
        (jax.ShapeDtypeStruct((cap, width), F32), jax.ShapeDtypeStruct((cap, width), BF16)),
        (modulation, hidden_in, mine, mate) + tuple(proj_parts) + tuple(plane),
        scratch=[
            pltpu.VMEM((heads * GROUP, HEAD_DIM, cap), F32),
            pltpu.VMEM((heads * GROUP, HEAD_DIM, width), F32),
        ],
        flops=2 * cap * width * width,
        name="project",
    )


def pack_kernel(row_counts, up_ref, down_ref, *refs):
    far_refs, (up_all, down_all, sems) = refs[:-3], refs[-3:]
    core, _, _ = place()
    hidden, parts = up_ref.shape[0], len(far_refs) // 2
    own = [
        pltpu.make_async_copy(up_ref, up_all.at[pl.ds(0, hidden)], sems.at[2 * parts]),
        pltpu.make_async_copy(down_ref, down_all.at[pl.ds(0, hidden)], sems.at[2 * parts + 1]),
    ]
    for copy in own:
        copy.start()

    def fetch(dests):
        copies = []
        for d, dest in enumerate(dests):
            at = hidden
            for rows, ref in zip(row_counts, far_refs[parts * d : parts * (d + 1)]):
                source = ref.at[pl.ds(ref.shape[0] - rows, rows)]
                copies.append(
                    pltpu.make_async_copy(source, dest.at[pl.ds(at, rows)], sems.at[len(copies)])
                )
                at += rows
        for copy in copies:
            copy.start()
        for copy in copies:
            copy.wait()

    pl.when(core == 0)(lambda: fetch((up_all, down_all)))
    pl.when(core == 1)(lambda: fetch((down_all, up_all)))
    for copy in own:
        copy.wait()


def pack(up, down, far, row_counts):
    hidden, width = up.shape
    both = jax.ShapeDtypeStruct((2 * hidden, width), BF16)
    return call(
        functools.partial(pack_kernel, row_counts),
        (both, both),
        (up, down) + tuple(far),
        scratch=[pltpu.SemaphoreType.DMA((2 + len(far),))],
        specs=[pl.BlockSpec(memory_space=pl.ANY)] * (2 + len(far)),
        name="pack",
    )


def mlp_kernel(row_count, out_count, up_ref, down_ref, *refs):
    row_refs, out_refs, rows = refs[:row_count], refs[row_count:-1], refs[-1]
    at = 0
    for ref in row_refs:
        rows[at : at + ref.shape[0], :] = ref[...]
        at += ref.shape[0]
    units = lax.dot_general(
        rows[...], up_ref[...], (((1,), (1,)), ((), ())), preferred_element_type=F32
    )
    units = 0.5 * units * (1.0 + jnp.tanh(0.7978845608 * (units + 0.044715 * (units * units * units))))
    partial = jnp.dot(units.astype(BF16), down_ref[...], preferred_element_type=F32)
    at = 0
    for ref in out_refs:
        ref[...] = partial[at : at + ref.shape[0]].astype(ref.dtype)
        at += ref.shape[0]


def mlp_rows(pieces, packed, out_rows, dtype, name):
    count = sum(p.shape[0] for p in pieces)
    hidden, width = packed[0].shape
    outs = tuple(jax.ShapeDtypeStruct((rows, width), dtype) for rows in out_rows)
    return call(
        functools.partial(mlp_kernel, len(pieces), len(outs)),
        outs,
        tuple(packed) + tuple(pieces),
        scratch=[pltpu.VMEM((count, width), BF16)],
        flops=4 * count * width * hidden,
        name=name,
    )


def final_kernel(
    counts_ref, guide_ref, coef_ref, mod_ref, mid_ref, part_ref, noisy_ref, weight_ref,
    *refs,
):
    core, latent, member = place()
    cap = mid_ref.shape[0]
    sum_refs, (block_ref, pred_ref, base_ref, total) = refs[:-4], refs[-4:]
    chunk = cap // CHUNKS
    for i, (first, second) in enumerate(zip(sum_refs[:CHUNKS], sum_refs[CHUNKS:])):
        rows = slice(i * chunk, (i + 1) * chunk)
        total[rows, :] = part_ref[rows, :] + first[:chunk, :].astype(F32) + second[...].astype(F32)
    rows = (mid_ref[...] + mod_row(mod_ref, latent, 5) * total[...]).astype(BF16).astype(F32)
    count = counts_ref[latent, member]
    rows = jnp.where(lax.broadcasted_iota(jnp.int32, (cap, 1), 0) < count, rows, 0.0)
    block_ref[...] = rows.astype(BF16)
    scale, shift = 1.0 + mod_row(mod_ref, latent, 7), mod_row(mod_ref, latent, 6)
    final_in = (normalized(rows) * scale + shift).astype(BF16)
    pred = lax.dot_general(
        weight_ref[...], final_in, (((1,), (1,)), ((), ())), preferred_element_type=F32
    )
    guide = guide_ref[latent]
    valid = lax.broadcasted_iota(jnp.int32, (1, cap), 1) < count
    weighted = (-coef_ref[latent, 1] * jnp.where(core == 0, guide, 1.0 - guide)) * pred
    pred_ref[...] = jnp.where(valid, weighted, 0.0)
    base_ref[...] = jnp.where(valid, coef_ref[latent, 0] * noisy_ref[...], 0.0)


def final(scalars, modulation, mid, part, noisy, weight, firsts, seconds):
    cap, width = mid.shape
    smem, vmem = pl.BlockSpec(memory_space=pltpu.SMEM), pl.BlockSpec(memory_space=pltpu.VMEM)
    flat = jax.ShapeDtypeStruct(noisy.shape, F32)
    return call(
        final_kernel,
        (jax.ShapeDtypeStruct((cap, width), BF16), flat, flat),
        tuple(scalars) + (modulation, mid, part, noisy, weight) + tuple(firsts) + tuple(seconds),
        scratch=[pltpu.VMEM((cap, width), F32)],
        specs=[smem] * 3 + [vmem] * (5 + 2 * CHUNKS),
        flops=2 * cap * width * weight.shape[0],
        name="finish",
    )


def shards(
    hidden_in,
    noisy_latent,
    piece_rows,
    modulation,
    qkv_weight,
    proj_weight,
    up_weight,
    down_weight,
    final_weight,
    guidance,
    solver_coef,
):
    cap, width = hidden_in.shape
    half = cap // 2
    large, small = 2 * half // 3, half // 3
    core, _, _ = place()
    modulation = modulation[0]
    qkv_rows_t, proj_t, up_t, down_t = (
        w[0].T for w in (qkv_weight, proj_weight, up_weight, down_weight)
    )

    hidden = up_t.shape[0]
    cuts = (0, FAR_EARLY[0], sum(FAR_EARLY), hidden)
    large_rows, small_rows = first_payloads(hidden_in, up_t, down_t, large, small, cuts[1])
    proj_rows = None
    got, away = [], []
    for step in range(3):
        payload = large_rows if step == 0 else jnp.concatenate([large_rows, proj_rows])
        got_large = permute_by(payload, [order[step] for order in LARGE])
        got_small = permute_by(small_rows, [SMALL[step]] * 2)
        if step == 0:
            up_t, down_t, _ = lax.optimization_barrier((up_t, down_t, got_large))
            sent = [
                jnp.where(core == 0, up_t[low:high], down_t[low:high])
                for low, high in zip(cuts[1:-1], cuts[2:])
            ]
            proj_own = [
                lax.dynamic_slice_in_dim(proj_t, head * HEAD_DIM, HEAD_DIM) for head in (core, 1 - core)
            ]
            proj_rows = proj_own[0]
        elif step == 1:
            proj_rows = jnp.concatenate([proj_rows, got_large[2 * large :]])
        else:
            early, qkv_padded = qkv_rows(
                modulation,
                qkv_rows_t,
                (hidden_in, got[0][0], got[1][0], got[0][1], got[1][1])
                + (away[0][0], away[1][0], away[0][1], away[1][1]),
                (cap, large, 2 * large, small, 2 * small) + (large, 2 * large, small, 2 * small),
                True,
                "qkv_early",
            )
            got_large, got_small, early, *sent = lax.optimization_barrier(
                (got_large, got_small, early, *sent)
            )
            proj_rows = jnp.concatenate([proj_rows, got_large[4 * large :]])
        if step < 2:
            large_rows = jnp.concatenate([large_rows, got_large[: large << step]])
            small_rows = jnp.concatenate([rows[: small << step] for rows in (small_rows, got_small)])
        got.append((got_large, got_small))
        away.append((from_other_half(got_large), from_other_half(got_small)))
    proj_last = permute_by(proj_rows, [order[2] for order in PROJ])
    far = [got[0][1], permute_by(sent[0], [GROUP // 2] * 2)]
    counts = (4 * large, 4 * small)
    late = list(qkv_rows(modulation, qkv_padded, got[2], counts, False, "qkv_late_own"))
    *other, late[0] = lax.optimization_barrier((*away[2], late[0]))
    late += qkv_rows(modulation, qkv_padded, other, counts, False, "qkv_late_other")
    mine, sent_heads = attention(piece_rows, early, late, cap)
    mate = permute_by(sent_heads, [order[2] for order in HEADS_TO])
    mate, proj_last = lax.optimization_barrier((mate, proj_last))
    proj_parts = [proj_own[0], got[1][0], got[2][0], proj_last]
    proj_parts += [proj_own[1], away[1][0], away[2][0], from_other_half(proj_last)]
    plane = []
    for j in range(1, GROUP // 2):
        both = jnp.concatenate([a[:, j * cap : (j + 1) * cap] for a in (mine, mate)], axis=1)
        plane.append(permute_by(both, [spread(order, j) for order in HEADS_TO]))
    far[1], *plane = lax.optimization_barrier((far[1], *plane))
    far.append(permute_by(after(sent[1], *plane), [GROUP // 2] * 2))
    mid, mlp_in = project(modulation, hidden_in, proj_parts, mine, mate, plane)

    chunk = cap // CHUNKS
    side = permute_by(mlp_in, (1, 2))
    both = [
        jnp.concatenate([rows[low : low + chunk] for rows in (mlp_in, side)])
        for low in range(0, cap, chunk)
    ]
    across = [permute_by(rows, (2, 1)) for rows in both]
    far[2] = after(far[2], *both)
    far += [away[0][1]] + [from_other_half(rows) for rows in far[1:]]
    packed = pack(up_t, down_t, far, [high - low for low, high in zip(cuts[:-1], cuts[1:])])
    sums = [
        mlp_rows((rows,), packed, (2 * chunk,), BF16, f"mlp_far{i}")[0] for i, rows in enumerate(across)
    ]
    firsts = [permute_by(rows, (2, 1)) for rows in sums]
    part, *side_parts = mlp_rows(
        (after(mlp_in, *sums), side), packed, (cap,) + (chunk,) * CHUNKS, F32, "mlp_near"
    )
    seconds = [
        permute_by((rows + first[chunk:].astype(F32)).astype(BF16), (1, 2))
        for rows, first in zip(side_parts, firsts)
    ]
    block_rows, pred, base = final(
        (piece_rows, guidance, solver_coef),
        modulation,
        mid,
        part,
        noisy_latent.T,
        final_weight.T,
        firsts,
        seconds,
    )
    next_latent = base + (pred + from_other_half(pred))
    return (next_latent.T, block_rows[None])


def solution(mesh):
    placed = (
        P("tok", None),
        P("tok", None),
        P(),
        P("cfg", None, None, None),
        P("tok", None, None),
        P("tok", None, None),
        P("tok", None, None),
        P("tok", None, None),
        P(),
        P(),
        P(),
    )
    return jax.shard_map(
        shards,
        mesh=mesh,
        in_specs=placed,
        out_specs=(P("tok", None), P("cfg", "tok", None)),
        check_vma=False,
    )
```

```python
import functools
import math

import jax
import jax.numpy as jnp
from jax import lax
from jax.experimental import pallas as pl
from jax.experimental.pallas import tpu as pltpu
from jax.sharding import PartitionSpec as P

HEAD_DIM = 72
GROUP = 8
LEN = 1024
LANES = 128
ALIGN = 16
LARGE = ((1, 2, 4), (2, 4, 1))
SMALL = (4, 1, 2)
PROJ = ((2, 4, 1), (4, 1, 2))
HEADS_TO = ((2, 4, 1), (4, 1, 2))
FAR_EARLY = (80, 320)
CHUNKS = 3
F32 = jnp.float32
BF16 = jnp.bfloat16


def permute_by(block, offsets):
    count = lax.axis_size("tok")
    route = [
        (half * count + i, half * count + (i ^ offset))
        for half, offset in enumerate(offsets)
        for i in range(count)
    ]
    return lax.ppermute(block, ("cfg", "tok"), route)


def from_other_half(block):
    return lax.ppermute(block, "cfg", [(0, 1), (1, 0)])


def after(value, *earlier):
    return lax.optimization_barrier((value,) + earlier)[0]


def place():
    pos = lax.axis_index("tok")
    return lax.axis_index("cfg"), pos // GROUP, pos % GROUP


def normalized(values):
    center = values - jnp.mean(values, axis=-1, keepdims=True)
    spread = jnp.mean(center * center, axis=-1, keepdims=True)
    return center * lax.rsqrt(spread + 1e-06)


def mod_row(mod_ref, latent, k):
    return mod_ref[latent, k : k + 1, :]


def call(kernel, out_shape, operands, scratch=(), specs=None, flops=0, name=None, vmem=40):
    whole = pl.BlockSpec(memory_space=pltpu.VMEM)
    moved = sum(math.prod(o.shape) * o.dtype.itemsize for o in operands)
    return pl.pallas_call(
        kernel,
        out_shape=out_shape,
        in_specs=specs or [whole] * len(operands),
        out_specs=jax.tree.map(lambda _: whole, out_shape),
        scratch_shapes=list(scratch),
        compiler_params=pltpu.CompilerParams(vmem_limit_bytes=vmem << 20),
        cost_estimate=pl.CostEstimate(flops=flops, bytes_accessed=moved, transcendentals=0),
        name=name,
    )(*operands)


def first_kernel(hidden_ref, up_ref, down_ref, large_ref, small_ref, sems):
    core, _, _ = place()
    half = hidden_ref.shape[0] // 2
    large, small = large_ref.shape[0], half - large_ref.shape[0]
    first = pl.multiple_of(core * half, 32)
    copies = [
        pltpu.make_async_copy(hidden_ref.at[pl.ds(first, large)], large_ref, sems.at[0]),
        pltpu.make_async_copy(
            hidden_ref.at[pl.ds(first + large, small)], small_ref.at[pl.ds(0, small)], sems.at[1]
        ),
    ]
    for copy in copies:
        copy.start()
    rest = small_ref.shape[0] - small

    def bring(weight_ref):
        copy = pltpu.make_async_copy(
            weight_ref.at[pl.ds(0, rest)], small_ref.at[pl.ds(small, rest)], sems.at[2]
        )
        copy.start()
        copy.wait()

    pl.when(core == 0)(lambda: bring(up_ref))
    pl.when(core == 1)(lambda: bring(down_ref))
    for copy in copies:
        copy.wait()


def first_payloads(hidden_in, up, down, large, small, weight_rows):
    width = hidden_in.shape[1]
    return call(
        first_kernel,
        (
            jax.ShapeDtypeStruct((large, width), BF16),
            jax.ShapeDtypeStruct((small + weight_rows, width), BF16),
        ),
        (hidden_in, up, down),
        scratch=[pltpu.SemaphoreType.DMA((3,))],
        specs=[pl.BlockSpec(memory_space=pl.ANY)] * 3,
        name="first",
        vmem=63,
    )


def pad_weight(weight_ref, padded):
    weight = weight_ref[...].astype(F32)
    unused = jnp.zeros((LANES - HEAD_DIM, weight.shape[1]), F32)
    for part in range(weight.shape[0] // HEAD_DIM):
        rows = jnp.concatenate([weight[part * HEAD_DIM : (part + 1) * HEAD_DIM], unused])
        padded[part * LANES : (part + 1) * LANES, :] = rows.astype(BF16)


def qkv_kernel(row_counts, mod_ref, weight_ref, *refs):
    row_refs, (out_ref, *made, normed) = refs[: len(row_counts)], refs[len(row_counts) :]
    _, latent, _ = place()
    shift, scale = mod_row(mod_ref, latent, 0), 1.0 + mod_row(mod_ref, latent, 1)
    chunk = 32
    at = 0
    for ref, count in zip(row_refs, row_counts):
        for low in range(0, count, chunk):
            rows = ref[low : low + chunk, :].astype(F32)
            normed[at : at + chunk, :] = (normalized(rows) * scale + shift).astype(BF16)
            at += chunk
    padded = weight_ref
    if made:
        padded = made[0]
        pad_weight(weight_ref, padded)
    lane = lax.broadcasted_iota(jnp.int32, (1, padded.shape[0]), 1)
    width = padded.shape[0] // 3
    factor = jnp.where(lane < width, HEAD_DIM ** (-0.5) * math.log2(math.e), 1.0)
    ones = jnp.where((lane >= 2 * width) & (lane % LANES == HEAD_DIM), 1.0, 0.0)
    block = at // 2
    for low in range(0, at, block):
        out = lax.dot_general(
            normed[low : low + block, :], padded[...], (((1,), (1,)), ((), ())), preferred_element_type=F32
        )
        out_ref[low : low + block, :] = (out * factor + ones).astype(BF16)


def qkv_rows(modulation, weight, pieces, row_counts, make_padded, name):
    count, width = sum(row_counts), weight.shape[1]
    padded_rows = weight.shape[0] // HEAD_DIM * LANES if make_padded else weight.shape[0]
    outs = [jax.ShapeDtypeStruct((count, padded_rows), BF16)]
    if make_padded:
        outs.append(jax.ShapeDtypeStruct((padded_rows, width), BF16))
    return call(
        functools.partial(qkv_kernel, row_counts),
        tuple(outs),
        (modulation, weight) + tuple(pieces),
        scratch=[pltpu.VMEM((count, width), BF16)],
        flops=2 * count * width * padded_rows,
        name=name,
    )


def position(order, offset):
    return sum(1 << i for i, bit in enumerate(order) if offset & bit)


def spread(order, index):
    return sum(bit for i, bit in enumerate(order) if index >> i & 1)


def attention_kernel(cap, packed_rows, counts_ref, early_ref, *refs):
    late_refs, (near_ref, far_ref, packed, out) = refs[:2], refs[2:]
    core, latent, member = place()
    half = cap // 2
    large, small = 2 * half // 3, half // 3
    width = early_ref.shape[1] // 3
    heads = width // LANES
    counts = [counts_ref[latent, member ^ d] for d in range(GROUP)]
    starts = [jnp.int32(0)]
    for d in range(GROUP):
        starts.append(starts[-1] + (counts[d] + ALIGN - 1) // ALIGN * ALIGN)
    total_rows = packed.shape[0]
    spare = total_rows - LEN
    packed[LEN:, :] = jnp.zeros((spare, packed.shape[1]), BF16)
    def lay(own_core):
        for d in range(GROUP):
            for k in range(2):
                away = own_core != k
                for is_small in range(2):
                    size = small if is_small else large
                    first = k * half + is_small * large
                    where = position(SMALL if is_small else LARGE[k], d)
                    source = early_ref
                    if where == 0:
                        base = first
                    elif where < 4:
                        base = cap + is_small * 3 * large + (where - 1) * size + away * 3 * half
                    else:
                        source = late_refs[away]
                        base = is_small * 4 * large + (where - 4) * size
                    packed[pl.ds(pl.multiple_of(starts[d] + first, ALIGN), size), :] = source[
                        base : base + size, :
                    ]

    pl.when(core == 0)(lambda: lay(0))
    pl.when(core == 1)(lambda: lay(1))
    slot = lax.broadcasted_iota(jnp.int32, (1, packed_rows), 1)
    valid = jnp.zeros((1, packed_rows), jnp.bool_)
    for d in range(GROUP):
        valid = valid | ((slot >= starts[d]) & (slot < starts[d] + counts[d]))
    bias = jnp.where(valid, 0.0, -1e30)
    out[LEN:, :] = jnp.zeros((spare, out.shape[1]), F32)
    block = packed_rows // 3
    for low in range(0, packed_rows, block):
        for head in range(heads):
            lanes = head * LANES
            queries = packed[low : low + block, lanes : lanes + LANES]
            keys = packed[:packed_rows, width + lanes : width + lanes + LANES]
            values = packed[:packed_rows, 2 * width + lanes : 2 * width + lanes + LANES]
            scores = lax.dot_general(
                queries, keys, (((1,), (1,)), ((), ())), preferred_element_type=F32
            )
            scores = scores + bias
            peak = jnp.max(scores, axis=-1, keepdims=True)
            probs = jnp.exp2(scores - peak).astype(BF16)
            mixed = jnp.dot(probs, values, preferred_element_type=F32)
            mixed = mixed / mixed[:, HEAD_DIM : HEAD_DIM + 1]
            out[low : low + block, lanes : lanes + LANES] = mixed
    targets = [
        jnp.where(core == 0, starts[spread(HEADS_TO[0], j)], starts[spread(HEADS_TO[1], j)])
        for j in range(GROUP)
    ]
    for pair in range(0, GROUP, 2):
        columns = []
        for head in range(heads):
            rows = [
                out[pl.ds(pl.multiple_of(targets[j], ALIGN), cap), head * LANES : (head + 1) * LANES]
                for j in (pair, pair + 1)
            ]
            columns.append(jnp.concatenate(rows).T[:HEAD_DIM])
        dest = near_ref if pair < GROUP // 2 else far_ref
        at = pair % (GROUP // 2) * cap
        dest[:, at : at + 2 * cap] = jnp.concatenate(columns).astype(BF16)


def attention(piece_rows, early, late, cap):
    packed_rows = LEN + GROUP * ALIGN
    total = -(-(packed_rows + cap) // 32) * 32
    width = early.shape[1] // 3
    heads = width // LANES
    shape = jax.ShapeDtypeStruct((heads * HEAD_DIM, GROUP // 2 * cap), BF16)
    return call(
        functools.partial(attention_kernel, cap, packed_rows),
        (shape, shape),
        (piece_rows, early) + tuple(late),
        scratch=[pltpu.VMEM((total, 3 * width), BF16), pltpu.VMEM((total, width), F32)],
        specs=[pl.BlockSpec(memory_space=pltpu.SMEM)] + [pl.BlockSpec(memory_space=pltpu.VMEM)] * 3,
        flops=4 * heads * packed_rows * packed_rows * LANES,
        name="attend",
    )


def project_kernel(cap, mod_ref, hidden_ref, mine_ref, mate_ref, *refs):
    proj_refs, plane_refs = refs[:8], refs[8 : 8 + GROUP // 2 - 1]
    mid_ref, mlp_ref, flat, weights = refs[8 + GROUP // 2 - 1 :]
    core, latent, member = place()
    heads = mine_ref.shape[0] // HEAD_DIM

    def put(block, j):
        offset = jnp.where(core == 0, spread(HEADS_TO[0], j), spread(HEADS_TO[1], j))
        for head in range(heads):
            rows = block[head * HEAD_DIM : (head + 1) * HEAD_DIM]
            flat[head * GROUP + offset] = rows

    put(mine_ref[...][:, :cap].astype(F32), 0)
    put(mate_ref[...][:, :cap].astype(F32), GROUP // 2)
    for j, ref in enumerate(plane_refs):
        both = ref[...].astype(F32)
        put(both[:, :cap], j + 1)
        put(both[:, cap:], (j + 1) ^ (GROUP // 2))
    for away in range(2):
        head = core if away == 0 else 1 - core
        at = 0
        for blocks, ref in zip((1, 1, 2, 4), proj_refs[4 * away : 4 * away + 4]):
            block = ref[ref.shape[0] - blocks * HEAD_DIM :, :].astype(F32)
            for row in range(0, block.shape[0], HEAD_DIM):
                offset = jnp.where(head == 0, spread(PROJ[0], at), spread(PROJ[1], at))
                weights[head * GROUP + offset] = block[row : row + HEAD_DIM]
                at += 1
    stacked = flat[...].reshape(heads * GROUP * HEAD_DIM, cap).astype(BF16)
    proj = weights[...].reshape(heads * GROUP * HEAD_DIM, weights.shape[2]).astype(BF16)
    attn_out = lax.dot_general(stacked, proj, (((0,), (0,)), ((), ())), preferred_element_type=F32)
    mid = hidden_ref[...].astype(F32) + mod_row(mod_ref, latent, 2) * attn_out
    mid_ref[...] = mid
    scale, shift = 1.0 + mod_row(mod_ref, latent, 4), mod_row(mod_ref, latent, 3)
    mlp_ref[...] = (normalized(mid) * scale + shift).astype(BF16)


def project(modulation, hidden_in, proj_parts, mine, mate, plane):
    cap, width = hidden_in.shape
    heads = mine.shape[0] // HEAD_DIM
    return call(
        functools.partial(project_kernel, cap),
        (jax.ShapeDtypeStruct((cap, width), F32), jax.ShapeDtypeStruct((cap, width), BF16)),
        (modulation, hidden_in, mine, mate) + tuple(proj_parts) + tuple(plane),
        scratch=[
            pltpu.VMEM((heads * GROUP, HEAD_DIM, cap), F32),
            pltpu.VMEM((heads * GROUP, HEAD_DIM, width), F32),
        ],
        flops=2 * cap * width * width,
        name="project",
    )


def pack_kernel(row_counts, up_ref, down_ref, *refs):
    far_refs, (up_all, down_all, sems) = refs[:-3], refs[-3:]
    core, _, _ = place()
    hidden, parts = up_ref.shape[0], len(far_refs) // 2
    own = [
        pltpu.make_async_copy(up_ref, up_all.at[pl.ds(0, hidden)], sems.at[2 * parts]),
        pltpu.make_async_copy(down_ref, down_all.at[pl.ds(0, hidden)], sems.at[2 * parts + 1]),
    ]
    for copy in own:
        copy.start()

    def fetch(dests):
        copies = []
        for d, dest in enumerate(dests):
            at = hidden
            for rows, ref in zip(row_counts, far_refs[parts * d : parts * (d + 1)]):
                source = ref.at[pl.ds(ref.shape[0] - rows, rows)]
                copies.append(
                    pltpu.make_async_copy(source, dest.at[pl.ds(at, rows)], sems.at[len(copies)])
                )
                at += rows
        for copy in copies:
            copy.start()
        for copy in copies:
            copy.wait()

    pl.when(core == 0)(lambda: fetch((up_all, down_all)))
    pl.when(core == 1)(lambda: fetch((down_all, up_all)))
    for copy in own:
        copy.wait()


def pack(up, down, far, row_counts):
    hidden, width = up.shape
    both = jax.ShapeDtypeStruct((2 * hidden, width), BF16)
    return call(
        functools.partial(pack_kernel, row_counts),
        (both, both),
        (up, down) + tuple(far),
        scratch=[pltpu.SemaphoreType.DMA((2 + len(far),))],
        specs=[pl.BlockSpec(memory_space=pl.ANY)] * (2 + len(far)),
        name="pack",
    )


def mlp_kernel(row_count, out_count, up_ref, down_ref, *refs):
    row_refs, out_refs, rows = refs[:row_count], refs[row_count:-1], refs[-1]
    at = 0
    for ref in row_refs:
        rows[at : at + ref.shape[0], :] = ref[...]
        at += ref.shape[0]
    units = lax.dot_general(
        rows[...], up_ref[...], (((1,), (1,)), ((), ())), preferred_element_type=F32
    )
    units = 0.5 * units * (1.0 + jnp.tanh(0.7978845608 * (units + 0.044715 * (units * units * units))))
    partial = jnp.dot(units.astype(BF16), down_ref[...], preferred_element_type=F32)
    at = 0
    for ref in out_refs:
        ref[...] = partial[at : at + ref.shape[0]].astype(ref.dtype)
        at += ref.shape[0]


def mlp_rows(pieces, packed, out_rows, dtype, name):
    count = sum(p.shape[0] for p in pieces)
    hidden, width = packed[0].shape
    outs = tuple(jax.ShapeDtypeStruct((rows, width), dtype) for rows in out_rows)
    return call(
        functools.partial(mlp_kernel, len(pieces), len(outs)),
        outs,
        tuple(packed) + tuple(pieces),
        scratch=[pltpu.VMEM((count, width), BF16)],
        flops=4 * count * width * hidden,
        name=name,
    )


def final_kernel(
    counts_ref, guide_ref, coef_ref, mod_ref, mid_ref, part_ref, noisy_ref, weight_ref,
    *refs,
):
    core, latent, member = place()
    cap = mid_ref.shape[0]
    sum_refs, (block_ref, pred_ref, base_ref, total) = refs[:-4], refs[-4:]
    chunk = cap // CHUNKS
    for i, (first, second) in enumerate(zip(sum_refs[:CHUNKS], sum_refs[CHUNKS:])):
        rows = slice(i * chunk, (i + 1) * chunk)
        total[rows, :] = part_ref[rows, :] + first[:chunk, :].astype(F32) + second[...].astype(F32)
    rows = (mid_ref[...] + mod_row(mod_ref, latent, 5) * total[...]).astype(BF16).astype(F32)
    count = counts_ref[latent, member]
    rows = jnp.where(lax.broadcasted_iota(jnp.int32, (cap, 1), 0) < count, rows, 0.0)
    block_ref[...] = rows.astype(BF16)
    scale, shift = 1.0 + mod_row(mod_ref, latent, 7), mod_row(mod_ref, latent, 6)
    final_in = (normalized(rows) * scale + shift).astype(BF16)
    pred = lax.dot_general(
        weight_ref[...], final_in, (((1,), (1,)), ((), ())), preferred_element_type=F32
    )
    guide = guide_ref[latent]
    valid = lax.broadcasted_iota(jnp.int32, (1, cap), 1) < count
    weighted = (-coef_ref[latent, 1] * jnp.where(core == 0, guide, 1.0 - guide)) * pred
    pred_ref[...] = jnp.where(valid, weighted, 0.0)
    base_ref[...] = jnp.where(valid, coef_ref[latent, 0] * noisy_ref[...], 0.0)


def final(scalars, modulation, mid, part, noisy, weight, firsts, seconds):
    cap, width = mid.shape
    smem, vmem = pl.BlockSpec(memory_space=pltpu.SMEM), pl.BlockSpec(memory_space=pltpu.VMEM)
    flat = jax.ShapeDtypeStruct(noisy.shape, F32)
    return call(
        final_kernel,
        (jax.ShapeDtypeStruct((cap, width), BF16), flat, flat),
        tuple(scalars) + (modulation, mid, part, noisy, weight) + tuple(firsts) + tuple(seconds),
        scratch=[pltpu.VMEM((cap, width), F32)],
        specs=[smem] * 3 + [vmem] * (5 + 2 * CHUNKS),
        flops=2 * cap * width * weight.shape[0],
        name="finish",
    )


def shards(
    hidden_in,
    noisy_latent,
    piece_rows,
    modulation,
    qkv_weight,
    proj_weight,
    up_weight,
    down_weight,
    final_weight,
    guidance,
    solver_coef,
):
    cap, width = hidden_in.shape
    half = cap // 2
    large, small = 2 * half // 3, half // 3
    core, _, _ = place()
    modulation = modulation[0]
    qkv_rows_t, proj_t, up_t, down_t = (
        w[0].T for w in (qkv_weight, proj_weight, up_weight, down_weight)
    )

    hidden = up_t.shape[0]
    cuts = (0, FAR_EARLY[0], sum(FAR_EARLY), hidden)
    large_rows, small_rows = first_payloads(hidden_in, up_t, down_t, large, small, cuts[1])
    own_rows = after(lax.dynamic_slice_in_dim(after(hidden_in, large_rows), core * half, half))
    proj_rows = None
    got, away = [], []
    for step in range(3):
        payload = large_rows if step == 0 else jnp.concatenate([large_rows, proj_rows])
        got_large = permute_by(payload, [order[step] for order in LARGE])
        got_small = permute_by(small_rows, [SMALL[step]] * 2)
        if step == 0:
            up_t, down_t, _ = lax.optimization_barrier((up_t, down_t, got_large))
            sent = [
                jnp.where(core == 0, up_t[low:high], down_t[low:high])
                for low, high in zip(cuts[1:-1], cuts[2:])
            ]
            proj_own = [
                lax.dynamic_slice_in_dim(proj_t, head * HEAD_DIM, HEAD_DIM) for head in (core, 1 - core)
            ]
            proj_rows = proj_own[0]
        elif step == 1:
            proj_rows = jnp.concatenate([proj_rows, got_large[2 * large :]])
        else:
            early, qkv_padded = qkv_rows(
                modulation,
                qkv_rows_t,
                (hidden_in, got[0][0], got[1][0], got[0][1], got[1][1])
                + (away[0][0], away[1][0], away[0][1], away[1][1]),
                (cap, large, 2 * large, small, 2 * small) + (large, 2 * large, small, 2 * small),
                True,
                "qkv_early",
            )
            got_large, got_small, early, *sent = lax.optimization_barrier(
                (got_large, got_small, early, *sent)
            )
            proj_rows = jnp.concatenate([proj_rows, got_large[4 * large :]])
        if step == 0:
            large_rows, small_rows = own_rows[:large], own_rows[large:]
        if step < 2:
            large_rows = jnp.concatenate([large_rows, got_large[: large << step]])
            small_rows = jnp.concatenate([rows[: small << step] for rows in (small_rows, got_small)])
        got.append((got_large, got_small))
        away.append((from_other_half(got_large), from_other_half(got_small)))
    proj_last = permute_by(proj_rows, [order[2] for order in PROJ])
    far = [got[0][1], permute_by(sent[0], [GROUP // 2] * 2)]
    counts = (4 * large, 4 * small)
    late = list(qkv_rows(modulation, qkv_padded, got[2], counts, False, "qkv_late_own"))
    *other, late[0] = lax.optimization_barrier((*away[2], late[0]))
    late += qkv_rows(modulation, qkv_padded, other, counts, False, "qkv_late_other")
    mine, sent_heads = attention(piece_rows, early, late, cap)
    mate = permute_by(sent_heads, [order[2] for order in HEADS_TO])
    mate, proj_last = lax.optimization_barrier((mate, proj_last))
    proj_parts = [proj_own[0], got[1][0], got[2][0], proj_last]
    proj_parts += [proj_own[1], away[1][0], away[2][0], from_other_half(proj_last)]
    plane = []
    for j in range(1, GROUP // 2):
        both = jnp.concatenate([a[:, j * cap : (j + 1) * cap] for a in (mine, mate)], axis=1)
        plane.append(permute_by(both, [spread(order, j) for order in HEADS_TO]))
    far[1], *plane = lax.optimization_barrier((far[1], *plane))
    far.append(permute_by(after(sent[1], *plane), [GROUP // 2] * 2))
    mid, mlp_in = project(modulation, hidden_in, proj_parts, mine, mate, plane)

    chunk = cap // CHUNKS
    side = permute_by(mlp_in, (1, 2))
    both = [
        jnp.concatenate([rows[low : low + chunk] for rows in (mlp_in, side)])
        for low in range(0, cap, chunk)
    ]
    across = [permute_by(rows, (2, 1)) for rows in both]
    far[2] = after(far[2], *both)
    far += [away[0][1]] + [from_other_half(rows) for rows in far[1:]]
    packed = pack(up_t, down_t, far, [high - low for low, high in zip(cuts[:-1], cuts[1:])])
    sums = [
        mlp_rows((rows,), packed, (2 * chunk,), BF16, f"mlp_far{i}")[0] for i, rows in enumerate(across)
    ]
    firsts = [permute_by(rows, (2, 1)) for rows in sums]
    part, *side_parts = mlp_rows(
        (after(mlp_in, *sums), side), packed, (cap,) + (chunk,) * CHUNKS, F32, "mlp_near"
    )
    seconds = [
        permute_by((rows + first[chunk:].astype(F32)).astype(BF16), (1, 2))
        for rows, first in zip(side_parts, firsts)
    ]
    block_rows, pred, base = final(
        (piece_rows, guidance, solver_coef),
        modulation,
        mid,
        part,
        noisy_latent.T,
        final_weight.T,
        firsts,
        seconds,
    )
    next_latent = base + (pred + from_other_half(pred))
    return (next_latent.T, block_rows[None])


def solution(mesh):
    placed = (
        P("tok", None),
        P("tok", None),
        P(),
        P("cfg", None, None, None),
        P("tok", None, None),
        P("tok", None, None),
        P("tok", None, None),
        P("tok", None, None),
        P(),
        P(),
        P(),
    )
    return jax.shard_map(
        shards,
        mesh=mesh,
        in_specs=placed,
        out_specs=(P("tok", None), P("cfg", "tok", None)),
        check_vma=False,
    )
```

```python
import functools
import math

import jax
import jax.numpy as jnp
from jax import lax
from jax.experimental import pallas as pl
from jax.experimental.pallas import tpu as pltpu
from jax.sharding import PartitionSpec as P

HEAD_DIM = 72
GROUP = 8
LEN = 1024
LANES = 128
ALIGN = 16
LARGE = ((1, 2, 4), (2, 4, 1))
SMALL = (4, 1, 2)
PROJ = ((2, 4, 1), (4, 1, 2))
HEADS_TO = ((2, 4, 1), (4, 1, 2))
FAR_EARLY = (80, 320)
CHUNKS = 4
F32 = jnp.float32
BF16 = jnp.bfloat16


def permute_by(block, offsets):
    count = lax.axis_size("tok")
    route = [
        (half * count + i, half * count + (i ^ offset))
        for half, offset in enumerate(offsets)
        for i in range(count)
    ]
    return lax.ppermute(block, ("cfg", "tok"), route)


def from_other_half(block):
    return lax.ppermute(block, "cfg", [(0, 1), (1, 0)])


def after(value, *earlier):
    return lax.optimization_barrier((value,) + earlier)[0]


def place():
    pos = lax.axis_index("tok")
    return lax.axis_index("cfg"), pos // GROUP, pos % GROUP


def normalized(values):
    center = values - jnp.mean(values, axis=-1, keepdims=True)
    spread = jnp.mean(center * center, axis=-1, keepdims=True)
    return center * lax.rsqrt(spread + 1e-06)


def mod_row(mod_ref, latent, k):
    return mod_ref[latent, k : k + 1, :]


def call(kernel, out_shape, operands, scratch=(), specs=None, flops=0, name=None, vmem=40):
    whole = pl.BlockSpec(memory_space=pltpu.VMEM)
    moved = sum(math.prod(o.shape) * o.dtype.itemsize for o in operands)
    return pl.pallas_call(
        kernel,
        out_shape=out_shape,
        in_specs=specs or [whole] * len(operands),
        out_specs=jax.tree.map(lambda _: whole, out_shape),
        scratch_shapes=list(scratch),
        compiler_params=pltpu.CompilerParams(vmem_limit_bytes=vmem << 20),
        cost_estimate=pl.CostEstimate(flops=flops, bytes_accessed=moved, transcendentals=0),
        name=name,
    )(*operands)


def first_kernel(hidden_ref, up_ref, down_ref, large_ref, small_ref, sems):
    core, _, _ = place()
    half = hidden_ref.shape[0] // 2
    large, small = large_ref.shape[0], half - large_ref.shape[0]
    first = pl.multiple_of(core * half, 32)
    copies = [
        pltpu.make_async_copy(hidden_ref.at[pl.ds(first, large)], large_ref, sems.at[0]),
        pltpu.make_async_copy(
            hidden_ref.at[pl.ds(first + large, small)], small_ref.at[pl.ds(0, small)], sems.at[1]
        ),
    ]
    for copy in copies:
        copy.start()
    rest = small_ref.shape[0] - small

    def bring(weight_ref):
        copy = pltpu.make_async_copy(
            weight_ref.at[pl.ds(0, rest)], small_ref.at[pl.ds(small, rest)], sems.at[2]
        )
        copy.start()
        copy.wait()

    pl.when(core == 0)(lambda: bring(up_ref))
    pl.when(core == 1)(lambda: bring(down_ref))
    for copy in copies:
        copy.wait()


def first_payloads(hidden_in, up, down, large, small, weight_rows):
    width = hidden_in.shape[1]
    return call(
        first_kernel,
        (
            jax.ShapeDtypeStruct((large, width), BF16),
            jax.ShapeDtypeStruct((small + weight_rows, width), BF16),
        ),
        (hidden_in, up, down),
        scratch=[pltpu.SemaphoreType.DMA((3,))],
        specs=[pl.BlockSpec(memory_space=pl.ANY)] * 3,
        name="first",
        vmem=63,
    )


def pad_weight(weight_ref, padded):
    weight = weight_ref[...].astype(F32)
    unused = jnp.zeros((LANES - HEAD_DIM, weight.shape[1]), F32)
    for part in range(weight.shape[0] // HEAD_DIM):
        rows = jnp.concatenate([weight[part * HEAD_DIM : (part + 1) * HEAD_DIM], unused])
        padded[part * LANES : (part + 1) * LANES, :] = rows.astype(BF16)


def qkv_kernel(row_counts, mod_ref, weight_ref, *refs):
    row_refs, (out_ref, *made, normed) = refs[: len(row_counts)], refs[len(row_counts) :]
    _, latent, _ = place()
    shift, scale = mod_row(mod_ref, latent, 0), 1.0 + mod_row(mod_ref, latent, 1)
    chunk = 32
    at = 0
    for ref, count in zip(row_refs, row_counts):
        for low in range(0, count, chunk):
            rows = ref[low : low + chunk, :].astype(F32)
            normed[at : at + chunk, :] = (normalized(rows) * scale + shift).astype(BF16)
            at += chunk
    padded = weight_ref
    if made:
        padded = made[0]
        pad_weight(weight_ref, padded)
    lane = lax.broadcasted_iota(jnp.int32, (1, padded.shape[0]), 1)
    width = padded.shape[0] // 3
    factor = jnp.where(lane < width, HEAD_DIM ** (-0.5) * math.log2(math.e), 1.0)
    ones = jnp.where((lane >= 2 * width) & (lane % LANES == HEAD_DIM), 1.0, 0.0)
    block = at // 2
    for low in range(0, at, block):
        out = lax.dot_general(
            normed[low : low + block, :], padded[...], (((1,), (1,)), ((), ())), preferred_element_type=F32
        )
        out_ref[low : low + block, :] = (out * factor + ones).astype(BF16)


def qkv_rows(modulation, weight, pieces, row_counts, make_padded, name):
    count, width = sum(row_counts), weight.shape[1]
    padded_rows = weight.shape[0] // HEAD_DIM * LANES if make_padded else weight.shape[0]
    outs = [jax.ShapeDtypeStruct((count, padded_rows), BF16)]
    if make_padded:
        outs.append(jax.ShapeDtypeStruct((padded_rows, width), BF16))
    return call(
        functools.partial(qkv_kernel, row_counts),
        tuple(outs),
        (modulation, weight) + tuple(pieces),
        scratch=[pltpu.VMEM((count, width), BF16)],
        flops=2 * count * width * padded_rows,
        name=name,
    )


def position(order, offset):
    return sum(1 << i for i, bit in enumerate(order) if offset & bit)


def spread(order, index):
    return sum(bit for i, bit in enumerate(order) if index >> i & 1)


def attention_kernel(cap, packed_rows, counts_ref, early_ref, *refs):
    late_refs, (near_ref, far_ref, packed, out) = refs[:2], refs[2:]
    core, latent, member = place()
    half = cap // 2
    large, small = 2 * half // 3, half // 3
    width = early_ref.shape[1] // 3
    heads = width // LANES
    counts = [counts_ref[latent, member ^ d] for d in range(GROUP)]
    starts = [jnp.int32(0)]
    for d in range(GROUP):
        starts.append(starts[-1] + (counts[d] + ALIGN - 1) // ALIGN * ALIGN)
    total_rows = packed.shape[0]
    spare = total_rows - LEN
    packed[LEN:, :] = jnp.zeros((spare, packed.shape[1]), BF16)
    def lay(own_core):
        for d in range(GROUP):
            for k in range(2):
                away = own_core != k
                for is_small in range(2):
                    size = small if is_small else large
                    first = k * half + is_small * large
                    where = position(SMALL if is_small else LARGE[k], d)
                    source = early_ref
                    if where == 0:
                        base = first
                    elif where < 4:
                        base = cap + is_small * 3 * large + (where - 1) * size + away * 3 * half
                    else:
                        source = late_refs[away]
                        base = is_small * 4 * large + (where - 4) * size
                    packed[pl.ds(pl.multiple_of(starts[d] + first, ALIGN), size), :] = source[
                        base : base + size, :
                    ]

    pl.when(core == 0)(lambda: lay(0))
    pl.when(core == 1)(lambda: lay(1))
    slot = lax.broadcasted_iota(jnp.int32, (1, packed_rows), 1)
    valid = jnp.zeros((1, packed_rows), jnp.bool_)
    for d in range(GROUP):
        valid = valid | ((slot >= starts[d]) & (slot < starts[d] + counts[d]))
    bias = jnp.where(valid, 0.0, -1e30)
    out[LEN:, :] = jnp.zeros((spare, out.shape[1]), F32)
    block = packed_rows // 3
    for low in range(0, packed_rows, block):
        for head in range(heads):
            lanes = head * LANES
            queries = packed[low : low + block, lanes : lanes + LANES]
            keys = packed[:packed_rows, width + lanes : width + lanes + LANES]
            values = packed[:packed_rows, 2 * width + lanes : 2 * width + lanes + LANES]
            scores = lax.dot_general(
                queries, keys, (((1,), (1,)), ((), ())), preferred_element_type=F32
            )
            scores = scores + bias
            peak = jnp.max(scores, axis=-1, keepdims=True)
            probs = jnp.exp2(scores - peak).astype(BF16)
            mixed = jnp.dot(probs, values, preferred_element_type=F32)
            mixed = mixed / mixed[:, HEAD_DIM : HEAD_DIM + 1]
            out[low : low + block, lanes : lanes + LANES] = mixed
    targets = [
        jnp.where(core == 0, starts[spread(HEADS_TO[0], j)], starts[spread(HEADS_TO[1], j)])
        for j in range(GROUP)
    ]
    for pair in range(0, GROUP, 2):
        columns = []
        for head in range(heads):
            rows = [
                out[pl.ds(pl.multiple_of(targets[j], ALIGN), cap), head * LANES : (head + 1) * LANES]
                for j in (pair, pair + 1)
            ]
            columns.append(jnp.concatenate(rows).T[:HEAD_DIM])
        dest = near_ref if pair < GROUP // 2 else far_ref
        at = pair % (GROUP // 2) * cap
        dest[:, at : at + 2 * cap] = jnp.concatenate(columns).astype(BF16)


def attention(piece_rows, early, late, cap):
    packed_rows = LEN + GROUP * ALIGN
    total = -(-(packed_rows + cap) // 32) * 32
    width = early.shape[1] // 3
    heads = width // LANES
    shape = jax.ShapeDtypeStruct((heads * HEAD_DIM, GROUP // 2 * cap), BF16)
    return call(
        functools.partial(attention_kernel, cap, packed_rows),
        (shape, shape),
        (piece_rows, early) + tuple(late),
        scratch=[pltpu.VMEM((total, 3 * width), BF16), pltpu.VMEM((total, width), F32)],
        specs=[pl.BlockSpec(memory_space=pltpu.SMEM)] + [pl.BlockSpec(memory_space=pltpu.VMEM)] * 3,
        flops=4 * heads * packed_rows * packed_rows * LANES,
        name="attend",
    )


def project_kernel(cap, mod_ref, hidden_ref, mine_ref, mate_ref, *refs):
    proj_refs, plane_refs = refs[:8], refs[8 : 8 + GROUP // 2 - 1]
    mid_ref, mlp_ref, flat, weights = refs[8 + GROUP // 2 - 1 :]
    core, latent, member = place()
    heads = mine_ref.shape[0] // HEAD_DIM

    def put(block, j):
        offset = jnp.where(core == 0, spread(HEADS_TO[0], j), spread(HEADS_TO[1], j))
        for head in range(heads):
            rows = block[head * HEAD_DIM : (head + 1) * HEAD_DIM]
            flat[head * GROUP + offset] = rows

    put(mine_ref[...][:, :cap].astype(F32), 0)
    put(mate_ref[...][:, :cap].astype(F32), GROUP // 2)
    for j, ref in enumerate(plane_refs):
        both = ref[...].astype(F32)
        put(both[:, :cap], j + 1)
        put(both[:, cap:], (j + 1) ^ (GROUP // 2))
    for away in range(2):
        head = core if away == 0 else 1 - core
        at = 0
        for blocks, ref in zip((1, 1, 2, 4), proj_refs[4 * away : 4 * away + 4]):
            block = ref[ref.shape[0] - blocks * HEAD_DIM :, :].astype(F32)
            for row in range(0, block.shape[0], HEAD_DIM):
                offset = jnp.where(head == 0, spread(PROJ[0], at), spread(PROJ[1], at))
                weights[head * GROUP + offset] = block[row : row + HEAD_DIM]
                at += 1
    stacked = flat[...].reshape(heads * GROUP * HEAD_DIM, cap).astype(BF16)
    proj = weights[...].reshape(heads * GROUP * HEAD_DIM, weights.shape[2]).astype(BF16)
    attn_out = lax.dot_general(stacked, proj, (((0,), (0,)), ((), ())), preferred_element_type=F32)
    mid = hidden_ref[...].astype(F32) + mod_row(mod_ref, latent, 2) * attn_out
    mid_ref[...] = mid
    scale, shift = 1.0 + mod_row(mod_ref, latent, 4), mod_row(mod_ref, latent, 3)
    mlp_ref[...] = (normalized(mid) * scale + shift).astype(BF16)


def project(modulation, hidden_in, proj_parts, mine, mate, plane):
    cap, width = hidden_in.shape
    heads = mine.shape[0] // HEAD_DIM
    return call(
        functools.partial(project_kernel, cap),
        (jax.ShapeDtypeStruct((cap, width), F32), jax.ShapeDtypeStruct((cap, width), BF16)),
        (modulation, hidden_in, mine, mate) + tuple(proj_parts) + tuple(plane),
        scratch=[
            pltpu.VMEM((heads * GROUP, HEAD_DIM, cap), F32),
            pltpu.VMEM((heads * GROUP, HEAD_DIM, width), F32),
        ],
        flops=2 * cap * width * width,
        name="project",
    )


def pack_kernel(row_counts, up_ref, down_ref, *refs):
    far_refs, (up_all, down_all, sems) = refs[:-3], refs[-3:]
    core, _, _ = place()
    hidden, parts = up_ref.shape[0], len(far_refs) // 2
    own = [
        pltpu.make_async_copy(up_ref, up_all.at[pl.ds(0, hidden)], sems.at[2 * parts]),
        pltpu.make_async_copy(down_ref, down_all.at[pl.ds(0, hidden)], sems.at[2 * parts + 1]),
    ]
    for copy in own:
        copy.start()

    def fetch(dests):
        copies = []
        for d, dest in enumerate(dests):
            at = hidden
            for rows, ref in zip(row_counts, far_refs[parts * d : parts * (d + 1)]):
                source = ref.at[pl.ds(ref.shape[0] - rows, rows)]
                copies.append(
                    pltpu.make_async_copy(source, dest.at[pl.ds(at, rows)], sems.at[len(copies)])
                )
                at += rows
        for copy in copies:
            copy.start()
        for copy in copies:
            copy.wait()

    pl.when(core == 0)(lambda: fetch((up_all, down_all)))
    pl.when(core == 1)(lambda: fetch((down_all, up_all)))
    for copy in own:
        copy.wait()


def pack(up, down, far, row_counts):
    hidden, width = up.shape
    both = jax.ShapeDtypeStruct((2 * hidden, width), BF16)
    return call(
        functools.partial(pack_kernel, row_counts),
        (both, both),
        (up, down) + tuple(far),
        scratch=[pltpu.SemaphoreType.DMA((2 + len(far),))],
        specs=[pl.BlockSpec(memory_space=pl.ANY)] * (2 + len(far)),
        name="pack",
    )


def mlp_kernel(row_count, out_count, up_ref, down_ref, *refs):
    row_refs, out_refs, rows = refs[:row_count], refs[row_count:-1], refs[-1]
    at = 0
    for ref in row_refs:
        rows[at : at + ref.shape[0], :] = ref[...]
        at += ref.shape[0]
    units = lax.dot_general(
        rows[...], up_ref[...], (((1,), (1,)), ((), ())), preferred_element_type=F32
    )
    units = 0.5 * units * (1.0 + jnp.tanh(0.7978845608 * (units + 0.044715 * (units * units * units))))
    partial = jnp.dot(units.astype(BF16), down_ref[...], preferred_element_type=F32)
    at = 0
    for ref in out_refs:
        ref[...] = partial[at : at + ref.shape[0]].astype(ref.dtype)
        at += ref.shape[0]


def mlp_rows(pieces, packed, out_rows, dtype, name):
    count = sum(p.shape[0] for p in pieces)
    hidden, width = packed[0].shape
    outs = tuple(jax.ShapeDtypeStruct((rows, width), dtype) for rows in out_rows)
    return call(
        functools.partial(mlp_kernel, len(pieces), len(outs)),
        outs,
        tuple(packed) + tuple(pieces),
        scratch=[pltpu.VMEM((count, width), BF16)],
        flops=4 * count * width * hidden,
        name=name,
    )


def final_kernel(
    counts_ref, guide_ref, coef_ref, mod_ref, mid_ref, part_ref, noisy_ref, weight_ref,
    *refs,
):
    core, latent, member = place()
    cap = mid_ref.shape[0]
    sum_refs, (block_ref, pred_ref, base_ref, total) = refs[:-4], refs[-4:]
    chunk = cap // CHUNKS
    for i, (first, second) in enumerate(zip(sum_refs[:CHUNKS], sum_refs[CHUNKS:])):
        rows = slice(i * chunk, (i + 1) * chunk)
        total[rows, :] = part_ref[rows, :] + first[:chunk, :].astype(F32) + second[...].astype(F32)
    rows = (mid_ref[...] + mod_row(mod_ref, latent, 5) * total[...]).astype(BF16).astype(F32)
    count = counts_ref[latent, member]
    rows = jnp.where(lax.broadcasted_iota(jnp.int32, (cap, 1), 0) < count, rows, 0.0)
    block_ref[...] = rows.astype(BF16)
    scale, shift = 1.0 + mod_row(mod_ref, latent, 7), mod_row(mod_ref, latent, 6)
    final_in = (normalized(rows) * scale + shift).astype(BF16)
    pred = lax.dot_general(
        weight_ref[...], final_in, (((1,), (1,)), ((), ())), preferred_element_type=F32
    )
    guide = guide_ref[latent]
    valid = lax.broadcasted_iota(jnp.int32, (1, cap), 1) < count
    weighted = (-coef_ref[latent, 1] * jnp.where(core == 0, guide, 1.0 - guide)) * pred
    pred_ref[...] = jnp.where(valid, weighted, 0.0)
    base_ref[...] = jnp.where(valid, coef_ref[latent, 0] * noisy_ref[...], 0.0)


def final(scalars, modulation, mid, part, noisy, weight, firsts, seconds):
    cap, width = mid.shape
    smem, vmem = pl.BlockSpec(memory_space=pltpu.SMEM), pl.BlockSpec(memory_space=pltpu.VMEM)
    flat = jax.ShapeDtypeStruct(noisy.shape, F32)
    return call(
        final_kernel,
        (jax.ShapeDtypeStruct((cap, width), BF16), flat, flat),
        tuple(scalars) + (modulation, mid, part, noisy, weight) + tuple(firsts) + tuple(seconds),
        scratch=[pltpu.VMEM((cap, width), F32)],
        specs=[smem] * 3 + [vmem] * (5 + 2 * CHUNKS),
        flops=2 * cap * width * weight.shape[0],
        name="finish",
    )


def shards(
    hidden_in,
    noisy_latent,
    piece_rows,
    modulation,
    qkv_weight,
    proj_weight,
    up_weight,
    down_weight,
    final_weight,
    guidance,
    solver_coef,
):
    cap, width = hidden_in.shape
    half = cap // 2
    large, small = 2 * half // 3, half // 3
    core, _, _ = place()
    modulation = modulation[0]
    qkv_rows_t, proj_t, up_t, down_t = (
        w[0].T for w in (qkv_weight, proj_weight, up_weight, down_weight)
    )

    hidden = up_t.shape[0]
    cuts = (0, FAR_EARLY[0], sum(FAR_EARLY), hidden)
    large_rows, small_rows = first_payloads(hidden_in, up_t, down_t, large, small, cuts[1])
    proj_rows = None
    got, away = [], []
    for step in range(3):
        payload = large_rows if step == 0 else jnp.concatenate([large_rows, proj_rows])
        got_large = permute_by(payload, [order[step] for order in LARGE])
        got_small = permute_by(small_rows, [SMALL[step]] * 2)
        if step == 0:
            up_t, down_t, _ = lax.optimization_barrier((up_t, down_t, got_large))
            sent = [
                jnp.where(core == 0, up_t[low:high], down_t[low:high])
                for low, high in zip(cuts[1:-1], cuts[2:])
            ]
            proj_own = [
                lax.dynamic_slice_in_dim(proj_t, head * HEAD_DIM, HEAD_DIM) for head in (core, 1 - core)
            ]
            proj_rows = proj_own[0]
        elif step == 1:
            proj_rows = jnp.concatenate([proj_rows, got_large[2 * large :]])
        else:
            early, qkv_padded = qkv_rows(
                modulation,
                qkv_rows_t,
                (hidden_in, got[0][0], got[1][0], got[0][1], got[1][1])
                + (away[0][0], away[1][0], away[0][1], away[1][1]),
                (cap, large, 2 * large, small, 2 * small) + (large, 2 * large, small, 2 * small),
                True,
                "qkv_early",
            )
            got_large, got_small, early, *sent = lax.optimization_barrier(
                (got_large, got_small, early, *sent)
            )
            proj_rows = jnp.concatenate([proj_rows, got_large[4 * large :]])
        if step < 2:
            large_rows = jnp.concatenate([large_rows, got_large[: large << step]])
            small_rows = jnp.concatenate([rows[: small << step] for rows in (small_rows, got_small)])
        got.append((got_large, got_small))
        away.append((from_other_half(got_large), from_other_half(got_small)))
    proj_last = permute_by(proj_rows, [order[2] for order in PROJ])
    far = [got[0][1], permute_by(sent[0], [GROUP // 2] * 2)]
    counts = (4 * large, 4 * small)
    late = list(qkv_rows(modulation, qkv_padded, got[2], counts, False, "qkv_late_own"))
    *other, late[0] = lax.optimization_barrier((*away[2], late[0]))
    late += qkv_rows(modulation, qkv_padded, other, counts, False, "qkv_late_other")
    mine, sent_heads = attention(piece_rows, early, late, cap)
    mate = permute_by(sent_heads, [order[2] for order in HEADS_TO])
    mate, proj_last = lax.optimization_barrier((mate, proj_last))
    proj_parts = [proj_own[0], got[1][0], got[2][0], proj_last]
    proj_parts += [proj_own[1], away[1][0], away[2][0], from_other_half(proj_last)]
    plane = []
    for j in range(1, GROUP // 2):
        both = jnp.concatenate([a[:, j * cap : (j + 1) * cap] for a in (mine, mate)], axis=1)
        plane.append(permute_by(both, [spread(order, j) for order in HEADS_TO]))
    far[1], *plane = lax.optimization_barrier((far[1], *plane))
    far.append(permute_by(after(sent[1], *plane), [GROUP // 2] * 2))
    mid, mlp_in = project(modulation, hidden_in, proj_parts, mine, mate, plane)

    chunk = cap // CHUNKS
    side = permute_by(mlp_in, (1, 2))
    both = [
        jnp.concatenate([rows[low : low + chunk] for rows in (mlp_in, side)])
        for low in range(0, cap, chunk)
    ]
    across = [permute_by(rows, (2, 1)) for rows in both]
    far[2] = after(far[2], *both)
    far += [away[0][1]] + [from_other_half(rows) for rows in far[1:]]
    packed = pack(up_t, down_t, far, [high - low for low, high in zip(cuts[:-1], cuts[1:])])
    sums = [
        mlp_rows((rows,), packed, (2 * chunk,), BF16, f"mlp_far{i}")[0] for i, rows in enumerate(across)
    ]
    firsts = [permute_by(rows, (2, 1)) for rows in sums]
    part, *side_parts = mlp_rows(
        (after(mlp_in, *sums), side), packed, (cap,) + (chunk,) * CHUNKS, F32, "mlp_near"
    )
    seconds = [
        permute_by((rows + first[chunk:].astype(F32)).astype(BF16), (1, 2))
        for rows, first in zip(side_parts, firsts)
    ]
    block_rows, pred, base = final(
        (piece_rows, guidance, solver_coef),
        modulation,
        mid,
        part,
        noisy_latent.T,
        final_weight.T,
        firsts,
        seconds,
    )
    next_latent = base + (pred + from_other_half(pred))
    return (next_latent.T, block_rows[None])


def solution(mesh):
    placed = (
        P("tok", None),
        P("tok", None),
        P(),
        P("cfg", None, None, None),
        P("tok", None, None),
        P("tok", None, None),
        P("tok", None, None),
        P("tok", None, None),
        P(),
        P(),
        P(),
    )
    return jax.shard_map(
        shards,
        mesh=mesh,
        in_specs=placed,
        out_specs=(P("tok", None), P("cfg", "tok", None)),
        check_vma=False,
    )
```
